256 devices in a mesh: tiles: 128 (over x, z, y_hi, core), chan: 2 (over y_lo).
Axes of the slice: x: 4, y: 4 (y_hi: 2, y_lo: 2; y = y_hi * 2 + y_lo), z: 8, core: 2. Of those that a mesh axis runs over, the one named last changes fastest.
Arguments:
- ocean_state: bfloat16 [1024, 8, 8, 256], P('tiles', None, None, 'chan'), may hold values from -6 to 6
- grad_state: bfloat16 [1024, 8, 8, 256], P('tiles', None, None, 'chan'), may hold values from -6 to 6
- sea_mask: int32 [1024, 8, 8], P('tiles'), may hold values 0 or 1
- tile_ids: int32 [1024], P('tiles'), may hold values from -1 to 1023, as said below
- neighbours: int32 [1024, 8], P('tiles'), may hold values from -1 to 1023, as said below
- fold_partner: int32 [1024], P('tiles'), may hold values from -1 to 1023, as said below
- kernel: float32 [7, 7, 256], P(None, None, 'chan'), may hold values from -0.875 to 0.875
- norm_gain: float32 [256], P('chan'), may hold values from 0.5 to 1.5
- expand_weight: bfloat16 [256, 1024], P(None, 'chan'), may hold values from -0.375 to 0.375
- reduce_weight: bfloat16 [1024, 256], P('chan'), may hold values from -0.1875 to 0.1875
Outputs:
- new_state: bfloat16 [1024, 8, 8, 256], P('tiles', None, None, 'chan')
- grad_input: bfloat16 [1024, 8, 8, 256], P('tiles', None, None, 'chan')
- grad_expand: float32 [256, 1024], P(None, 'chan')
- grad_reduce: float32 [1024, 256], P('chan')
- grad_gain: float32 [256], P('chan')
- grad_kernel: float32 [7, 7, 256], P(None, None, 'chan')
The draws below stay inside these ranges and needn't reach their ends.
Inputs may be any that keep to these rules, and one draw needn't show every extreme that they name: `tile_ids`: tile number is row times 256 plus column in a grid of 256 x 4 tiles. Device d holds slots d * 8 to d * 8 + 7; device 2 j holds the tiles of columns j * 2 to j * 2 + 1 and device 2 j + 1 those of the mirrored block 254 - j * 2 to 255 - j * 2, all rows, in any slot order; each wet tile is in exactly one slot, land tiles in none, and their slots hold -1. Every tile of the top row is wet. Some device has all 8 slots wet. `neighbours`: columns wrap around; an entry is -1 where that tile is land, below row 0 or above the top row, and throughout an empty slot; it is symmetric (if t names u as south then u names t as north, and so on). Every other entry is a slot on the same device, on a device two indices away, or on the device whose index differs only in its lowest bit. `fold_partner`: for a tile in the top row at column j, the slot of the top-row tile at column 255 - j; -1 for every other slot. It is symmetric, and the partner lies on the device whose index differs only in its lowest bit.
All inputs are finite; a program needn't handle non-finite values. No bound on the sum of `sea_mask` on one device may be relied on, other than what follows from the above.
Results may differ from the reference program's by a relative error of at most 0.019.
Values may be sent and summed in bfloat16 or wider, within the bound.
No kernel may reach another device: no remote copies, remote signals or barrier semaphores. Data moves between devices by JAX's collectives and lax.ppermute only.
A program may use at most 64 MiB of HBM per device.

```python
import math
import jax
import jax.numpy as jnp
from jax import lax

C = 256
HID = 1024
TS = 8
GY = 4
SX = 2
SLOTS = 8
GX = 256
NS = 1024


def tile_layout(key):
    devices = GX // SX
    wet_key, full_key, order_key = jax.random.split(key, 3)
    wet_block = jax.random.randint(wet_key, (devices, SLOTS), 0, 4) > 0
    full_device = jax.random.randint(full_key, (), 0, devices)
    device_index = jnp.arange(devices, dtype=jnp.int32)
    position = jnp.arange(SLOTS, dtype=jnp.int32)
    wet_block = jnp.logical_or(wet_block, (device_index == full_device)[:, None])
    wet_block = jnp.logical_or(wet_block, (position // SX == GY - 1)[None, :])
    scores = jax.random.randint(order_key, (devices, SLOTS), 0, 1 << 20) * SLOTS + position[None, :]
    slot_order = jnp.argsort(scores, axis=1).astype(jnp.int32)
    slot_wet = jnp.take_along_axis(wet_block, slot_order, axis=1).reshape(-1)
    pair_index = device_index // 2
    strip_index = jnp.where(device_index % 2 == 0, pair_index, devices - 1 - pair_index)
    tile_row = (slot_order // SX).reshape(-1)
    column = (strip_index[:, None] * SX + slot_order % SX).reshape(-1)
    tile_number = tile_row * GX + column
    slot_index = jnp.arange(NS, dtype=jnp.int32)
    owner_slot = jnp.full((GX * GY,), -1, jnp.int32).at[tile_number].set(jnp.where(slot_wet, slot_index, -1))
    return (slot_wet, tile_row, column, tile_number, owner_slot)


def draw_tile_ids(key, part):
    slot_wet, tile_row, column, tile_number, owner_slot = tile_layout(key)
    return jnp.where(slot_wet, tile_number, -1).astype(jnp.int32)


def draw_neighbours(key, part):
    slot_wet, tile_row, column, tile_number, owner_slot = tile_layout(key)
    direction_steps = ((0, -1), (0, 1), (-1, 0), (1, 0), (-1, -1), (1, -1), (-1, 1), (1, 1))
    listed = []
    for column_step, row_step in direction_steps:
        next_row = tile_row + row_step
        next_column = (column + column_step) % GX
        inside = (next_row >= 0) & (next_row < GY) & slot_wet
        found_slot = owner_slot[jnp.clip(next_row, 0, GY - 1) * GX + next_column]
        listed.append(jnp.where(inside, found_slot, -1))
    return jnp.stack(listed, axis=1).astype(jnp.int32)


def draw_fold_partner(key, part):
    slot_wet, tile_row, column, tile_number, owner_slot = tile_layout(key)
    inside = slot_wet & (tile_row == GY - 1)
    found_slot = owner_slot[(GY - 1) * GX + GX - 1 - column]
    return jnp.where(inside, found_slot, -1).astype(jnp.int32)


def plant(result, rng, smallest, top_value):
    spot = [jax.random.randint(jax.random.fold_in(rng, axis), (), 0, length) for axis, length in enumerate(result.shape)]
    widest = result.shape.index(max(result.shape))
    beside = spot[:widest] + [(spot[widest] + 1) % result.shape[widest]] + spot[widest + 1:]
    return result.at[tuple(spot)].set(smallest).at[tuple(beside)].set(top_value)


def block_scale(rng, extent, cuts, low, top_value):
    level, own = 1.0, jax.random.fold_in(rng, 6)
    for axis_at, blocks in cuts:
        draws = jnp.exp(jax.random.uniform(jax.random.fold_in(own, axis_at), (blocks,), jnp.float32, low / len(cuts), top_value / len(cuts)))
        level = level * jnp.repeat(draws, extent[axis_at] // blocks).reshape([-1 if axis == axis_at else 1 for axis in range(len(extent))])
    return level


def normal_values(rng, extent, deviation, most, shards=(), kind=jnp.bfloat16):
    entries = deviation * jax.random.normal(rng, extent, jnp.float32)
    if shards:
        entries = entries * block_scale(rng, extent, shards, -0.22, 0.18)
    return jnp.clip(entries, -most, most).astype(kind)


def setup_inputs(seed: int = 0) -> dict:
    seeds = jax.random.split(jax.random.key(seed), 11)
    ocean_state = normal_values(seeds[0], (NS, TS, TS, C), 1.0, 6.0, ((0, 128), (3, 2)))
    grad_state = normal_values(seeds[1], (NS, TS, TS, C), 1.0, 6.0, ((0, 128), (3, 2)))
    sea_mask = plant((jax.random.randint(seeds[2], (NS, TS, TS), 0, 8) < 7).astype(jnp.int32), jax.random.fold_in(seeds[2], 1), 0, 1)
    tile_ids = draw_tile_ids(jax.random.fold_in(seeds[10], 71), 0)
    neighbours = draw_neighbours(jax.random.fold_in(seeds[10], 71), 0)
    fold_partner = draw_fold_partner(jax.random.fold_in(seeds[10], 71), 0)
    kernel = normal_values(seeds[6], (7, 7, C), 49 ** -0.5, 0.875, ((2, 2),), jnp.float32)
    norm_gain = jnp.clip(0.5 + 1.0 * jax.random.uniform(seeds[7], (C,), jnp.float32) ** block_scale(seeds[7], (C,), ((0, 2),), -0.2, 0.2), 0.5, 1.5)
    expand_weight = normal_values(seeds[8], (C, HID), C ** -0.5, 0.375, ((1, 2),))
    reduce_weight = normal_values(seeds[9], (HID, C), HID ** -0.5, 0.1875, ((0, 2),))
    return {"ocean_state": ocean_state, "grad_state": grad_state, "sea_mask": sea_mask, "tile_ids": tile_ids, "neighbours": neighbours, "fold_partner": fold_partner, "kernel": kernel, "norm_gain": norm_gain, "expand_weight": expand_weight, "reduce_weight": reduce_weight}


norm_eps = 1e-06
root_half = 0.7071067811865476
inv_root_tau = 0.3989422804014327

def gelu_value(hidden_input):
    return 0.5 * hidden_input * (1.0 + lax.erf(hidden_input * root_half))

def gelu_slope(hidden_input):
    return 0.5 * (1.0 + lax.erf(hidden_input * root_half)) + hidden_input * jnp.exp(-0.5 * hidden_input * hidden_input) * inv_root_tau

def edge_rims(field):
    slot_count, tile_size, _, local_width = field.shape
    lower_rows = field[:, 0:3].reshape(slot_count, 3 * tile_size, local_width)
    upper_rows = field[:, tile_size - 3:].reshape(slot_count, 3 * tile_size, local_width)
    left_columns = field[:, :, 0:3].reshape(slot_count, 3 * tile_size, local_width)
    right_columns = field[:, :, tile_size - 3:].reshape(slot_count, 3 * tile_size, local_width)
    return jnp.concatenate([lower_rows, upper_rows, left_columns, right_columns], axis=1)

def rim_strip(near_rims, direction, strip_kind, tile_size):
    slot_count, local_width = (near_rims.shape[0], near_rims.shape[-1])
    strip_rows = near_rims[:, direction, strip_kind * 3 * tile_size:(strip_kind + 1) * 3 * tile_size]
    if strip_kind < 2:
        return strip_rows.reshape(slot_count, 3, tile_size, local_width)
    return strip_rows.reshape(slot_count, tile_size, 3, local_width)

def extend_tile(field, near_rims, fold_strip):
    tile_size = field.shape[1]
    south_band = rim_strip(near_rims, 0, 1, tile_size)
    north_band = rim_strip(near_rims, 1, 0, tile_size) + fold_strip[:, ::-1, ::-1]
    west_band = rim_strip(near_rims, 2, 3, tile_size)
    east_band = rim_strip(near_rims, 3, 2, tile_size)
    south_west = rim_strip(near_rims, 4, 1, tile_size)[:, :, tile_size - 3:]
    south_east = rim_strip(near_rims, 5, 1, tile_size)[:, :, 0:3]
    north_west = rim_strip(near_rims, 6, 0, tile_size)[:, :, tile_size - 3:]
    north_east = rim_strip(near_rims, 7, 0, tile_size)[:, :, 0:3]
    bottom = jnp.concatenate([south_west, south_band, south_east], axis=2)
    middle = jnp.concatenate([west_band, field, east_band], axis=2)
    top_rows = jnp.concatenate([north_west, north_band, north_east], axis=2)
    return jnp.concatenate([bottom, middle, top_rows], axis=1)

def correlate(padded, kernel, out_rows, out_columns):
    widened = padded.astype(jnp.float32)
    accum = jnp.zeros((padded.shape[0], out_rows, out_columns, padded.shape[3]), jnp.float32)
    for row_shift in range(7):
        for column_shift in range(7):
            accum = accum + kernel[row_shift, column_shift] * widened[:, row_shift:row_shift + out_rows, column_shift:column_shift + out_columns]
    return accum

def kernel_grad(grad_conv, padded):
    out_rows, out_columns = (grad_conv.shape[1], grad_conv.shape[2])
    widened = padded.astype(jnp.float32)
    grad_wide = grad_conv.astype(jnp.float32)
    kernel_terms = []
    for row_shift in range(7):
        for column_shift in range(7):
            kernel_terms.append(lax.optimization_barrier(jnp.sum(grad_wide * widened[:, row_shift:row_shift + out_rows, column_shift:column_shift + out_columns], axis=(0, 1, 2))))
    return jnp.stack(kernel_terms).reshape(7, 7, grad_conv.shape[3])

def back_conv(grad_extended, partner_rows, kernel, tile_size):
    flipped = kernel[::-1, ::-1]
    interior = correlate(grad_extended, flipped, tile_size, tile_size)
    padded = jnp.pad(partner_rows, ((0, 0), (0, 6), (3, 3), (0, 0)))
    fold_terms = correlate(padded, flipped, 3, tile_size)
    return interior.at[:, tile_size - 3:].add(fold_terms[:, ::-1, ::-1])

def pick_rims(rim_rows, upper_part, targets, fold_targets, tile_size):
    zero_value = jnp.zeros((), rim_rows.dtype)
    chosen = jnp.take(rim_rows, jnp.maximum(targets, 0), axis=0)
    chosen = jnp.where((targets >= 0)[:, :, None, None], chosen, zero_value)
    partner_rows = jnp.take(upper_part, jnp.maximum(fold_targets, 0), axis=0)
    partner_rows = jnp.where((fold_targets >= 0)[:, None, None], partner_rows, zero_value)
    return (chosen, partner_rows.reshape(fold_targets.shape[0], 3, tile_size, rim_rows.shape[-1]))

def reference(ocean_state, grad_state, sea_mask, tile_ids, neighbours, fold_partner, kernel, norm_gain, expand_weight, reduce_weight):
    slot_total, tile_size, width = (ocean_state.shape[0], ocean_state.shape[1], ocean_state.shape[3])
    live_mask = (sea_mask * (tile_ids >= 0).astype(jnp.int32)[:, None, None]).astype(jnp.bfloat16)[..., None]
    masked = ocean_state * live_mask
    grad_output = grad_state * live_mask
    rim_rows = edge_rims(masked)
    upper_part = rim_rows[:, 3 * tile_size:6 * tile_size]
    blocks = slot_total // SLOTS
    contract_rows = (((0,), (0,)), ((), ()))
    contract_cols = (((1,), (1,)), ((), ()))

    def forward_step(carry, block_index):
        first_slot = block_index * SLOTS
        block_state = lax.dynamic_slice_in_dim(masked, first_slot, SLOTS, 0)
        block_grad = lax.dynamic_slice_in_dim(grad_output, first_slot, SLOTS, 0)
        block_live = lax.dynamic_slice_in_dim(live_mask, first_slot, SLOTS, 0)
        block_near = lax.dynamic_slice_in_dim(neighbours, first_slot, SLOTS, 0)
        block_fold = lax.dynamic_slice_in_dim(fold_partner, first_slot, SLOTS, 0)
        near_rims, fold_strip = pick_rims(rim_rows, upper_part, block_near, block_fold, tile_size)
        extended = extend_tile(block_state, near_rims, fold_strip)
        convolved = correlate(extended, kernel, tile_size, tile_size)
        centred = convolved - lax.optimization_barrier(jnp.mean(convolved, axis=-1, keepdims=True))
        variance = lax.optimization_barrier(jnp.mean(centred * centred, axis=-1, keepdims=True))
        inverse = lax.rsqrt(variance + norm_eps)
        standard = centred * inverse
        normed = (standard * norm_gain).astype(jnp.bfloat16)
        flat_normed = normed.reshape(-1, width)
        hidden_input = jnp.dot(flat_normed, expand_weight, preferred_element_type=jnp.float32)
        activated = gelu_value(hidden_input).astype(jnp.bfloat16)
        mixed_out = jnp.dot(activated, reduce_weight, preferred_element_type=jnp.float32).reshape(convolved.shape)
        new_block = ((block_state.astype(jnp.float32) + mixed_out) * block_live).astype(jnp.bfloat16)
        grad_flat = block_grad.reshape(-1, width)
        grad_reduce = lax.dot_general(activated, grad_flat, contract_rows, preferred_element_type=jnp.float32)
        grad_activated = lax.dot_general(grad_flat, reduce_weight, contract_cols, preferred_element_type=jnp.float32)
        grad_hidden = (grad_activated * gelu_slope(hidden_input)).astype(jnp.bfloat16)
        grad_expand = lax.dot_general(flat_normed, grad_hidden, contract_rows, preferred_element_type=jnp.float32)
        grad_normed = lax.dot_general(grad_hidden, expand_weight, contract_cols, preferred_element_type=jnp.float32).reshape(convolved.shape)
        grad_gain = lax.optimization_barrier(jnp.sum(grad_normed * standard, axis=(0, 1, 2)))
        grad_standard = grad_normed * norm_gain
        first_moment = lax.optimization_barrier(jnp.mean(grad_standard, axis=-1, keepdims=True))
        second_moment = lax.optimization_barrier(jnp.mean(grad_standard * standard, axis=-1, keepdims=True))
        grad_conv = (inverse * (grad_standard - first_moment - standard * second_moment)).astype(jnp.bfloat16)
        grad_kernel = kernel_grad(grad_conv, extended)
        updated = (carry[0] + grad_expand, carry[1] + grad_reduce, carry[2] + grad_gain, carry[3] + grad_kernel)
        return (updated, (new_block, grad_conv))
    start_carry = (jnp.zeros((width, HID), jnp.float32), jnp.zeros((HID, width), jnp.float32), jnp.zeros((width,), jnp.float32), jnp.zeros((7, 7, width), jnp.float32))
    totals, (new_blocks, grad_blocks) = lax.scan(forward_step, start_carry, jnp.arange(blocks, dtype=jnp.int32))
    new_state = new_blocks.reshape(ocean_state.shape)
    grad_convs = grad_blocks.reshape(ocean_state.shape)
    grad_rims = edge_rims(grad_convs)
    grad_upper = grad_rims[:, 3 * tile_size:6 * tile_size]

    def backward_step(block_index):
        first_slot = block_index * SLOTS
        block_conv = lax.dynamic_slice_in_dim(grad_convs, first_slot, SLOTS, 0)
        block_grad = lax.dynamic_slice_in_dim(grad_output, first_slot, SLOTS, 0)
        block_live = lax.dynamic_slice_in_dim(live_mask, first_slot, SLOTS, 0)
        block_near = lax.dynamic_slice_in_dim(neighbours, first_slot, SLOTS, 0)
        block_fold = lax.dynamic_slice_in_dim(fold_partner, first_slot, SLOTS, 0)
        near_rims, partner_rows = pick_rims(grad_rims, grad_upper, block_near, block_fold, tile_size)
        grad_extended = extend_tile(block_conv, near_rims, jnp.zeros_like(partner_rows))
        contribution = back_conv(grad_extended, partner_rows, kernel, tile_size)
        return ((block_grad.astype(jnp.float32) + contribution) * block_live).astype(jnp.bfloat16)
    grad_input = lax.map(backward_step, jnp.arange(blocks, dtype=jnp.int32)).reshape(ocean_state.shape)
    grad_scale = 1.0 / math.sqrt(slot_total * tile_size * tile_size)
    return (new_state, grad_input, totals[0] * grad_scale, totals[1] * grad_scale, totals[2] * grad_scale, totals[3] * grad_scale)
```

```python
import functools
import math

import jax
import jax.numpy as jnp
from jax import lax
from jax.experimental import pallas as pl
from jax.experimental.pallas import tpu as pltpu
from jax.sharding import PartitionSpec as P

F32, BF16 = jnp.float32, jnp.bfloat16
TS = 8
CELLS = TS * TS
SLOTS = 8
ROWS = CELLS * SLOTS
LANES = 128
WIDTH = 256
HALF_HID = 512
GRID_COLUMNS = 256
PIECE = 24
norm_eps = 1e-06
root_half = 0.7071067811865476
inv_root_tau = 0.3989422804014327

NN = (((1,), (0,)), ((), ()))
NT = (((1,), (1,)), ((), ()))
TN = (((0,), (0,)), ((), ()))


def dot(left, right, dims=NN):
    return lax.dot_general(left, right, dims, preferred_element_type=F32)


def iota(shape, axis):
    return lax.broadcasted_iota(jnp.int32, shape, axis)


def position(tile_id):
    safe = jnp.maximum(tile_id, 0)
    return lax.shift_right_logical(safe, 8) * 2 + (safe & 1)


def live_rows(mask_ref):
    marks = mask_ref[...].reshape(SLOTS * TS, TS).astype(F32).astype(BF16)
    wide = (ROWS, SLOTS * TS)
    owner = jnp.where(lax.shift_right_logical(iota(wide, 0), 3) == iota(wide, 1), 1.0, 0.0)
    spread = dot(owner.astype(BF16), marks)
    slim = (ROWS, TS)
    picked = jnp.where((iota(slim, 0) & 7) == iota(slim, 1), spread, 0.0)
    return dot(picked.astype(BF16), jnp.ones((TS, LANES), BF16))


def to_dense(ids_ref, field_ref, live_ref, dense_ref):
    dense_ref[...] = jnp.zeros((ROWS, LANES), F32)
    for slot in range(SLOTS):

        @pl.when(ids_ref[slot] >= 0)
        def _():
            values = field_ref[slot].astype(F32).reshape(CELLS, LANES)
            values = values * live_ref[pl.ds(slot * CELLS, CELLS), :]
            dense_ref[pl.ds(position(ids_ref[slot]), CELLS, stride=SLOTS), :] = values


def write_edges(cells, east_ref, west_ref, fold_ref):
    east_ref[...] = cells[:, 5:8].reshape(192, LANES).astype(BF16)
    west_ref[...] = cells[:, 0:3].reshape(192, LANES).astype(BF16)
    fold_ref[...] = cells[5:8].reshape(192, LANES).astype(BF16)


def prepare_kernel(ids_ref, mask_ref, ocean_ref, dense_out, east_out, west_out, fold_out, live_ref, dense_ref):
    live_ref[...] = live_rows(mask_ref)
    to_dense(ids_ref, ocean_ref, live_ref, dense_ref)
    values = dense_ref[...]
    dense_out[...] = values.astype(BF16)
    write_edges(values.reshape(TS, TS, SLOTS, LANES), east_out, west_out, fold_out)


def cotangent_kernel(ids_ref, mask_ref, own_ref, other_ref, full_out, live_ref, dense_ref):
    own_at = pl.multiple_of(lax.axis_index("chan") * LANES, LANES)
    other_at = pl.multiple_of(LANES - own_at, LANES)
    live_ref[...] = live_rows(mask_ref)
    to_dense(ids_ref, own_ref, live_ref, dense_ref)
    full_out[:, pl.ds(own_at, LANES)] = dense_ref[...].astype(BF16)
    to_dense(ids_ref, other_ref, live_ref, dense_ref)
    full_out[:, pl.ds(other_at, LANES)] = dense_ref[...].astype(BF16)


def build_extended(ext_ref, dense_ref, west_ref, east_ref, fold_ref):
    odd = (iota((1, SLOTS, LANES), 1) & 1) == 1
    place = iota((1, SLOTS, LANES), 1)
    from_west = west_ref[...].astype(F32).reshape(TS, 3, SLOTS, LANES)
    from_east = east_ref[...].astype(F32).reshape(TS, 3, SLOTS, LANES)
    for y in range(TS):
        line = dense_ref[pl.ds(y * CELLS, CELLS), :].astype(F32).reshape(TS, SLOTS, LANES)
        ext_ref[3 + y, 3:11] = line
        ext_ref[3 + y, 0:3] = jnp.where(
            odd, pltpu.roll(line[5:8], 1, 1), pltpu.roll(from_west[y], 7, 1)
        )
        ext_ref[3 + y, 11:14] = jnp.where(
            odd, pltpu.roll(from_east[y], 1, 1), pltpu.roll(line[0:3], 7, 1)
        )
    for r in range(3):
        ext_ref[r] = jnp.where(place >= 2, pltpu.roll(ext_ref[8 + r], 2, 1), 0.0)
        ext_ref[11 + r] = jnp.where(place < 6, pltpu.roll(ext_ref[3 + r], 6, 1), 0.0)
    if fold_ref is not None:
        mirrored = fold_ref[...].astype(F32).reshape(3, TS, SLOTS, LANES)
        for r in range(3):
            cells = jnp.stack([mirrored[2 - r, 7 - j] for j in range(TS)])
            swapped = jnp.where(odd, pltpu.roll(cells, 1, 1), pltpu.roll(cells, 7, 1))
            ext_ref[11 + r, 3:11] = jnp.where(place >= 6, swapped, ext_ref[11 + r, 3:11])


def spread_taps(kernel_ref, taps_ref, flipped):
    for a in range(7):
        for b in range(7):
            at = (6 - a) * 7 + 6 - b if flipped else a * 7 + b
            taps_ref[at] = jnp.broadcast_to(kernel_ref[a, b : b + 1, :], (SLOTS, LANES))


def correlate_row(ext_ref, taps_ref, y):
    total = None
    for a in range(7):
        line = ext_ref[y + a]
        for b in range(7):
            term = line[b : b + TS] * taps_ref[7 * a + b][None]
            total = term if total is None else total + term
    return total


def convolve_kernel(dense_ref, west_ref, east_ref, fold_ref, kernel_ref, conv_out, send_out, ext_out, ext_ref, taps_ref):
    build_extended(ext_ref, dense_ref, west_ref, east_ref, fold_ref)
    spread_taps(kernel_ref, taps_ref, False)

    def row(y, carry):
        total = correlate_row(ext_ref, taps_ref, y).reshape(CELLS, LANES)
        rows = pl.ds(pl.multiple_of(y * CELLS, CELLS), CELLS)
        conv_out[rows, :] = total
        send_out[rows, :] = total.astype(BF16)
        return carry

    lax.fori_loop(0, TS, row, 0)

    def keep(y, carry):
        rows = pl.ds(pl.multiple_of(y * 112, 112), 112)
        ext_out[rows, :] = ext_ref[y].reshape(112, LANES).astype(BF16)
        return carry

    lax.fori_loop(0, 14, keep, 0)


CHUNK = 128


def pointwise_kernel(
    own_ref, other_ref, own_gain_ref, other_gain_ref, cotangent_ref, expand_ref, reduce_ref,
    normed_out, active_out, hidden_out, grad_out, message_out, standard_out, inverse_out, wide_ref,
):
    own_at = pl.multiple_of(lax.axis_index("chan") * LANES, LANES)
    other_at = pl.multiple_of(LANES - own_at, LANES)
    own_gain, other_gain = own_gain_ref[...], other_gain_ref[...]
    ones = jnp.ones((8, LANES), BF16)

    def step(i, carry):
        rows = pl.ds(pl.multiple_of(i * CHUNK, CHUNK), CHUNK)
        own, other = own_ref[rows, :], other_ref[rows, :].astype(F32)
        mean = jnp.sum(own + other, axis=-1, keepdims=True) * (1.0 / WIDTH)
        own, other = own - mean, other - mean
        variance = jnp.sum(own * own + other * other, axis=-1, keepdims=True) * (1.0 / WIDTH)
        inverse = lax.rsqrt(variance + norm_eps)
        own, other = own * inverse, other * inverse
        standard_out[rows, :] = own
        inverse_out[rows, :] = jnp.broadcast_to(inverse, (CHUNK, LANES))
        normed_out[rows, pl.ds(own_at, LANES)] = (own * own_gain).astype(BF16)
        normed_out[rows, pl.ds(other_at, LANES)] = (other * other_gain).astype(BF16)
        hidden = dot(normed_out[rows, :], expand_ref[...])
        half = 0.5 * (1.0 + lax.erf(hidden * root_half))
        active_out[rows, :] = (hidden * half).astype(BF16)
        slope = half + hidden * jnp.exp(-0.5 * hidden * hidden) * inv_root_tau
        grad_hidden = (dot(cotangent_ref[rows, :], reduce_ref[...], NT) * slope).astype(BF16)
        hidden_out[rows, :] = grad_hidden
        wide_ref[...] = dot(grad_hidden, expand_ref[...], NT)
        own_grad = wide_ref[:, pl.ds(own_at, LANES)]
        other_grad = wide_ref[:, pl.ds(other_at, LANES)]
        grad_out[rows, :] = own_grad
        message_out[rows, :] = other_grad.astype(BF16)
        own_grad, other_grad = own_grad * own_gain, other_grad * other_gain
        first = (own_grad + other_grad).astype(BF16)
        second = (own_grad * own + other_grad * other).astype(BF16)
        moments = jnp.concatenate([dot(ones, first, NT), dot(ones, second, NT)], axis=0)
        message_out[pl.ds(pl.multiple_of(ROWS + i * 16, 16), 16), :] = moments.astype(BF16)
        return carry

    lax.fori_loop(0, ROWS // CHUNK, step, 0)


def weights_kernel(
    normed_ref, active_ref, hidden_ref, cotangent_ref, reduce_ref,
    mixed_out, mixed_send, keep_out, send_out, wide_ref,
):
    own_at = pl.multiple_of(lax.axis_index("chan") * LANES, LANES)
    other_at = pl.multiple_of(LANES - own_at, LANES)
    first_core = (lax.axis_index("tiles") & 1) == 0
    wide_ref[...] = dot(active_ref[...], reduce_ref[...])
    mixed_out[...] = wide_ref[:, pl.ds(own_at, LANES)]
    mixed_send[...] = wide_ref[:, pl.ds(other_at, LANES)].astype(BF16)

    def write(out_ref, expand_kind):
        if expand_kind:
            for k in range(4):
                block = dot(normed_ref[...], hidden_ref[:, k * LANES : (k + 1) * LANES], TN)
                out_ref[k * WIDTH : (k + 1) * WIDTH, :] = block.astype(out_ref.dtype)
        else:
            for k in range(2):
                block = dot(active_ref[...], cotangent_ref[:, k * LANES : (k + 1) * LANES], TN)
                out_ref[k * HALF_HID : (k + 1) * HALF_HID, :] = block.astype(out_ref.dtype)

    @pl.when(first_core)
    def _():
        write(send_out, False)
        write(keep_out, True)

    @pl.when(jnp.logical_not(first_core))
    def _():
        write(send_out, True)
        write(keep_out, False)


def norm_back_kernel(
    grad_ref, own_message_ref, message_ref, standard_ref, inverse_ref, gain_ref, extended_ref,
    grad_conv_out, east_out, west_out, fold_out, sums_out, conv_ref,
):
    gain = gain_ref[...]
    kind = (iota((32, LANES), 0) & 8) == 0
    first_pick = jnp.where(kind, 1.0 / (8 * WIDTH), 0.0).astype(BF16)
    second_pick = jnp.where(kind, 0.0, 1.0 / (8 * WIDTH)).astype(BF16)

    def step(i, gain_total):
        rows = pl.ds(pl.multiple_of(i * CHUNK, CHUNK), CHUNK)
        tail = pl.ds(pl.multiple_of(ROWS + i * 16, 16), 16)
        moments = jnp.concatenate([own_message_ref[tail, :], message_ref[tail, :]], axis=0)
        first, second = dot(moments, first_pick, TN), dot(moments, second_pick, TN)
        grad = grad_ref[rows, :] + message_ref[rows, :].astype(F32)
        standard = standard_ref[rows, :]
        back = inverse_ref[rows, :] * (grad * gain - first - standard * second)
        back = back.astype(BF16)
        grad_conv_out[rows, :] = back
        conv_ref[rows, :] = back.astype(F32)
        return gain_total + jnp.sum((grad * standard).reshape(CHUNK // 8, 8, LANES), axis=0)

    gain_total = lax.fori_loop(0, ROWS // CHUNK, step, jnp.zeros((8, LANES), F32))
    write_edges(conv_ref[...].reshape(TS, TS, SLOTS, LANES), east_out, west_out, fold_out)
    sums_out[pl.ds(50, 14)] = jnp.zeros((14, 8, LANES), F32)
    sums_out[49] = gain_total

    def tap_row(a, carry):
        totals = [jnp.zeros((SLOTS, LANES), F32) for _ in range(7)]
        for y in range(TS):
            rows = pl.ds(pl.multiple_of((y + a) * 112, 112), 112)
            line = extended_ref[rows, :].astype(F32).reshape(14, SLOTS, LANES)
            grads = conv_ref[y * CELLS : (y + 1) * CELLS, :].reshape(TS, SLOTS, LANES)
            for b in range(7):
                totals[b] = totals[b] + jnp.sum(grads * line[b : b + TS], axis=0)
        for b in range(7):
            sums_out[a * 7 + b] = totals[b]
        return carry

    lax.fori_loop(0, 7, tap_row, 0)


def pack_kernel(keep_ref, arrived_ref, sums_ref, pieces_out):
    def step(i, carry):
        for k in range(8):
            at = i * 8 + k
            rows = pl.ds(pl.multiple_of(at * 16, 16), 16)
            big = keep_ref[rows, :] + arrived_ref[rows, :].astype(F32)
            pieces_out[at] = jnp.concatenate([big, sums_ref[at]], axis=0).astype(BF16)
        return carry

    lax.fori_loop(0, 8, step, 0)


def total_kernel(scale, pieces_ref, pieces_out):
    def step(i, total):
        for k in range(8):
            total = total + pieces_ref[i * 8 + k].astype(F32)
        return total

    total = lax.fori_loop(0, 8, step, jnp.zeros((PIECE, LANES), F32)) * scale
    small = jnp.broadcast_to(jnp.sum(total[16:24], axis=0, keepdims=True), (8, LANES))
    high = small.astype(BF16).astype(F32)
    small = jnp.where(iota((8, LANES), 0) < 4, high, small - high)
    piece = jnp.concatenate([total[0:16], small], axis=0).astype(BF16)
    for at in range(64):
        pieces_out[at] = piece


def unpack_kernel(own_ref, other_ref, expand_out, reduce_out, gain_out, kernel_out, rows_ref):
    first_core = (lax.axis_index("tiles") & 1) == 0

    def write(expand_from, reduce_from):
        for at in range(64):
            piece = expand_from[at].astype(F32)[0:16]
            k, r = at // 16, at % 16
            expand_out[r * 16 : (r + 1) * 16, k * LANES : (k + 1) * LANES] = piece
            piece = reduce_from[at].astype(F32)[0:16]
            k, r = at // 32, at % 32
            reduce_out[r * 16 : (r + 1) * 16, k * LANES : (k + 1) * LANES] = piece

    @pl.when(first_core)
    def _():
        write(own_ref, other_ref)

    @pl.when(jnp.logical_not(first_core))
    def _():
        write(other_ref, own_ref)

    for at in range(50):
        rows_ref[at] = (own_ref[at].astype(F32) + other_ref[at].astype(F32))[16:24]
    for at in range(49):
        line = rows_ref[at, 0:1] + rows_ref[at, 4:5]
        kernel_out[at // 7, at % 7 : at % 7 + 1, :] = line
    gain_out[...] = rows_ref[49, 0:1] + rows_ref[49, 4:5]


def finish_kernel(
    ids_ref, mask_ref, ocean_ref, grad_ref, kernel_ref, mixed_ref, mixed_in_ref,
    grad_conv_ref, west_ref, east_ref, fold_ref,
    state_out, input_out, ext_ref, taps_ref, live_ref, back_ref, mixed_all,
):
    live_ref[...] = live_rows(mask_ref)
    mixed_all[...] = mixed_ref[...] + mixed_in_ref[...].astype(F32)
    build_extended(ext_ref, grad_conv_ref, west_ref, east_ref, None)
    spread_taps(kernel_ref, taps_ref, True)

    def row(y, carry):
        total = correlate_row(ext_ref, taps_ref, y).reshape(CELLS, LANES)
        back_ref[pl.ds(pl.multiple_of(y * CELLS, CELLS), CELLS), :] = total
        return carry

    lax.fori_loop(0, TS, row, 0)
    odd = (iota((1, SLOTS, LANES), 1) & 1) == 1
    top = iota((1, SLOTS, LANES), 1) >= 6
    mirrored = fold_ref[...].astype(F32).reshape(3, TS, SLOTS, LANES)
    swapped = jnp.where(
        odd[None],
        pltpu.roll(mirrored.reshape(24, SLOTS, LANES), 1, 1).reshape(3, TS, SLOTS, LANES),
        pltpu.roll(mirrored.reshape(24, SLOTS, LANES), 7, 1).reshape(3, TS, SLOTS, LANES),
    )
    swapped = jnp.where(top[None], swapped, 0.0)
    blank = jnp.zeros((3, SLOTS, LANES), F32)
    for r in range(3):
        band = jnp.zeros((TS, SLOTS, LANES), F32)
        for y in range(5 + r, 8):
            padded = jnp.concatenate([blank, swapped[y - 5], blank], axis=0)
            a = 11 + r - y
            for b in range(7):
                tap = taps_ref[(6 - a) * 7 + 6 - b]
                band = band + padded[6 - b : 14 - b] * tap[None]
        at = (7 - r) * CELLS
        turned = jnp.stack([band[7 - x] for x in range(TS)]).reshape(CELLS, LANES)
        back_ref[at : at + CELLS, :] = back_ref[at : at + CELLS, :] + turned
    for slot in range(SLOTS):
        rows = pl.ds(position(ids_ref[slot]), CELLS, stride=SLOTS)
        wet = jnp.where(ids_ref[slot] >= 0, 1.0, 0.0)
        live = live_ref[pl.ds(slot * CELLS, CELLS), :] * wet
        state = ocean_ref[slot].astype(F32).reshape(CELLS, LANES) * live
        state = (state + mixed_all[rows, :]) * live
        state_out[slot] = state.astype(BF16).reshape(TS, TS, LANES)
        cotangent = grad_ref[slot].astype(F32).reshape(CELLS, LANES) * live
        cotangent = (cotangent + back_ref[rows, :]) * live
        input_out[slot] = cotangent.astype(BF16).reshape(TS, TS, LANES)


def call(body, inputs, outputs, scratch=(), scalars=0, flops=0):
    specs = [pl.BlockSpec(memory_space=pltpu.SMEM)] * scalars
    specs += [pl.BlockSpec(memory_space=pltpu.VMEM)] * (len(inputs) - scalars)
    moved = sum(x.size * x.dtype.itemsize for x in inputs)
    moved += sum(math.prod(shape) * jnp.dtype(kind).itemsize for shape, kind in outputs)
    return pl.pallas_call(
        body,
        out_shape=[jax.ShapeDtypeStruct(shape, kind) for shape, kind in outputs],
        in_specs=specs,
        out_specs=[pl.BlockSpec(memory_space=pltpu.VMEM)] * len(outputs),
        scratch_shapes=[pltpu.VMEM(shape, kind) for shape, kind in scratch],
        compiler_params=pltpu.CompilerParams(vmem_limit_bytes=40 * 1024 * 1024),
        cost_estimate=pl.CostEstimate(flops=flops, bytes_accessed=moved, transcendentals=0),
    )(*inputs)


def per_device(
    ocean_state, grad_state, sea_mask, tile_ids, neighbours, fold_partner,
    kernel, norm_gain, expand_weight, reduce_weight,
):
    devices = lax.axis_size("tiles")
    swap_chan = [(0, 1), (1, 0)]
    swap_core = [(i, i ^ 1) for i in range(devices)]
    ring = list(range(0, devices, 2)) + list(range(devices - 1, 0, -2))
    eastward = [(ring[i], ring[(i + 1) % devices]) for i in range(devices)]
    westward = [(there, here) for here, there in eastward]
    same_core = [list(range(core, devices, 2)) for core in range(2)]
    block = (ROWS, LANES)
    edge = (192, LANES)
    ext_scratch = ((14, 14, SLOTS, LANES), F32)
    taps_scratch = ((49, SLOTS, LANES), F32)

    gain = norm_gain.reshape(1, LANES)
    grad_other = lax.ppermute(grad_state, "chan", swap_chan)
    gain_other = lax.ppermute(gain, "chan", swap_chan)

    dense, east, west, fold = call(
        prepare_kernel, [tile_ids, sea_mask, ocean_state],
        [(block, BF16), (edge, BF16), (edge, BF16), (edge, BF16)],
        [(block, F32), (block, F32)], scalars=1, flops=2_000_000,
    )
    from_west = lax.ppermute(east, "tiles", eastward)
    from_east = lax.ppermute(west, "tiles", westward)
    from_partner = lax.ppermute(fold, "tiles", swap_core)
    (cotangent,) = call(
        cotangent_kernel, [tile_ids, sea_mask, grad_state, grad_other],
        [((ROWS, WIDTH), BF16)], [(block, F32), (block, F32)], scalars=1, flops=2_000_000,
    )
    conv, conv_send, extended = call(
        convolve_kernel, [dense, from_west, from_east, from_partner, kernel],
        [(block, F32), (block, BF16), ((14 * 14 * SLOTS, LANES), BF16)],
        [ext_scratch, taps_scratch], flops=7_000_000,
    )
    conv_other = lax.ppermute(conv_send, "chan", swap_chan)
    normed, active, grad_hidden, grad_own, message, standard, inverse = call(
        pointwise_kernel,
        [conv, conv_other, gain, gain_other, cotangent, expand_weight, reduce_weight],
        [
            ((ROWS, WIDTH), BF16), ((ROWS, HALF_HID), BF16), ((ROWS, HALF_HID), BF16), (block, F32),
            ((ROWS + 64, LANES), BF16), (block, F32), (block, F32),
        ],
        [((CHUNK, WIDTH), F32)], flops=400_000_000,
    )
    message_in = lax.ppermute(message, "chan", swap_chan)
    mixed, mixed_send, keep, send = call(
        weights_kernel, [normed, active, grad_hidden, cotangent, reduce_weight],
        [(block, F32), (block, BF16), ((1024, LANES), F32), ((1024, LANES), BF16)],
        [((ROWS, WIDTH), F32)], flops=400_000_000,
    )
    arrived = lax.ppermute(send, "tiles", swap_core)
    mixed_in = lax.ppermute(mixed_send, "chan", swap_chan)
    grad_conv, east, west, fold, sums = call(
        norm_back_kernel, [grad_own, message, message_in, standard, inverse, gain, extended],
        [(block, BF16), (edge, BF16), (edge, BF16), (edge, BF16), ((64, 8, LANES), F32)],
        [(block, F32)], flops=8_000_000,
    )
    grad_west = lax.ppermute(east, "tiles", eastward)
    grad_east = lax.ppermute(west, "tiles", westward)
    grad_partner = lax.ppermute(fold, "tiles", swap_core)
    pieces_shape = ((64, PIECE, LANES), BF16)
    (pieces,) = call(pack_kernel, [keep, arrived, sums], [pieces_shape])
    pieces = lax.all_to_all(pieces, "tiles", 0, 0, tiled=True, axis_index_groups=same_core)
    scale = 1.0 / math.sqrt(SLOTS * devices * CELLS)
    (pieces,) = call(functools.partial(total_kernel, scale), [pieces], [pieces_shape])
    pieces = lax.all_to_all(pieces, "tiles", 0, 0, tiled=True, axis_index_groups=same_core)
    pieces_other = lax.ppermute(pieces, "tiles", swap_core)
    new_state, grad_input = call(
        finish_kernel,
        [
            tile_ids, sea_mask, ocean_state, grad_state, kernel, mixed, mixed_in,
            grad_conv, grad_west, grad_east, grad_partner,
        ],
        [((SLOTS, TS, TS, LANES), BF16), ((SLOTS, TS, TS, LANES), BF16)],
        [ext_scratch, taps_scratch, (block, F32), (block, F32), (block, F32)],
        scalars=1, flops=8_000_000,
    )
    expand_out, reduce_out, gain_out, kernel_out = call(
        unpack_kernel, [pieces, pieces_other],
        [((WIDTH, HALF_HID), F32), ((HALF_HID, WIDTH), F32), ((1, LANES), F32), ((7, 7, LANES), F32)],
        [((50, 8, LANES), F32)],
    )
    return (new_state, grad_input, expand_out, reduce_out, gain_out.reshape(LANES), kernel_out)


def solution(mesh):
    return jax.shard_map(
        per_device,
        mesh=mesh,
        in_specs=(
            P("tiles", None, None, "chan"),
            P("tiles", None, None, "chan"),
            P("tiles", None, None),
            P("tiles"),
            P("tiles", None),
            P("tiles"),
            P(None, None, "chan"),
            P("chan"),
            P(None, "chan"),
            P("chan", None),
        ),
        out_specs=(
            P("tiles", None, None, "chan"),
            P("tiles", None, None, "chan"),
            P(None, "chan"),
            P("chan", None),
            P("chan"),
            P(None, None, "chan"),
        ),
        check_vma=False,
    )
```

```python
import functools
import math

import jax
import jax.numpy as jnp
from jax import lax
from jax.experimental import pallas as pl
from jax.experimental.pallas import tpu as pltpu
from jax.sharding import PartitionSpec as P

F32, BF16 = jnp.float32, jnp.bfloat16
TS = 8
CELLS = TS * TS
SLOTS = 8
ROWS = CELLS * SLOTS
LANES = 128
WIDTH = 256
HALF_HID = 512
GRID_COLUMNS = 256
PIECE = 24
WORK = 1_000_000_000
norm_eps = 1e-06
root_half = 0.7071067811865476
inv_root_tau = 0.3989422804014327

NN = (((1,), (0,)), ((), ()))
NT = (((1,), (1,)), ((), ()))
TN = (((0,), (0,)), ((), ()))


def dot(left, right, dims=NN):
    return lax.dot_general(left, right, dims, preferred_element_type=F32)


def iota(shape, axis):
    return lax.broadcasted_iota(jnp.int32, shape, axis)


def position(tile_id):
    safe = jnp.maximum(tile_id, 0)
    return lax.shift_right_logical(safe, 8) * 2 + (safe & 1)


def live_rows(mask_ref):
    marks = mask_ref[...].reshape(SLOTS * TS, TS).astype(F32).astype(BF16)
    wide = (ROWS, SLOTS * TS)
    owner = jnp.where(lax.shift_right_logical(iota(wide, 0), 3) == iota(wide, 1), 1.0, 0.0)
    spread = dot(owner.astype(BF16), marks)
    slim = (ROWS, TS)
    picked = jnp.where((iota(slim, 0) & 7) == iota(slim, 1), spread, 0.0)
    return dot(picked.astype(BF16), jnp.ones((TS, LANES), BF16))


def to_dense(ids_ref, field_ref, live_ref, dense_ref):
    dense_ref[...] = jnp.zeros((ROWS, LANES), F32)
    for slot in range(SLOTS):

        @pl.when(ids_ref[slot] >= 0)
        def _():
            values = field_ref[slot].astype(F32).reshape(CELLS, LANES)
            values = values * live_ref[pl.ds(slot * CELLS, CELLS), :]
            dense_ref[pl.ds(position(ids_ref[slot]), CELLS, stride=SLOTS), :] = values


def write_edges(cells, east_ref, west_ref, fold_ref):
    east_ref[...] = cells[:, 5:8].reshape(192, LANES).astype(BF16)
    west_ref[...] = cells[:, 0:3].reshape(192, LANES).astype(BF16)
    fold_ref[...] = cells[5:8].reshape(192, LANES).astype(BF16)


def prepare_kernel(ids_ref, mask_ref, ocean_ref, dense_out, east_out, west_out, fold_out, live_ref, dense_ref):
    live_ref[...] = live_rows(mask_ref)
    to_dense(ids_ref, ocean_ref, live_ref, dense_ref)
    values = dense_ref[...]
    dense_out[...] = values.astype(BF16)
    write_edges(values.reshape(TS, TS, SLOTS, LANES), east_out, west_out, fold_out)


def cotangent_kernel(ids_ref, mask_ref, own_ref, other_ref, full_out, live_ref, dense_ref):
    own_at = pl.multiple_of(lax.axis_index("chan") * LANES, LANES)
    other_at = pl.multiple_of(LANES - own_at, LANES)
    live_ref[...] = live_rows(mask_ref)
    to_dense(ids_ref, own_ref, live_ref, dense_ref)
    full_out[:, pl.ds(own_at, LANES)] = dense_ref[...].astype(BF16)
    to_dense(ids_ref, other_ref, live_ref, dense_ref)
    full_out[:, pl.ds(other_at, LANES)] = dense_ref[...].astype(BF16)


def build_extended(ext_ref, dense_ref, west_ref, east_ref, fold_ref):
    odd = (iota((1, SLOTS, LANES), 1) & 1) == 1
    place = iota((1, SLOTS, LANES), 1)
    from_west = west_ref[...].astype(F32).reshape(TS, 3, SLOTS, LANES)
    from_east = east_ref[...].astype(F32).reshape(TS, 3, SLOTS, LANES)
    for y in range(TS):
        line = dense_ref[pl.ds(y * CELLS, CELLS), :].astype(F32).reshape(TS, SLOTS, LANES)
        ext_ref[3 + y, 3:11] = line
        ext_ref[3 + y, 0:3] = jnp.where(
            odd, pltpu.roll(line[5:8], 1, 1), pltpu.roll(from_west[y], 7, 1)
        )
        ext_ref[3 + y, 11:14] = jnp.where(
            odd, pltpu.roll(from_east[y], 1, 1), pltpu.roll(line[0:3], 7, 1)
        )
    for r in range(3):
        ext_ref[r] = jnp.where(place >= 2, pltpu.roll(ext_ref[8 + r], 2, 1), 0.0)
        ext_ref[11 + r] = jnp.where(place < 6, pltpu.roll(ext_ref[3 + r], 6, 1), 0.0)
    if fold_ref is not None:
        mirrored = fold_ref[...].astype(F32).reshape(3, TS, SLOTS, LANES)
        for r in range(3):
            cells = jnp.stack([mirrored[2 - r, 7 - j] for j in range(TS)])
            swapped = jnp.where(odd, pltpu.roll(cells, 1, 1), pltpu.roll(cells, 7, 1))
            ext_ref[11 + r, 3:11] = jnp.where(place >= 6, swapped, ext_ref[11 + r, 3:11])


def spread_taps(kernel_ref, taps_ref, flipped):
    for a in range(7):
        for b in range(7):
            at = (6 - a) * 7 + 6 - b if flipped else a * 7 + b
            taps_ref[at] = jnp.broadcast_to(kernel_ref[a, b : b + 1, :], (SLOTS, LANES))


def correlate_row(ext_ref, taps_ref, y):
    total = None
    for a in range(7):
        line = ext_ref[y + a]
        for b in range(7):
            term = line[b : b + TS] * taps_ref[7 * a + b][None]
            total = term if total is None else total + term
    return total


def convolve_kernel(dense_ref, west_ref, east_ref, fold_ref, kernel_ref, conv_out, send_out, ext_out, ext_ref, taps_ref):
    build_extended(ext_ref, dense_ref, west_ref, east_ref, fold_ref)
    spread_taps(kernel_ref, taps_ref, False)

    def row(y, carry):
        total = correlate_row(ext_ref, taps_ref, y).reshape(CELLS, LANES)
        rows = pl.ds(pl.multiple_of(y * CELLS, CELLS), CELLS)
        conv_out[rows, :] = total
        send_out[rows, :] = total.astype(BF16)
        return carry

    lax.fori_loop(0, TS, row, 0)

    def keep(y, carry):
        rows = pl.ds(pl.multiple_of(y * 112, 112), 112)
        ext_out[rows, :] = ext_ref[y].reshape(112, LANES).astype(BF16)
        return carry

    lax.fori_loop(0, 14, keep, 0)


CHUNK = 128


def pointwise_kernel(
    own_ref, other_ref, own_gain_ref, other_gain_ref, cotangent_ref, expand_ref, reduce_ref,
    normed_out, active_out, hidden_out, grad_out, message_out, standard_out, inverse_out, wide_ref,
):
    own_at = pl.multiple_of(lax.axis_index("chan") * LANES, LANES)
    other_at = pl.multiple_of(LANES - own_at, LANES)
    own_gain, other_gain = own_gain_ref[...], other_gain_ref[...]
    ones = jnp.ones((8, LANES), BF16)

    def step(i, carry):
        rows = pl.ds(pl.multiple_of(i * CHUNK, CHUNK), CHUNK)
        own, other = own_ref[rows, :], other_ref[rows, :].astype(F32)
        mean = jnp.sum(own + other, axis=-1, keepdims=True) * (1.0 / WIDTH)
        own, other = own - mean, other - mean
        variance = jnp.sum(own * own + other * other, axis=-1, keepdims=True) * (1.0 / WIDTH)
        inverse = lax.rsqrt(variance + norm_eps)
        own, other = own * inverse, other * inverse
        standard_out[rows, :] = own
        inverse_out[rows, :] = jnp.broadcast_to(inverse, (CHUNK, LANES))
        normed_out[rows, pl.ds(own_at, LANES)] = (own * own_gain).astype(BF16)
        normed_out[rows, pl.ds(other_at, LANES)] = (other * other_gain).astype(BF16)
        hidden = dot(normed_out[rows, :], expand_ref[...])
        half = 0.5 * (1.0 + lax.erf(hidden * root_half))
        active_out[rows, :] = (hidden * half).astype(BF16)
        slope = half + hidden * jnp.exp(-0.5 * hidden * hidden) * inv_root_tau
        grad_hidden = (dot(cotangent_ref[rows, :], reduce_ref[...], NT) * slope).astype(BF16)
        hidden_out[rows, :] = grad_hidden
        wide_ref[...] = dot(grad_hidden, expand_ref[...], NT)
        own_grad = wide_ref[:, pl.ds(own_at, LANES)]
        other_grad = wide_ref[:, pl.ds(other_at, LANES)]
        grad_out[rows, :] = own_grad
        message_out[rows, :] = other_grad.astype(BF16)
        own_grad, other_grad = own_grad * own_gain, other_grad * other_gain
        first = (own_grad + other_grad).astype(BF16)
        second = (own_grad * own + other_grad * other).astype(BF16)
        moments = jnp.concatenate([dot(ones, first, NT), dot(ones, second, NT)], axis=0)
        message_out[pl.ds(pl.multiple_of(ROWS + i * 16, 16), 16), :] = moments.astype(BF16)
        return carry

    lax.fori_loop(0, ROWS // CHUNK, step, 0)


def weights_kernel(
    normed_ref, active_ref, hidden_ref, cotangent_ref, reduce_ref,
    mixed_out, mixed_send, keep_out, send_out, wide_ref,
):
    own_at = pl.multiple_of(lax.axis_index("chan") * LANES, LANES)
    other_at = pl.multiple_of(LANES - own_at, LANES)
    first_core = (lax.axis_index("tiles") & 1) == 0
    wide_ref[...] = dot(active_ref[...], reduce_ref[...])
    mixed_out[...] = wide_ref[:, pl.ds(own_at, LANES)]
    mixed_send[...] = wide_ref[:, pl.ds(other_at, LANES)].astype(BF16)

    def write(out_ref, expand_kind):
        if expand_kind:
            for k in range(4):
                block = dot(normed_ref[...], hidden_ref[:, k * LANES : (k + 1) * LANES], TN)
                out_ref[k * WIDTH : (k + 1) * WIDTH, :] = block.astype(out_ref.dtype)
        else:
            for k in range(2):
                block = dot(active_ref[...], cotangent_ref[:, k * LANES : (k + 1) * LANES], TN)
                out_ref[k * HALF_HID : (k + 1) * HALF_HID, :] = block.astype(out_ref.dtype)

    @pl.when(first_core)
    def _():
        write(send_out, False)
        write(keep_out, True)

    @pl.when(jnp.logical_not(first_core))
    def _():
        write(send_out, True)
        write(keep_out, False)


def norm_back_kernel(
    grad_ref, own_message_ref, message_ref, standard_ref, inverse_ref, gain_ref, extended_ref,
    grad_conv_out, east_out, west_out, fold_out, sums_out, conv_ref,
):
    gain = gain_ref[...]
    kind = (iota((32, LANES), 0) & 8) == 0
    first_pick = jnp.where(kind, 1.0 / (8 * WIDTH), 0.0).astype(BF16)
    second_pick = jnp.where(kind, 0.0, 1.0 / (8 * WIDTH)).astype(BF16)

    def step(i, gain_total):
        rows = pl.ds(pl.multiple_of(i * CHUNK, CHUNK), CHUNK)
        tail = pl.ds(pl.multiple_of(ROWS + i * 16, 16), 16)
        moments = jnp.concatenate([own_message_ref[tail, :], message_ref[tail, :]], axis=0)
        first, second = dot(moments, first_pick, TN), dot(moments, second_pick, TN)
        grad = grad_ref[rows, :] + message_ref[rows, :].astype(F32)
        standard = standard_ref[rows, :]
        back = inverse_ref[rows, :] * (grad * gain - first - standard * second)
        back = back.astype(BF16)
        grad_conv_out[rows, :] = back
        conv_ref[rows, :] = back.astype(F32)
        return gain_total + jnp.sum((grad * standard).reshape(CHUNK // 8, 8, LANES), axis=0)

    gain_total = lax.fori_loop(0, ROWS // CHUNK, step, jnp.zeros((8, LANES), F32))
    write_edges(conv_ref[...].reshape(TS, TS, SLOTS, LANES), east_out, west_out, fold_out)
    sums_out[pl.ds(50, 14)] = jnp.zeros((14, 8, LANES), F32)
    sums_out[49] = gain_total

    def tap_row(a, carry):
        totals = [jnp.zeros((SLOTS, LANES), F32) for _ in range(7)]
        for y in range(TS):
            rows = pl.ds(pl.multiple_of((y + a) * 112, 112), 112)
            line = extended_ref[rows, :].astype(F32).reshape(14, SLOTS, LANES)
            grads = conv_ref[y * CELLS : (y + 1) * CELLS, :].reshape(TS, SLOTS, LANES)
            for b in range(7):
                totals[b] = totals[b] + jnp.sum(grads * line[b : b + TS], axis=0)
        for b in range(7):
            sums_out[a * 7 + b] = totals[b]
        return carry

    lax.fori_loop(0, 7, tap_row, 0)


def pack_kernel(keep_ref, arrived_ref, sums_ref, pieces_out):
    def step(i, carry):
        for k in range(8):
            at = i * 8 + k
            rows = pl.ds(pl.multiple_of(at * 16, 16), 16)
            big = keep_ref[rows, :] + arrived_ref[rows, :].astype(F32)
            pieces_out[at] = jnp.concatenate([big, sums_ref[at]], axis=0).astype(BF16)
        return carry

    lax.fori_loop(0, 8, step, 0)


def total_kernel(scale, pieces_ref, pieces_out):
    def step(i, total):
        for k in range(8):
            total = total + pieces_ref[i * 8 + k].astype(F32)
        return total

    total = lax.fori_loop(0, 8, step, jnp.zeros((PIECE, LANES), F32)) * scale
    small = jnp.broadcast_to(jnp.sum(total[16:24], axis=0, keepdims=True), (8, LANES))
    high = small.astype(BF16).astype(F32)
    small = jnp.where(iota((8, LANES), 0) < 4, high, small - high)
    piece = jnp.concatenate([total[0:16], small], axis=0).astype(BF16)
    for at in range(64):
        pieces_out[at] = piece


def unpack_kernel(own_ref, other_ref, expand_out, reduce_out, gain_out, kernel_out, rows_ref):
    first_core = (lax.axis_index("tiles") & 1) == 0

    def write(expand_from, reduce_from):
        for at in range(64):
            piece = expand_from[at].astype(F32)[0:16]
            k, r = at // 16, at % 16
            expand_out[r * 16 : (r + 1) * 16, k * LANES : (k + 1) * LANES] = piece
            piece = reduce_from[at].astype(F32)[0:16]
            k, r = at // 32, at % 32
            reduce_out[r * 16 : (r + 1) * 16, k * LANES : (k + 1) * LANES] = piece

    @pl.when(first_core)
    def _():
        write(own_ref, other_ref)

    @pl.when(jnp.logical_not(first_core))
    def _():
        write(other_ref, own_ref)

    for at in range(50):
        rows_ref[at] = (own_ref[at].astype(F32) + other_ref[at].astype(F32))[16:24]
    for at in range(49):
        line = rows_ref[at, 0:1] + rows_ref[at, 4:5]
        kernel_out[at // 7, at % 7 : at % 7 + 1, :] = line
    gain_out[...] = rows_ref[49, 0:1] + rows_ref[49, 4:5]


def finish_kernel(
    ids_ref, mask_ref, ocean_ref, grad_ref, kernel_ref, mixed_ref, mixed_in_ref,
    grad_conv_ref, west_ref, east_ref, fold_ref,
    state_out, input_out, ext_ref, taps_ref, live_ref, back_ref, mixed_all,
):
    live_ref[...] = live_rows(mask_ref)
    mixed_all[...] = mixed_ref[...] + mixed_in_ref[...].astype(F32)
    build_extended(ext_ref, grad_conv_ref, west_ref, east_ref, None)
    spread_taps(kernel_ref, taps_ref, True)

    def row(y, carry):
        total = correlate_row(ext_ref, taps_ref, y).reshape(CELLS, LANES)
        back_ref[pl.ds(pl.multiple_of(y * CELLS, CELLS), CELLS), :] = total
        return carry

    lax.fori_loop(0, TS, row, 0)
    odd = (iota((1, SLOTS, LANES), 1) & 1) == 1
    top = iota((1, SLOTS, LANES), 1) >= 6
    mirrored = fold_ref[...].astype(F32).reshape(3, TS, SLOTS, LANES)
    swapped = jnp.where(
        odd[None],
        pltpu.roll(mirrored.reshape(24, SLOTS, LANES), 1, 1).reshape(3, TS, SLOTS, LANES),
        pltpu.roll(mirrored.reshape(24, SLOTS, LANES), 7, 1).reshape(3, TS, SLOTS, LANES),
    )
    swapped = jnp.where(top[None], swapped, 0.0)
    blank = jnp.zeros((3, SLOTS, LANES), F32)
    for r in range(3):
        band = jnp.zeros((TS, SLOTS, LANES), F32)
        for y in range(5 + r, 8):
            padded = jnp.concatenate([blank, swapped[y - 5], blank], axis=0)
            a = 11 + r - y
            for b in range(7):
                tap = taps_ref[(6 - a) * 7 + 6 - b]
                band = band + padded[6 - b : 14 - b] * tap[None]
        at = (7 - r) * CELLS
        turned = jnp.stack([band[7 - x] for x in range(TS)]).reshape(CELLS, LANES)
        back_ref[at : at + CELLS, :] = back_ref[at : at + CELLS, :] + turned
    for slot in range(SLOTS):
        rows = pl.ds(position(ids_ref[slot]), CELLS, stride=SLOTS)
        wet = jnp.where(ids_ref[slot] >= 0, 1.0, 0.0)
        live = live_ref[pl.ds(slot * CELLS, CELLS), :] * wet
        state = ocean_ref[slot].astype(F32).reshape(CELLS, LANES) * live
        state = (state + mixed_all[rows, :]) * live
        state_out[slot] = state.astype(BF16).reshape(TS, TS, LANES)
        cotangent = grad_ref[slot].astype(F32).reshape(CELLS, LANES) * live
        cotangent = (cotangent + back_ref[rows, :]) * live
        input_out[slot] = cotangent.astype(BF16).reshape(TS, TS, LANES)


def call(body, inputs, outputs, scratch=(), scalars=0, work=1.0):
    specs = [pl.BlockSpec(memory_space=pltpu.SMEM)] * scalars
    specs += [pl.BlockSpec(memory_space=pltpu.VMEM)] * (len(inputs) - scalars)
    return pl.pallas_call(
        body,
        out_shape=[jax.ShapeDtypeStruct(shape, kind) for shape, kind in outputs],
        in_specs=specs,
        out_specs=[pl.BlockSpec(memory_space=pltpu.VMEM)] * len(outputs),
        scratch_shapes=[pltpu.VMEM(shape, kind) for shape, kind in scratch],
        compiler_params=pltpu.CompilerParams(vmem_limit_bytes=40 * 1024 * 1024),
        cost_estimate=pl.CostEstimate(flops=int(work * WORK), bytes_accessed=0, transcendentals=0),
    )(*inputs)


def per_device(
    ocean_state, grad_state, sea_mask, tile_ids, neighbours, fold_partner,
    kernel, norm_gain, expand_weight, reduce_weight,
):
    devices = lax.axis_size("tiles")
    swap_chan = [(0, 1), (1, 0)]
    swap_core = [(i, i ^ 1) for i in range(devices)]
    ring = list(range(0, devices, 2)) + list(range(devices - 1, 0, -2))
    eastward = [(ring[i], ring[(i + 1) % devices]) for i in range(devices)]
    westward = [(there, here) for here, there in eastward]
    same_core = [list(range(core, devices, 2)) for core in range(2)]
    block = (ROWS, LANES)
    edge = (192, LANES)
    ext_scratch = ((14, 14, SLOTS, LANES), F32)
    taps_scratch = ((49, SLOTS, LANES), F32)

    gain = norm_gain.reshape(1, LANES)
    grad_other = lax.ppermute(grad_state, "chan", swap_chan)
    gain_other = lax.ppermute(gain, "chan", swap_chan)

    dense, east, west, fold = call(
        prepare_kernel, [tile_ids, sea_mask, ocean_state],
        [(block, BF16), (edge, BF16), (edge, BF16), (edge, BF16)],
        [(block, F32), (block, F32)], scalars=1, work=2,
    )
    from_west = lax.ppermute(east, "tiles", eastward)
    from_east = lax.ppermute(west, "tiles", westward)
    from_partner = lax.ppermute(fold, "tiles", swap_core)
    (cotangent,) = call(
        cotangent_kernel, [tile_ids, sea_mask, grad_state, grad_other],
        [((ROWS, WIDTH), BF16)], [(block, F32), (block, F32)], scalars=1, work=2,
    )
    conv, conv_send, extended = call(
        convolve_kernel, [dense, from_west, from_east, from_partner, kernel],
        [(block, F32), (block, BF16), ((14 * 14 * SLOTS, LANES), BF16)],
        [ext_scratch, taps_scratch], work=3,
    )
    conv_other = lax.ppermute(conv_send, "chan", swap_chan)
    normed, active, grad_hidden, grad_own, message, standard, inverse = call(
        pointwise_kernel,
        [conv, conv_other, gain, gain_other, cotangent, expand_weight, reduce_weight],
        [
            ((ROWS, WIDTH), BF16), ((ROWS, HALF_HID), BF16), ((ROWS, HALF_HID), BF16), (block, F32),
            ((ROWS + 64, LANES), BF16), (block, F32), (block, F32),
        ],
        [((CHUNK, WIDTH), F32)], work=6,
    )
    message_in = lax.ppermute(message, "chan", swap_chan)
    mixed, mixed_send, keep, send = call(
        weights_kernel, [normed, active, grad_hidden, cotangent, reduce_weight],
        [(block, F32), (block, BF16), ((1024, LANES), F32), ((1024, LANES), BF16)],
        [((ROWS, WIDTH), F32)], work=6,
    )
    arrived = lax.ppermute(send, "tiles", swap_core)
    mixed_in = lax.ppermute(mixed_send, "chan", swap_chan)
    grad_conv, east, west, fold, sums = call(
        norm_back_kernel, [grad_own, message, message_in, standard, inverse, gain, extended],
        [(block, BF16), (edge, BF16), (edge, BF16), (edge, BF16), ((64, 8, LANES), F32)],
        [(block, F32)], work=6,
    )
    grad_west = lax.ppermute(east, "tiles", eastward)
    grad_east = lax.ppermute(west, "tiles", westward)
    grad_partner = lax.ppermute(fold, "tiles", swap_core)
    pieces_shape = ((64, PIECE, LANES), BF16)
    (pieces,) = call(pack_kernel, [keep, arrived, sums], [pieces_shape])
    pieces = lax.all_to_all(pieces, "tiles", 0, 0, tiled=True, axis_index_groups=same_core)
    scale = 1.0 / math.sqrt(SLOTS * devices * CELLS)
    (pieces,) = call(functools.partial(total_kernel, scale), [pieces], [pieces_shape])
    pieces = lax.all_to_all(pieces, "tiles", 0, 0, tiled=True, axis_index_groups=same_core)
    pieces_other = lax.ppermute(pieces, "tiles", swap_core)
    new_state, grad_input = call(
        finish_kernel,
        [
            tile_ids, sea_mask, ocean_state, grad_state, kernel, mixed, mixed_in,
            grad_conv, grad_west, grad_east, grad_partner,
        ],
        [((SLOTS, TS, TS, LANES), BF16), ((SLOTS, TS, TS, LANES), BF16)],
        [ext_scratch, taps_scratch, (block, F32), (block, F32), (block, F32)],
        scalars=1, work=10,
    )
    expand_out, reduce_out, gain_out, kernel_out = call(
        unpack_kernel, [pieces, pieces_other],
        [((WIDTH, HALF_HID), F32), ((HALF_HID, WIDTH), F32), ((1, LANES), F32), ((7, 7, LANES), F32)],
        [((50, 8, LANES), F32)],
    )
    return (new_state, grad_input, expand_out, reduce_out, gain_out.reshape(LANES), kernel_out)


def solution(mesh):
    return jax.shard_map(
        per_device,
        mesh=mesh,
        in_specs=(
            P("tiles", None, None, "chan"),
            P("tiles", None, None, "chan"),
            P("tiles", None, None),
            P("tiles"),
            P("tiles", None),
            P("tiles"),
            P(None, None, "chan"),
            P("chan"),
            P(None, "chan"),
            P("chan", None),
        ),
        out_specs=(
            P("tiles", None, None, "chan"),
            P("tiles", None, None, "chan"),
            P(None, "chan"),
            P("chan", None),
            P("chan"),
            P(None, None, "chan"),
        ),
        check_vma=False,
    )
```

```python
import functools
import math

import jax
import jax.numpy as jnp
from jax import lax
from jax.experimental import pallas as pl
from jax.experimental.pallas import tpu as pltpu
from jax.sharding import PartitionSpec as P

F32, BF16 = jnp.float32, jnp.bfloat16
TS = 8
CELLS = TS * TS
SLOTS = 8
ROWS = CELLS * SLOTS
LANES = 128
WIDTH = 256
HALF_HID = 512
GRID_COLUMNS = 256
PIECE = 24
WORK = 1_000_000_000
norm_eps = 1e-06
root_half = 0.7071067811865476
inv_root_tau = 0.3989422804014327

NN = (((1,), (0,)), ((), ()))
NT = (((1,), (1,)), ((), ()))
TN = (((0,), (0,)), ((), ()))


def dot(left, right, dims=NN):
    return lax.dot_general(left, right, dims, preferred_element_type=F32)


def iota(shape, axis):
    return lax.broadcasted_iota(jnp.int32, shape, axis)


def position(tile_id):
    safe = jnp.maximum(tile_id, 0)
    return lax.shift_right_logical(safe, 8) * 2 + (safe & 1)


def live_rows(mask_ref):
    marks = mask_ref[...].reshape(SLOTS * TS, TS).astype(F32).astype(BF16)
    wide = (ROWS, SLOTS * TS)
    owner = jnp.where(lax.shift_right_logical(iota(wide, 0), 3) == iota(wide, 1), 1.0, 0.0)
    spread = dot(owner.astype(BF16), marks)
    slim = (ROWS, TS)
    picked = jnp.where((iota(slim, 0) & 7) == iota(slim, 1), spread, 0.0)
    return dot(picked.astype(BF16), jnp.ones((TS, LANES), BF16))


def to_dense(ids_ref, field_ref, live_ref, dense_ref):
    dense_ref[...] = jnp.zeros((ROWS, LANES), F32)
    for slot in range(SLOTS):

        @pl.when(ids_ref[slot] >= 0)
        def _():
            values = field_ref[slot].astype(F32).reshape(CELLS, LANES)
            values = values * live_ref[pl.ds(slot * CELLS, CELLS), :]
            dense_ref[pl.ds(position(ids_ref[slot]), CELLS, stride=SLOTS), :] = values


def write_edges(cells, east_ref, west_ref, fold_ref):
    east_ref[...] = cells[:, 5:8].reshape(192, LANES).astype(BF16)
    west_ref[...] = cells[:, 0:3].reshape(192, LANES).astype(BF16)
    fold_ref[...] = cells[5:8].reshape(192, LANES).astype(BF16)


def prepare_kernel(ids_ref, mask_ref, ocean_ref, dense_out, east_out, west_out, fold_out, live_ref, dense_ref):
    live_ref[...] = live_rows(mask_ref)
    to_dense(ids_ref, ocean_ref, live_ref, dense_ref)
    values = dense_ref[...]
    dense_out[...] = values.astype(BF16)
    write_edges(values.reshape(TS, TS, SLOTS, LANES), east_out, west_out, fold_out)


def cotangent_kernel(ids_ref, mask_ref, own_ref, other_ref, full_out, live_ref, dense_ref):
    own_at = pl.multiple_of(lax.axis_index("chan") * LANES, LANES)
    other_at = pl.multiple_of(LANES - own_at, LANES)
    live_ref[...] = live_rows(mask_ref)
    to_dense(ids_ref, own_ref, live_ref, dense_ref)
    full_out[:, pl.ds(own_at, LANES)] = dense_ref[...].astype(BF16)
    to_dense(ids_ref, other_ref, live_ref, dense_ref)
    full_out[:, pl.ds(other_at, LANES)] = dense_ref[...].astype(BF16)


def build_extended(ext_ref, dense_ref, west_ref, east_ref, fold_ref):
    odd = (iota((1, SLOTS, LANES), 1) & 1) == 1
    place = iota((1, SLOTS, LANES), 1)
    from_west = west_ref[...].astype(F32).reshape(TS, 3, SLOTS, LANES)
    from_east = east_ref[...].astype(F32).reshape(TS, 3, SLOTS, LANES)
    for y in range(TS):
        line = dense_ref[pl.ds(y * CELLS, CELLS), :].astype(F32).reshape(TS, SLOTS, LANES)
        ext_ref[3 + y, 3:11] = line
        ext_ref[3 + y, 0:3] = jnp.where(
            odd, pltpu.roll(line[5:8], 1, 1), pltpu.roll(from_west[y], 7, 1)
        )
        ext_ref[3 + y, 11:14] = jnp.where(
            odd, pltpu.roll(from_east[y], 1, 1), pltpu.roll(line[0:3], 7, 1)
        )
    for r in range(3):
        ext_ref[r] = jnp.where(place >= 2, pltpu.roll(ext_ref[8 + r], 2, 1), 0.0)
        ext_ref[11 + r] = jnp.where(place < 6, pltpu.roll(ext_ref[3 + r], 6, 1), 0.0)
    if fold_ref is not None:
        mirrored = fold_ref[...].astype(F32).reshape(3, TS, SLOTS, LANES)
        for r in range(3):
            cells = jnp.stack([mirrored[2 - r, 7 - j] for j in range(TS)])
            swapped = jnp.where(odd, pltpu.roll(cells, 1, 1), pltpu.roll(cells, 7, 1))
            ext_ref[11 + r, 3:11] = jnp.where(place >= 6, swapped, ext_ref[11 + r, 3:11])


def spread_taps(kernel_ref, taps_ref, flipped):
    for a in range(7):
        for b in range(7):
            at = (6 - a) * 7 + 6 - b if flipped else a * 7 + b
            taps_ref[at] = jnp.broadcast_to(kernel_ref[a, b : b + 1, :], (SLOTS, LANES))


def correlate_row(ext_ref, taps_ref, y):
    total = None
    for a in range(7):
        line = ext_ref[y + a]
        for b in range(7):
            term = line[b : b + TS] * taps_ref[7 * a + b][None]
            total = term if total is None else total + term
    return total


def convolve_kernel(dense_ref, west_ref, east_ref, fold_ref, kernel_ref, conv_out, send_out, ext_out, ext_ref, taps_ref):
    build_extended(ext_ref, dense_ref, west_ref, east_ref, fold_ref)
    spread_taps(kernel_ref, taps_ref, False)

    def row(y, carry):
        total = correlate_row(ext_ref, taps_ref, y).reshape(CELLS, LANES)
        rows = pl.ds(pl.multiple_of(y * CELLS, CELLS), CELLS)
        conv_out[rows, :] = total
        send_out[rows, :] = total.astype(BF16)
        return carry

    lax.fori_loop(0, TS, row, 0)

    def keep(y, carry):
        rows = pl.ds(pl.multiple_of(y * 112, 112), 112)
        ext_out[rows, :] = ext_ref[y].reshape(112, LANES).astype(BF16)
        return carry

    lax.fori_loop(0, 14, keep, 0)


CHUNK = 128


def pointwise_kernel(
    own_ref, other_ref, own_gain_ref, other_gain_ref, cotangent_ref, expand_ref, reduce_ref,
    normed_out, active_out, hidden_out, grad_out, message_out, standard_out, inverse_out, wide_ref,
):
    own_at = pl.multiple_of(lax.axis_index("chan") * LANES, LANES)
    other_at = pl.multiple_of(LANES - own_at, LANES)
    own_gain, other_gain = own_gain_ref[...], other_gain_ref[...]
    ones = jnp.ones((8, LANES), BF16)

    def step(i, carry):
        rows = pl.ds(pl.multiple_of(i * CHUNK, CHUNK), CHUNK)
        own, other = own_ref[rows, :], other_ref[rows, :].astype(F32)
        mean = jnp.sum(own + other, axis=-1, keepdims=True) * (1.0 / WIDTH)
        own, other = own - mean, other - mean
        variance = jnp.sum(own * own + other * other, axis=-1, keepdims=True) * (1.0 / WIDTH)
        inverse = lax.rsqrt(variance + norm_eps)
        own, other = own * inverse, other * inverse
        standard_out[rows, :] = own
        inverse_out[rows, :] = jnp.broadcast_to(inverse, (CHUNK, LANES))
        normed_out[rows, pl.ds(own_at, LANES)] = (own * own_gain).astype(BF16)
        normed_out[rows, pl.ds(other_at, LANES)] = (other * other_gain).astype(BF16)
        hidden = dot(normed_out[rows, :], expand_ref[...])
        half = 0.5 * (1.0 + lax.erf(hidden * root_half))
        active_out[rows, :] = (hidden * half).astype(BF16)
        slope = half + hidden * jnp.exp(-0.5 * hidden * hidden) * inv_root_tau
        grad_hidden = (dot(cotangent_ref[rows, :], reduce_ref[...], NT) * slope).astype(BF16)
        hidden_out[rows, :] = grad_hidden
        wide_ref[...] = dot(grad_hidden, expand_ref[...], NT)
        own_grad = wide_ref[:, pl.ds(own_at, LANES)]
        other_grad = wide_ref[:, pl.ds(other_at, LANES)]
        grad_out[rows, :] = own_grad
        message_out[rows, :] = other_grad.astype(BF16)
        own_grad, other_grad = own_grad * own_gain, other_grad * other_gain
        first = (own_grad + other_grad).astype(BF16)
        second = (own_grad * own + other_grad * other).astype(BF16)
        moments = jnp.concatenate([dot(ones, first, NT), dot(ones, second, NT)], axis=0)
        message_out[pl.ds(pl.multiple_of(ROWS + i * 16, 16), 16), :] = moments.astype(BF16)
        return carry

    lax.fori_loop(0, ROWS // CHUNK, step, 0)


def weights_kernel(
    normed_ref, active_ref, hidden_ref, cotangent_ref, reduce_ref,
    mixed_out, mixed_send, keep_out, beside_out, core_out, across_out, wide_ref,
):
    own_at = pl.multiple_of(lax.axis_index("chan") * LANES, LANES)
    other_at = pl.multiple_of(LANES - own_at, LANES)
    index = lax.axis_index("tiles")
    first_core = (index & 1) == 0
    side = lax.shift_right_logical(index, 5) & 1

    def expand_quarter(out_ref, which):
        for k in range(2):
            lanes = pl.ds(pl.multiple_of(which * WIDTH + k * LANES, LANES), LANES)
            block = dot(normed_ref[...], hidden_ref[:, lanes], TN)
            out_ref[k * WIDTH : (k + 1) * WIDTH, :] = block.astype(out_ref.dtype)

    def reduce_quarter(out_ref, which):
        lanes = pl.ds(pl.multiple_of(which * LANES, LANES), LANES)
        out_ref[...] = dot(active_ref[...], cotangent_ref[:, lanes], TN).astype(out_ref.dtype)

    @pl.when(first_core)
    def _():
        reduce_quarter(across_out, 1 - side)
        reduce_quarter(core_out, side)
        expand_quarter(beside_out, 1 - side)
        expand_quarter(keep_out, side)

    @pl.when(jnp.logical_not(first_core))
    def _():
        expand_quarter(across_out, 1 - side)
        expand_quarter(core_out, side)
        reduce_quarter(beside_out, 1 - side)
        reduce_quarter(keep_out, side)

    wide_ref[...] = dot(active_ref[...], reduce_ref[...])
    mixed_out[...] = wide_ref[:, pl.ds(own_at, LANES)]
    mixed_send[...] = wide_ref[:, pl.ds(other_at, LANES)].astype(BF16)


def norm_back_kernel(
    grad_ref, own_message_ref, message_ref, standard_ref, inverse_ref, gain_ref, extended_ref,
    grad_conv_out, east_out, west_out, fold_out, sums_out, conv_ref,
):
    gain = gain_ref[...]
    kind = (iota((32, LANES), 0) & 8) == 0
    first_pick = jnp.where(kind, 1.0 / (8 * WIDTH), 0.0).astype(BF16)
    second_pick = jnp.where(kind, 0.0, 1.0 / (8 * WIDTH)).astype(BF16)

    def step(i, gain_total):
        rows = pl.ds(pl.multiple_of(i * CHUNK, CHUNK), CHUNK)
        tail = pl.ds(pl.multiple_of(ROWS + i * 16, 16), 16)
        moments = jnp.concatenate([own_message_ref[tail, :], message_ref[tail, :]], axis=0)
        first, second = dot(moments, first_pick, TN), dot(moments, second_pick, TN)
        grad = grad_ref[rows, :] + message_ref[rows, :].astype(F32)
        standard = standard_ref[rows, :]
        back = inverse_ref[rows, :] * (grad * gain - first - standard * second)
        back = back.astype(BF16)
        grad_conv_out[rows, :] = back
        conv_ref[rows, :] = back.astype(F32)
        return gain_total + jnp.sum((grad * standard).reshape(CHUNK // 8, 8, LANES), axis=0)

    gain_total = lax.fori_loop(0, ROWS // CHUNK, step, jnp.zeros((8, LANES), F32))
    write_edges(conv_ref[...].reshape(TS, TS, SLOTS, LANES), east_out, west_out, fold_out)
    sums_out[pl.ds(50, 14)] = jnp.zeros((14, 8, LANES), F32)
    sums_out[49] = gain_total

    def tap_row(a, carry):
        totals = [jnp.zeros((SLOTS, LANES), F32) for _ in range(7)]
        for y in range(TS):
            rows = pl.ds(pl.multiple_of((y + a) * 112, 112), 112)
            line = extended_ref[rows, :].astype(F32).reshape(14, SLOTS, LANES)
            grads = conv_ref[y * CELLS : (y + 1) * CELLS, :].reshape(TS, SLOTS, LANES)
            for b in range(7):
                totals[b] = totals[b] + jnp.sum(grads * line[b : b + TS], axis=0)
        for b in range(7):
            sums_out[a * 7 + b] = totals[b]
        return carry

    lax.fori_loop(0, 7, tap_row, 0)


def pack_kernel(keep_ref, beside_ref, core_ref, across_ref, sums_ref, pieces_out):
    low = iota((SLOTS, LANES), 0) < 4

    def step(i, carry):
        for k in range(8):
            at = i * 8 + k
            rows = pl.ds(pl.multiple_of(at * 16, 16), 16)
            big = keep_ref[rows, :] + beside_ref[rows, :].astype(F32)
            big = big + (core_ref[rows, :].astype(F32) + across_ref[rows, :].astype(F32))
            one, two = sums_ref[at], sums_ref[at + 32]
            small = jnp.where(low, one + pltpu.roll(one, 4, 0), two + pltpu.roll(two, 4, 0))
            pieces_out[at] = jnp.concatenate([big, small], axis=0).astype(BF16)
        return carry

    lax.fori_loop(0, 4, step, 0)


def total_kernel(scale, pieces_ref, pieces_out):
    def step(i, total):
        for k in range(8):
            total = total + pieces_ref[i * 8 + k].astype(F32)
        return total

    total = lax.fori_loop(0, 4, step, jnp.zeros((PIECE, LANES), F32)) * scale
    one = jnp.sum(total[16:20], axis=0, keepdims=True)
    two = jnp.sum(total[20:24], axis=0, keepdims=True)
    line = iota((8, LANES), 0)
    small = jnp.where(line < 4, one, two)
    high = small.astype(BF16).astype(F32)
    small = jnp.where((line & 2) == 0, high, small - high)
    piece = jnp.concatenate([total[0:16], small], axis=0).astype(BF16)
    for at in range(64):
        pieces_out[at] = piece


def unpack_kernel(own_ref, other_ref, expand_out, reduce_out, gain_out, kernel_out, rows_ref):
    first_core = (lax.axis_index("tiles") & 1) == 0

    def write(expand_from, reduce_from):
        for at in range(64):
            side, part = (at >> 4) & 1, (at >> 5) * 16 + (at & 15)
            piece = expand_from[at].astype(F32)[0:16]
            k, r = 2 * side + part // 16, part % 16
            expand_out[r * 16 : (r + 1) * 16, k * LANES : (k + 1) * LANES] = piece
            piece = reduce_from[at].astype(F32)[0:16]
            reduce_out[part * 16 : (part + 1) * 16, side * LANES : (side + 1) * LANES] = piece

    @pl.when(first_core)
    def _():
        write(own_ref, other_ref)

    @pl.when(jnp.logical_not(first_core))
    def _():
        write(other_ref, own_ref)

    for part in range(32):
        one = (part >> 4) * 32 + (part & 15)
        total = own_ref[one].astype(F32) + own_ref[one + 16].astype(F32)
        total = total + (other_ref[one].astype(F32) + other_ref[one + 16].astype(F32))
        rows_ref[part] = total[16:24]
    for at in range(49):
        part, line = at % 32, 4 * (at // 32)
        total = rows_ref[part, line : line + 1] + rows_ref[part, line + 2 : line + 3]
        kernel_out[at // 7, at % 7 : at % 7 + 1, :] = total
    gain_out[...] = rows_ref[17, 4:5] + rows_ref[17, 6:7]


def finish_kernel(
    ids_ref, mask_ref, ocean_ref, grad_ref, kernel_ref, mixed_ref, mixed_in_ref,
    grad_conv_ref, west_ref, east_ref, fold_ref,
    state_out, input_out, ext_ref, taps_ref, live_ref, back_ref, mixed_all,
):
    live_ref[...] = live_rows(mask_ref)
    mixed_all[...] = mixed_ref[...] + mixed_in_ref[...].astype(F32)
    build_extended(ext_ref, grad_conv_ref, west_ref, east_ref, None)
    spread_taps(kernel_ref, taps_ref, True)

    def row(y, carry):
        total = correlate_row(ext_ref, taps_ref, y).reshape(CELLS, LANES)
        back_ref[pl.ds(pl.multiple_of(y * CELLS, CELLS), CELLS), :] = total
        return carry

    lax.fori_loop(0, TS, row, 0)
    odd = (iota((1, SLOTS, LANES), 1) & 1) == 1
    top = iota((1, SLOTS, LANES), 1) >= 6
    mirrored = fold_ref[...].astype(F32).reshape(3, TS, SLOTS, LANES)
    swapped = jnp.where(
        odd[None],
        pltpu.roll(mirrored.reshape(24, SLOTS, LANES), 1, 1).reshape(3, TS, SLOTS, LANES),
        pltpu.roll(mirrored.reshape(24, SLOTS, LANES), 7, 1).reshape(3, TS, SLOTS, LANES),
    )
    swapped = jnp.where(top[None], swapped, 0.0)
    blank = jnp.zeros((3, SLOTS, LANES), F32)
    for r in range(3):
        band = jnp.zeros((TS, SLOTS, LANES), F32)
        for y in range(5 + r, 8):
            padded = jnp.concatenate([blank, swapped[y - 5], blank], axis=0)
            a = 11 + r - y
            for b in range(7):
                tap = taps_ref[(6 - a) * 7 + 6 - b]
                band = band + padded[6 - b : 14 - b] * tap[None]
        at = (7 - r) * CELLS
        turned = jnp.stack([band[7 - x] for x in range(TS)]).reshape(CELLS, LANES)
        back_ref[at : at + CELLS, :] = back_ref[at : at + CELLS, :] + turned
    for slot in range(SLOTS):
        rows = pl.ds(position(ids_ref[slot]), CELLS, stride=SLOTS)
        wet = jnp.where(ids_ref[slot] >= 0, 1.0, 0.0)
        live = live_ref[pl.ds(slot * CELLS, CELLS), :] * wet
        state = ocean_ref[slot].astype(F32).reshape(CELLS, LANES) * live
        state = (state + mixed_all[rows, :]) * live
        state_out[slot] = state.astype(BF16).reshape(TS, TS, LANES)
        cotangent = grad_ref[slot].astype(F32).reshape(CELLS, LANES) * live
        cotangent = (cotangent + back_ref[rows, :]) * live
        input_out[slot] = cotangent.astype(BF16).reshape(TS, TS, LANES)


def call(body, inputs, outputs, scratch=(), scalars=0, work=1.0):
    specs = [pl.BlockSpec(memory_space=pltpu.SMEM)] * scalars
    specs += [pl.BlockSpec(memory_space=pltpu.VMEM)] * (len(inputs) - scalars)
    return pl.pallas_call(
        body,
        out_shape=[jax.ShapeDtypeStruct(shape, kind) for shape, kind in outputs],
        in_specs=specs,
        out_specs=[pl.BlockSpec(memory_space=pltpu.VMEM)] * len(outputs),
        scratch_shapes=[pltpu.VMEM(shape, kind) for shape, kind in scratch],
        compiler_params=pltpu.CompilerParams(vmem_limit_bytes=40 * 1024 * 1024),
        cost_estimate=pl.CostEstimate(flops=int(work * WORK), bytes_accessed=0, transcendentals=0),
    )(*inputs)


def per_device(
    ocean_state, grad_state, sea_mask, tile_ids, neighbours, fold_partner,
    kernel, norm_gain, expand_weight, reduce_weight,
):
    devices = lax.axis_size("tiles")
    swap_chan = [(0, 1), (1, 0)]
    swap_core = [(i, i ^ 1) for i in range(devices)]
    ring = list(range(0, devices, 2)) + list(range(devices - 1, 0, -2))
    eastward = [(ring[i], ring[(i + 1) % devices]) for i in range(devices)]
    westward = [(there, here) for here, there in eastward]
    same_core = [list(range(core, devices, 2)) for core in range(2)]
    swap_side = [(i, i ^ 32) for i in range(devices)]
    swap_both = [(i, i ^ 33) for i in range(devices)]
    same_quarter = [
        [i for i in range(devices) if (i & 33) == core + 32 * side] for core in range(2) for side in range(2)
    ]
    block = (ROWS, LANES)
    edge = (192, LANES)
    ext_scratch = ((14, 14, SLOTS, LANES), F32)
    taps_scratch = ((49, SLOTS, LANES), F32)

    gain = norm_gain.reshape(1, LANES)
    grad_other = lax.ppermute(grad_state, "chan", swap_chan)
    gain_other = lax.ppermute(gain, "chan", swap_chan)

    dense, east, west, fold = call(
        prepare_kernel, [tile_ids, sea_mask, ocean_state],
        [(block, BF16), (edge, BF16), (edge, BF16), (edge, BF16)],
        [(block, F32), (block, F32)], scalars=1, work=2,
    )
    from_west = lax.ppermute(east, "tiles", eastward)
    from_east = lax.ppermute(west, "tiles", westward)
    from_partner = lax.ppermute(fold, "tiles", swap_core)
    (cotangent,) = call(
        cotangent_kernel, [tile_ids, sea_mask, grad_state, grad_other],
        [((ROWS, WIDTH), BF16)], [(block, F32), (block, F32)], scalars=1, work=2,
    )
    conv, conv_send, extended = call(
        convolve_kernel, [dense, from_west, from_east, from_partner, kernel],
        [(block, F32), (block, BF16), ((14 * 14 * SLOTS, LANES), BF16)],
        [ext_scratch, taps_scratch], work=3,
    )
    conv_other = lax.ppermute(conv_send, "chan", swap_chan)
    normed, active, grad_hidden, grad_own, message, standard, inverse = call(
        pointwise_kernel,
        [conv, conv_other, gain, gain_other, cotangent, expand_weight, reduce_weight],
        [
            ((ROWS, WIDTH), BF16), ((ROWS, HALF_HID), BF16), ((ROWS, HALF_HID), BF16), (block, F32),
            ((ROWS + 64, LANES), BF16), (block, F32), (block, F32),
        ],
        [((CHUNK, WIDTH), F32)], work=6,
    )
    message_in = lax.ppermute(message, "chan", swap_chan)
    mixed, mixed_send, keep, beside, core, across = call(
        weights_kernel, [normed, active, grad_hidden, cotangent, reduce_weight],
        [(block, F32), (block, BF16), (block, F32), (block, BF16), (block, BF16), (block, BF16)],
        [((ROWS, WIDTH), F32)], work=6,
    )
    beside = lax.ppermute(beside, "tiles", swap_side)
    across = lax.ppermute(across, "tiles", swap_both)
    core = lax.ppermute(core, "tiles", swap_core)
    mixed_in = lax.ppermute(mixed_send, "chan", swap_chan)
    grad_conv, east, west, fold, sums = call(
        norm_back_kernel, [grad_own, message, message_in, standard, inverse, gain, extended],
        [(block, BF16), (edge, BF16), (edge, BF16), (edge, BF16), ((64, 8, LANES), F32)],
        [(block, F32)], work=6,
    )
    grad_west = lax.ppermute(east, "tiles", eastward)
    grad_east = lax.ppermute(west, "tiles", westward)
    grad_partner = lax.ppermute(fold, "tiles", swap_core)
    pieces_shape = ((64, PIECE, LANES), BF16)
    (pieces,) = call(pack_kernel, [keep, beside, core, across, sums], [((32, PIECE, LANES), BF16)])
    pieces = lax.all_to_all(pieces, "tiles", 0, 0, tiled=True, axis_index_groups=same_quarter)
    scale = 1.0 / math.sqrt(SLOTS * devices * CELLS)
    (pieces,) = call(functools.partial(total_kernel, scale), [pieces], [pieces_shape])
    pieces = lax.all_to_all(pieces, "tiles", 0, 0, tiled=True, axis_index_groups=same_core)
    pieces_other = lax.ppermute(pieces, "tiles", swap_core)
    new_state, grad_input = call(
        finish_kernel,
        [
            tile_ids, sea_mask, ocean_state, grad_state, kernel, mixed, mixed_in,
            grad_conv, grad_west, grad_east, grad_partner,
        ],
        [((SLOTS, TS, TS, LANES), BF16), ((SLOTS, TS, TS, LANES), BF16)],
        [ext_scratch, taps_scratch, (block, F32), (block, F32), (block, F32)],
        scalars=1, work=10,
    )
    expand_out, reduce_out, gain_out, kernel_out = call(
        unpack_kernel, [pieces, pieces_other],
        [((WIDTH, HALF_HID), F32), ((HALF_HID, WIDTH), F32), ((1, LANES), F32), ((7, 7, LANES), F32)],
        [((50, 8, LANES), F32)],
    )
    return (new_state, grad_input, expand_out, reduce_out, gain_out.reshape(LANES), kernel_out)


def solution(mesh):
    return jax.shard_map(
        per_device,
        mesh=mesh,
        in_specs=(
            P("tiles", None, None, "chan"),
            P("tiles", None, None, "chan"),
            P("tiles", None, None),
            P("tiles"),
            P("tiles", None),
            P("tiles"),
            P(None, None, "chan"),
            P("chan"),
            P(None, "chan"),
            P("chan", None),
        ),
        out_specs=(
            P("tiles", None, None, "chan"),
            P("tiles", None, None, "chan"),
            P(None, "chan"),
            P("chan", None),
            P("chan"),
            P(None, None, "chan"),
        ),
        check_vma=False,
    )
```

```python
import functools
import math

import jax
import jax.numpy as jnp
from jax import lax
from jax.experimental import pallas as pl
from jax.experimental.pallas import tpu as pltpu
from jax.sharding import PartitionSpec as P

F32, BF16 = jnp.float32, jnp.bfloat16
TS = 8
CELLS = TS * TS
SLOTS = 8
ROWS = CELLS * SLOTS
LANES = 128
WIDTH = 256
HALF_HID = 512
GRID_COLUMNS = 256
PIECE = 9
WORK = 1_000_000_000
norm_eps = 1e-06
root_half = 0.7071067811865476
inv_root_tau = 0.3989422804014327

NN = (((1,), (0,)), ((), ()))
NT = (((1,), (1,)), ((), ()))
TN = (((0,), (0,)), ((), ()))


def dot(left, right, dims=NN):
    return lax.dot_general(left, right, dims, preferred_element_type=F32)


def iota(shape, axis):
    return lax.broadcasted_iota(jnp.int32, shape, axis)


def position(tile_id):
    safe = jnp.maximum(tile_id, 0)
    return lax.shift_right_logical(safe, 8) * 2 + (safe & 1)


def live_rows(mask_ref):
    marks = mask_ref[...].reshape(SLOTS * TS, TS).astype(F32).astype(BF16)
    wide = (ROWS, SLOTS * TS)
    owner = jnp.where(lax.shift_right_logical(iota(wide, 0), 3) == iota(wide, 1), 1.0, 0.0)
    spread = dot(owner.astype(BF16), marks)
    slim = (ROWS, TS)
    picked = jnp.where((iota(slim, 0) & 7) == iota(slim, 1), spread, 0.0)
    return dot(picked.astype(BF16), jnp.ones((TS, LANES), BF16))


def to_dense(ids_ref, field_ref, live_ref, dense_ref):
    dense_ref[...] = jnp.zeros((ROWS, LANES), F32)
    for slot in range(SLOTS):

        @pl.when(ids_ref[slot] >= 0)
        def _():
            values = field_ref[slot].astype(F32).reshape(CELLS, LANES)
            values = values * live_ref[pl.ds(slot * CELLS, CELLS), :]
            dense_ref[pl.ds(position(ids_ref[slot]), CELLS, stride=SLOTS), :] = values


def write_edges(cells, east_ref, west_ref, fold_ref):
    east_ref[...] = cells[:, 5:8].reshape(192, LANES).astype(BF16)
    west_ref[...] = cells[:, 0:3].reshape(192, LANES).astype(BF16)
    fold_ref[...] = cells[5:8].reshape(192, LANES).astype(BF16)


def prepare_kernel(ids_ref, mask_ref, ocean_ref, dense_out, east_out, west_out, fold_out, live_ref, dense_ref):
    live_ref[...] = live_rows(mask_ref)
    to_dense(ids_ref, ocean_ref, live_ref, dense_ref)
    values = dense_ref[...]
    dense_out[...] = values.astype(BF16)
    write_edges(values.reshape(TS, TS, SLOTS, LANES), east_out, west_out, fold_out)


def cotangent_kernel(ids_ref, mask_ref, own_ref, other_ref, full_out, live_ref, dense_ref):
    own_at = pl.multiple_of(lax.axis_index("chan") * LANES, LANES)
    other_at = pl.multiple_of(LANES - own_at, LANES)
    live_ref[...] = live_rows(mask_ref)
    to_dense(ids_ref, own_ref, live_ref, dense_ref)
    full_out[:, pl.ds(own_at, LANES)] = dense_ref[...].astype(BF16)
    to_dense(ids_ref, other_ref, live_ref, dense_ref)
    full_out[:, pl.ds(other_at, LANES)] = dense_ref[...].astype(BF16)


def build_extended(ext_ref, dense_ref, west_ref, east_ref, fold_ref):
    odd = (iota((1, SLOTS, LANES), 1) & 1) == 1
    place = iota((1, SLOTS, LANES), 1)
    from_west = west_ref[...].astype(F32).reshape(TS, 3, SLOTS, LANES)
    from_east = east_ref[...].astype(F32).reshape(TS, 3, SLOTS, LANES)
    for y in range(TS):
        line = dense_ref[pl.ds(y * CELLS, CELLS), :].astype(F32).reshape(TS, SLOTS, LANES)
        ext_ref[3 + y, 3:11] = line
        ext_ref[3 + y, 0:3] = jnp.where(
            odd, pltpu.roll(line[5:8], 1, 1), pltpu.roll(from_west[y], 7, 1)
        )
        ext_ref[3 + y, 11:14] = jnp.where(
            odd, pltpu.roll(from_east[y], 1, 1), pltpu.roll(line[0:3], 7, 1)
        )
    for r in range(3):
        ext_ref[r] = jnp.where(place >= 2, pltpu.roll(ext_ref[8 + r], 2, 1), 0.0)
        ext_ref[11 + r] = jnp.where(place < 6, pltpu.roll(ext_ref[3 + r], 6, 1), 0.0)
    if fold_ref is not None:
        mirrored = fold_ref[...].astype(F32).reshape(3, TS, SLOTS, LANES)
        for r in range(3):
            cells = jnp.stack([mirrored[2 - r, 7 - j] for j in range(TS)])
            swapped = jnp.where(odd, pltpu.roll(cells, 1, 1), pltpu.roll(cells, 7, 1))
            ext_ref[11 + r, 3:11] = jnp.where(place >= 6, swapped, ext_ref[11 + r, 3:11])


def spread_taps(kernel_ref, taps_ref, flipped):
    for a in range(7):
        for b in range(7):
            at = (6 - a) * 7 + 6 - b if flipped else a * 7 + b
            taps_ref[at] = jnp.broadcast_to(kernel_ref[a, b : b + 1, :], (SLOTS, LANES))


def correlate_row(ext_ref, taps_ref, y):
    total = None
    for a in range(7):
        line = ext_ref[y + a]
        for b in range(7):
            term = line[b : b + TS] * taps_ref[7 * a + b][None]
            total = term if total is None else total + term
    return total


def convolve_kernel(dense_ref, west_ref, east_ref, fold_ref, kernel_ref, conv_out, send_out, ext_out, ext_ref, taps_ref):
    build_extended(ext_ref, dense_ref, west_ref, east_ref, fold_ref)
    spread_taps(kernel_ref, taps_ref, False)

    def row(y, carry):
        total = correlate_row(ext_ref, taps_ref, y).reshape(CELLS, LANES)
        rows = pl.ds(pl.multiple_of(y * CELLS, CELLS), CELLS)
        conv_out[rows, :] = total
        send_out[rows, :] = total.astype(BF16)
        return carry

    lax.fori_loop(0, TS, row, 0)

    def keep(y, carry):
        rows = pl.ds(pl.multiple_of(y * 112, 112), 112)
        ext_out[rows, :] = ext_ref[y].reshape(112, LANES).astype(BF16)
        return carry

    lax.fori_loop(0, 14, keep, 0)


CHUNK = 128


def pointwise_kernel(
    own_ref, other_ref, own_gain_ref, other_gain_ref, cotangent_ref, expand_ref, reduce_ref,
    normed_out, active_out, hidden_out, grad_out, message_out, standard_out, inverse_out, wide_ref,
):
    own_at = pl.multiple_of(lax.axis_index("chan") * LANES, LANES)
    other_at = pl.multiple_of(LANES - own_at, LANES)
    own_gain, other_gain = own_gain_ref[...], other_gain_ref[...]
    ones = jnp.ones((8, LANES), BF16)

    def step(i, carry):
        rows = pl.ds(pl.multiple_of(i * CHUNK, CHUNK), CHUNK)
        own, other = own_ref[rows, :], other_ref[rows, :].astype(F32)
        mean = jnp.sum(own + other, axis=-1, keepdims=True) * (1.0 / WIDTH)
        own, other = own - mean, other - mean
        variance = jnp.sum(own * own + other * other, axis=-1, keepdims=True) * (1.0 / WIDTH)
        inverse = lax.rsqrt(variance + norm_eps)
        own, other = own * inverse, other * inverse
        standard_out[rows, :] = own
        inverse_out[rows, :] = jnp.broadcast_to(inverse, (CHUNK, LANES))
        normed_out[rows, pl.ds(own_at, LANES)] = (own * own_gain).astype(BF16)
        normed_out[rows, pl.ds(other_at, LANES)] = (other * other_gain).astype(BF16)
        hidden = dot(normed_out[rows, :], expand_ref[...])
        half = 0.5 * (1.0 + lax.erf(hidden * root_half))
        active_out[rows, :] = (hidden * half).astype(BF16)
        slope = half + hidden * jnp.exp(-0.5 * hidden * hidden) * inv_root_tau
        grad_hidden = (dot(cotangent_ref[rows, :], reduce_ref[...], NT) * slope).astype(BF16)
        hidden_out[rows, :] = grad_hidden
        wide_ref[...] = dot(grad_hidden, expand_ref[...], NT)
        own_grad = wide_ref[:, pl.ds(own_at, LANES)]
        other_grad = wide_ref[:, pl.ds(other_at, LANES)]
        grad_out[rows, :] = own_grad
        message_out[rows, :] = other_grad.astype(BF16)
        own_grad, other_grad = own_grad * own_gain, other_grad * other_gain
        first = (own_grad + other_grad).astype(BF16)
        second = (own_grad * own + other_grad * other).astype(BF16)
        moments = jnp.concatenate([dot(ones, first, NT), dot(ones, second, NT)], axis=0)
        message_out[pl.ds(pl.multiple_of(ROWS + i * 16, 16), 16), :] = moments.astype(BF16)
        return carry

    lax.fori_loop(0, ROWS // CHUNK, step, 0)


def weights_kernel(
    normed_ref, active_ref, hidden_ref, cotangent_ref, reduce_ref,
    mixed_out, mixed_send, keep_out, send_out, wide_ref,
):
    own_at = pl.multiple_of(lax.axis_index("chan") * LANES, LANES)
    other_at = pl.multiple_of(LANES - own_at, LANES)
    first_core = (lax.axis_index("tiles") & 1) == 0
    wide_ref[...] = dot(active_ref[...], reduce_ref[...])
    mixed_out[...] = wide_ref[:, pl.ds(own_at, LANES)]
    mixed_send[...] = wide_ref[:, pl.ds(other_at, LANES)].astype(BF16)

    def write(out_ref, expand_kind):
        if expand_kind:
            for k in range(4):
                block = dot(normed_ref[...], hidden_ref[:, k * LANES : (k + 1) * LANES], TN)
                out_ref[k * WIDTH : (k + 1) * WIDTH, :] = block.astype(out_ref.dtype)
        else:
            for k in range(2):
                block = dot(active_ref[...], cotangent_ref[:, k * LANES : (k + 1) * LANES], TN)
                out_ref[k * HALF_HID : (k + 1) * HALF_HID, :] = block.astype(out_ref.dtype)

    @pl.when(first_core)
    def _():
        write(send_out, False)
        write(keep_out, True)

    @pl.when(jnp.logical_not(first_core))
    def _():
        write(send_out, True)
        write(keep_out, False)


def norm_back_kernel(
    grad_ref, own_message_ref, message_ref, standard_ref, inverse_ref, gain_ref, extended_ref,
    grad_conv_out, east_out, west_out, fold_out, sums_out, conv_ref,
):
    gain = gain_ref[...]
    kind = (iota((32, LANES), 0) & 8) == 0
    first_pick = jnp.where(kind, 1.0 / (8 * WIDTH), 0.0).astype(BF16)
    second_pick = jnp.where(kind, 0.0, 1.0 / (8 * WIDTH)).astype(BF16)

    def step(i, gain_total):
        rows = pl.ds(pl.multiple_of(i * CHUNK, CHUNK), CHUNK)
        tail = pl.ds(pl.multiple_of(ROWS + i * 16, 16), 16)
        moments = jnp.concatenate([own_message_ref[tail, :], message_ref[tail, :]], axis=0)
        first, second = dot(moments, first_pick, TN), dot(moments, second_pick, TN)
        grad = grad_ref[rows, :] + message_ref[rows, :].astype(F32)
        standard = standard_ref[rows, :]
        back = inverse_ref[rows, :] * (grad * gain - first - standard * second)
        back = back.astype(BF16)
        grad_conv_out[rows, :] = back
        conv_ref[rows, :] = back.astype(F32)
        return gain_total + jnp.sum((grad * standard).reshape(CHUNK // 8, 8, LANES), axis=0)

    gain_total = lax.fori_loop(0, ROWS // CHUNK, step, jnp.zeros((8, LANES), F32))
    write_edges(conv_ref[...].reshape(TS, TS, SLOTS, LANES), east_out, west_out, fold_out)
    sums_out[pl.ds(50, 14)] = jnp.zeros((14, 8, LANES), F32)
    sums_out[49] = gain_total

    def tap_row(a, carry):
        totals = [jnp.zeros((SLOTS, LANES), F32) for _ in range(7)]
        for y in range(TS):
            rows = pl.ds(pl.multiple_of((y + a) * 112, 112), 112)
            line = extended_ref[rows, :].astype(F32).reshape(14, SLOTS, LANES)
            grads = conv_ref[y * CELLS : (y + 1) * CELLS, :].reshape(TS, SLOTS, LANES)
            for b in range(7):
                totals[b] = totals[b] + jnp.sum(grads * line[b : b + TS], axis=0)
        for b in range(7):
            sums_out[a * 7 + b] = totals[b]
        return carry

    lax.fori_loop(0, 7, tap_row, 0)


def pack_kernel(keep_ref, arrived_ref, sums_ref, pieces_out):
    def step(i, carry):
        for k in range(8):
            at = i * 8 + k
            rows = pl.ds(pl.multiple_of(at * 16, 16), 16)
            big = keep_ref[rows, :] + arrived_ref[rows, :].astype(F32)
            pieces_out[pl.ds(at * PIECE, 8)] = big.astype(BF16).reshape(8, 2, LANES)
            small = sums_ref[at]
            small = small + pltpu.roll(small, 4, 0)
            small = small + pltpu.roll(small, 2, 0)
            pieces_out[at * PIECE + 8] = small[0:2].astype(BF16)
        return carry

    lax.fori_loop(0, 8, step, 0)


def total_kernel(scale, pieces_ref, pieces_out):
    total = jnp.zeros((PIECE, 2, LANES), F32)
    for at in range(64):
        total = total + pieces_ref[at * PIECE : (at + 1) * PIECE].astype(F32)
    total = total * scale
    small = jnp.sum(total[8], axis=0, keepdims=True)
    high = small.astype(BF16).astype(F32)
    small = jnp.where(iota((2, LANES), 0) == 0, high, small - high)
    big = total[0:8].astype(BF16)
    small = small.astype(BF16)
    for at in range(64):
        pieces_out[at * PIECE : at * PIECE + 8] = big
        pieces_out[at * PIECE + 8] = small


def unpack_kernel(own_ref, other_ref, expand_out, reduce_out, gain_out, kernel_out):
    first_core = (lax.axis_index("tiles") & 1) == 0

    def write(expand_from, reduce_from):
        for at in range(64):
            rows = slice(at * PIECE, at * PIECE + 8)
            piece = expand_from[rows].reshape(16, LANES).astype(F32)
            k, r = at // 16, at % 16
            expand_out[r * 16 : (r + 1) * 16, k * LANES : (k + 1) * LANES] = piece
            piece = reduce_from[rows].reshape(16, LANES).astype(F32)
            k, r = at // 32, at % 32
            reduce_out[r * 16 : (r + 1) * 16, k * LANES : (k + 1) * LANES] = piece

    @pl.when(first_core)
    def _():
        write(own_ref, other_ref)

    @pl.when(jnp.logical_not(first_core))
    def _():
        write(other_ref, own_ref)

    for at in range(50):
        total = own_ref[at * PIECE + 8].astype(F32) + other_ref[at * PIECE + 8].astype(F32)
        line = jnp.sum(total, axis=0, keepdims=True)
        if at < 49:
            kernel_out[at // 7, at % 7 : at % 7 + 1, :] = line
        else:
            gain_out[...] = line


def finish_kernel(
    ids_ref, mask_ref, ocean_ref, grad_ref, kernel_ref, mixed_ref, mixed_in_ref,
    grad_conv_ref, west_ref, east_ref, fold_ref,
    state_out, input_out, ext_ref, taps_ref, live_ref, back_ref, mixed_all,
):
    live_ref[...] = live_rows(mask_ref)
    mixed_all[...] = mixed_ref[...] + mixed_in_ref[...].astype(F32)
    build_extended(ext_ref, grad_conv_ref, west_ref, east_ref, None)
    spread_taps(kernel_ref, taps_ref, True)

    def row(y, carry):
        total = correlate_row(ext_ref, taps_ref, y).reshape(CELLS, LANES)
        back_ref[pl.ds(pl.multiple_of(y * CELLS, CELLS), CELLS), :] = total
        return carry

    lax.fori_loop(0, TS, row, 0)
    odd = (iota((1, SLOTS, LANES), 1) & 1) == 1
    top = iota((1, SLOTS, LANES), 1) >= 6
    mirrored = fold_ref[...].astype(F32).reshape(3, TS, SLOTS, LANES)
    swapped = jnp.where(
        odd[None],
        pltpu.roll(mirrored.reshape(24, SLOTS, LANES), 1, 1).reshape(3, TS, SLOTS, LANES),
        pltpu.roll(mirrored.reshape(24, SLOTS, LANES), 7, 1).reshape(3, TS, SLOTS, LANES),
    )
    swapped = jnp.where(top[None], swapped, 0.0)
    blank = jnp.zeros((3, SLOTS, LANES), F32)
    for r in range(3):
        band = jnp.zeros((TS, SLOTS, LANES), F32)
        for y in range(5 + r, 8):
            padded = jnp.concatenate([blank, swapped[y - 5], blank], axis=0)
            a = 11 + r - y
            for b in range(7):
                tap = taps_ref[(6 - a) * 7 + 6 - b]
                band = band + padded[6 - b : 14 - b] * tap[None]
        at = (7 - r) * CELLS
        turned = jnp.stack([band[7 - x] for x in range(TS)]).reshape(CELLS, LANES)
        back_ref[at : at + CELLS, :] = back_ref[at : at + CELLS, :] + turned
    for slot in range(SLOTS):
        rows = pl.ds(position(ids_ref[slot]), CELLS, stride=SLOTS)
        wet = jnp.where(ids_ref[slot] >= 0, 1.0, 0.0)
        live = live_ref[pl.ds(slot * CELLS, CELLS), :] * wet
        state = ocean_ref[slot].astype(F32).reshape(CELLS, LANES) * live
        state = (state + mixed_all[rows, :]) * live
        state_out[slot] = state.astype(BF16).reshape(TS, TS, LANES)
        cotangent = grad_ref[slot].astype(F32).reshape(CELLS, LANES) * live
        cotangent = (cotangent + back_ref[rows, :]) * live
        input_out[slot] = cotangent.astype(BF16).reshape(TS, TS, LANES)


def call(body, inputs, outputs, scratch=(), scalars=0, work=1.0):
    specs = [pl.BlockSpec(memory_space=pltpu.SMEM)] * scalars
    specs += [pl.BlockSpec(memory_space=pltpu.VMEM)] * (len(inputs) - scalars)
    return pl.pallas_call(
        body,
        out_shape=[jax.ShapeDtypeStruct(shape, kind) for shape, kind in outputs],
        in_specs=specs,
        out_specs=[pl.BlockSpec(memory_space=pltpu.VMEM)] * len(outputs),
        scratch_shapes=[pltpu.VMEM(shape, kind) for shape, kind in scratch],
        compiler_params=pltpu.CompilerParams(vmem_limit_bytes=40 * 1024 * 1024),
        cost_estimate=pl.CostEstimate(flops=int(work * WORK), bytes_accessed=0, transcendentals=0),
    )(*inputs)


def per_device(
    ocean_state, grad_state, sea_mask, tile_ids, neighbours, fold_partner,
    kernel, norm_gain, expand_weight, reduce_weight,
):
    devices = lax.axis_size("tiles")
    swap_chan = [(0, 1), (1, 0)]
    swap_core = [(i, i ^ 1) for i in range(devices)]
    ring = list(range(0, devices, 2)) + list(range(devices - 1, 0, -2))
    eastward = [(ring[i], ring[(i + 1) % devices]) for i in range(devices)]
    westward = [(there, here) for here, there in eastward]
    same_core = [list(range(core, devices, 2)) for core in range(2)]
    block = (ROWS, LANES)
    edge = (192, LANES)
    ext_scratch = ((14, 14, SLOTS, LANES), F32)
    taps_scratch = ((49, SLOTS, LANES), F32)

    gain = norm_gain.reshape(1, LANES)
    grad_other = lax.ppermute(grad_state, "chan", swap_chan)
    gain_other = lax.ppermute(gain, "chan", swap_chan)

    dense, east, west, fold = call(
        prepare_kernel, [tile_ids, sea_mask, ocean_state],
        [(block, BF16), (edge, BF16), (edge, BF16), (edge, BF16)],
        [(block, F32), (block, F32)], scalars=1, work=2,
    )
    from_west = lax.ppermute(east, "tiles", eastward)
    from_east = lax.ppermute(west, "tiles", westward)
    from_partner = lax.ppermute(fold, "tiles", swap_core)
    (cotangent,) = call(
        cotangent_kernel, [tile_ids, sea_mask, grad_state, grad_other],
        [((ROWS, WIDTH), BF16)], [(block, F32), (block, F32)], scalars=1, work=2,
    )
    conv, conv_send, extended = call(
        convolve_kernel, [dense, from_west, from_east, from_partner, kernel],
        [(block, F32), (block, BF16), ((14 * 14 * SLOTS, LANES), BF16)],
        [ext_scratch, taps_scratch], work=3,
    )
    conv_other = lax.ppermute(conv_send, "chan", swap_chan)
    normed, active, grad_hidden, grad_own, message, standard, inverse = call(
        pointwise_kernel,
        [conv, conv_other, gain, gain_other, cotangent, expand_weight, reduce_weight],
        [
            ((ROWS, WIDTH), BF16), ((ROWS, HALF_HID), BF16), ((ROWS, HALF_HID), BF16), (block, F32),
            ((ROWS + 64, LANES), BF16), (block, F32), (block, F32),
        ],
        [((CHUNK, WIDTH), F32)], work=6,
    )
    message_in = lax.ppermute(message, "chan", swap_chan)
    mixed, mixed_send, keep, send = call(
        weights_kernel, [normed, active, grad_hidden, cotangent, reduce_weight],
        [(block, F32), (block, BF16), ((1024, LANES), F32), ((1024, LANES), BF16)],
        [((ROWS, WIDTH), F32)], work=6,
    )
    arrived = lax.ppermute(send, "tiles", swap_core)
    mixed_in = lax.ppermute(mixed_send, "chan", swap_chan)
    grad_conv, east, west, fold, sums = call(
        norm_back_kernel, [grad_own, message, message_in, standard, inverse, gain, extended],
        [(block, BF16), (edge, BF16), (edge, BF16), (edge, BF16), ((64, 8, LANES), F32)],
        [(block, F32)], work=6,
    )
    grad_west = lax.ppermute(east, "tiles", eastward)
    grad_east = lax.ppermute(west, "tiles", westward)
    grad_partner = lax.ppermute(fold, "tiles", swap_core)
    pieces_shape = ((64 * PIECE, 2, LANES), BF16)
    (pieces,) = call(pack_kernel, [keep, arrived, sums], [pieces_shape])
    pieces = lax.all_to_all(pieces, "tiles", 0, 0, tiled=True, axis_index_groups=same_core)
    scale = 1.0 / math.sqrt(SLOTS * devices * CELLS)
    (pieces,) = call(functools.partial(total_kernel, scale), [pieces], [pieces_shape])
    pieces = lax.all_to_all(pieces, "tiles", 0, 0, tiled=True, axis_index_groups=same_core)
    pieces_other = lax.ppermute(pieces, "tiles", swap_core)
    new_state, grad_input = call(
        finish_kernel,
        [
            tile_ids, sea_mask, ocean_state, grad_state, kernel, mixed, mixed_in,
            grad_conv, grad_west, grad_east, grad_partner,
        ],
        [((SLOTS, TS, TS, LANES), BF16), ((SLOTS, TS, TS, LANES), BF16)],
        [ext_scratch, taps_scratch, (block, F32), (block, F32), (block, F32)],
        scalars=1, work=10,
    )
    expand_out, reduce_out, gain_out, kernel_out = call(
        unpack_kernel, [pieces, pieces_other],
        [((WIDTH, HALF_HID), F32), ((HALF_HID, WIDTH), F32), ((1, LANES), F32), ((7, 7, LANES), F32)],
    )
    return (new_state, grad_input, expand_out, reduce_out, gain_out.reshape(LANES), kernel_out)


def solution(mesh):
    return jax.shard_map(
        per_device,
        mesh=mesh,
        in_specs=(
            P("tiles", None, None, "chan"),
            P("tiles", None, None, "chan"),
            P("tiles", None, None),
            P("tiles"),
            P("tiles", None),
            P("tiles"),
            P(None, None, "chan"),
            P("chan"),
            P(None, "chan"),
            P("chan", None),
        ),
        out_specs=(
            P("tiles", None, None, "chan"),
            P("tiles", None, None, "chan"),
            P(None, "chan"),
            P("chan", None),
            P("chan"),
            P(None, None, "chan"),
        ),
        check_vma=False,
    )
```

```python
import functools
import math

import jax
import jax.numpy as jnp
from jax import lax
from jax.experimental import pallas as pl
from jax.experimental.pallas import tpu as pltpu
from jax.sharding import PartitionSpec as P

F32, BF16 = jnp.float32, jnp.bfloat16
TS = 8
CELLS = TS * TS
SLOTS = 8
ROWS = CELLS * SLOTS
LANES = 128
WIDTH = 256
HALF_HID = 512
GRID_COLUMNS = 256
PIECE = 9
WORK = 1_000_000_000
norm_eps = 1e-06
root_half = 0.7071067811865476
inv_root_tau = 0.3989422804014327

NN = (((1,), (0,)), ((), ()))
NT = (((1,), (1,)), ((), ()))
TN = (((0,), (0,)), ((), ()))


def dot(left, right, dims=NN):
    return lax.dot_general(left, right, dims, preferred_element_type=F32)


def iota(shape, axis):
    return lax.broadcasted_iota(jnp.int32, shape, axis)


def position(tile_id):
    safe = jnp.maximum(tile_id, 0)
    return lax.shift_right_logical(safe, 8) * 2 + (safe & 1)


def live_rows(mask_ref):
    marks = mask_ref[...].reshape(SLOTS * TS, TS).astype(F32).astype(BF16)
    wide = (ROWS, SLOTS * TS)
    owner = jnp.where(lax.shift_right_logical(iota(wide, 0), 3) == iota(wide, 1), 1.0, 0.0)
    spread = dot(owner.astype(BF16), marks)
    slim = (ROWS, TS)
    picked = jnp.where((iota(slim, 0) & 7) == iota(slim, 1), spread, 0.0)
    return dot(picked.astype(BF16), jnp.ones((TS, LANES), BF16))


def to_dense(ids_ref, field_ref, live_ref, dense_ref):
    dense_ref[...] = jnp.zeros((ROWS, LANES), F32)
    for slot in range(SLOTS):

        @pl.when(ids_ref[slot] >= 0)
        def _():
            values = field_ref[slot].astype(F32).reshape(CELLS, LANES)
            values = values * live_ref[pl.ds(slot * CELLS, CELLS), :]
            dense_ref[pl.ds(position(ids_ref[slot]), CELLS, stride=SLOTS), :] = values


def write_edges(cells, east_ref, west_ref, fold_ref):
    odd = (iota((1, SLOTS, LANES), 1) & 1) == 1
    for y in range(4):
        rows = slice(y * 24, (y + 1) * 24)
        packed = jnp.where(odd, cells[y, 5:8], pltpu.roll(cells[y + 4, 5:8], 7, 1))
        east_ref[rows, :] = packed.reshape(24, LANES).astype(BF16)
        packed = jnp.where(odd, pltpu.roll(cells[y + 4, 0:3], 1, 1), cells[y, 0:3])
        west_ref[rows, :] = packed.reshape(24, LANES).astype(BF16)
    fold_ref[...] = cells[5:8].reshape(192, LANES).astype(BF16)


def prepare_kernel(ids_ref, mask_ref, ocean_ref, dense_out, east_out, west_out, fold_out, live_ref, dense_ref):
    live_ref[...] = live_rows(mask_ref)
    to_dense(ids_ref, ocean_ref, live_ref, dense_ref)
    values = dense_ref[...]
    dense_out[...] = values.astype(BF16)
    write_edges(values.reshape(TS, TS, SLOTS, LANES), east_out, west_out, fold_out)


def cotangent_kernel(ids_ref, mask_ref, own_ref, other_ref, full_out, live_ref, dense_ref):
    own_at = pl.multiple_of(lax.axis_index("chan") * LANES, LANES)
    other_at = pl.multiple_of(LANES - own_at, LANES)
    live_ref[...] = live_rows(mask_ref)
    to_dense(ids_ref, own_ref, live_ref, dense_ref)
    full_out[:, pl.ds(own_at, LANES)] = dense_ref[...].astype(BF16)
    to_dense(ids_ref, other_ref, live_ref, dense_ref)
    full_out[:, pl.ds(other_at, LANES)] = dense_ref[...].astype(BF16)


def build_extended(ext_ref, dense_ref, west_ref, east_ref, fold_ref):
    odd = (iota((1, SLOTS, LANES), 1) & 1) == 1
    place = iota((1, SLOTS, LANES), 1)
    from_west = west_ref[...].astype(F32).reshape(4, 3, SLOTS, LANES)
    from_east = east_ref[...].astype(F32).reshape(4, 3, SLOTS, LANES)
    for y in range(TS):
        line = dense_ref[pl.ds(y * CELLS, CELLS), :].astype(F32).reshape(TS, SLOTS, LANES)
        ext_ref[3 + y, 3:11] = line
        west = pltpu.roll(from_west[y], 7, 1) if y < 4 else from_west[y - 4]
        east = pltpu.roll(from_east[y], 1, 1) if y < 4 else from_east[y - 4]
        ext_ref[3 + y, 0:3] = jnp.where(odd, pltpu.roll(line[5:8], 1, 1), west)
        ext_ref[3 + y, 11:14] = jnp.where(odd, east, pltpu.roll(line[0:3], 7, 1))
    for r in range(3):
        ext_ref[r] = jnp.where(place >= 2, pltpu.roll(ext_ref[8 + r], 2, 1), 0.0)
        ext_ref[11 + r] = jnp.where(place < 6, pltpu.roll(ext_ref[3 + r], 6, 1), 0.0)
    if fold_ref is not None:
        mirrored = fold_ref[...].astype(F32).reshape(3, TS, SLOTS, LANES)
        for r in range(3):
            cells = jnp.stack([mirrored[2 - r, 7 - j] for j in range(TS)])
            swapped = jnp.where(odd, pltpu.roll(cells, 1, 1), pltpu.roll(cells, 7, 1))
            ext_ref[11 + r, 3:11] = jnp.where(place >= 6, swapped, ext_ref[11 + r, 3:11])


def spread_taps(kernel_ref, taps_ref, flipped):
    for a in range(7):
        for b in range(7):
            at = (6 - a) * 7 + 6 - b if flipped else a * 7 + b
            taps_ref[at] = jnp.broadcast_to(kernel_ref[a, b : b + 1, :], (SLOTS, LANES))


def correlate_row(ext_ref, taps_ref, y):
    total = None
    for a in range(7):
        line = ext_ref[y + a]
        for b in range(7):
            term = line[b : b + TS] * taps_ref[7 * a + b][None]
            total = term if total is None else total + term
    return total


def convolve_kernel(dense_ref, west_ref, east_ref, fold_ref, kernel_ref, conv_out, send_out, ext_out, ext_ref, taps_ref):
    build_extended(ext_ref, dense_ref, west_ref, east_ref, fold_ref)
    spread_taps(kernel_ref, taps_ref, False)

    def row(y, carry):
        total = correlate_row(ext_ref, taps_ref, y).reshape(CELLS, LANES)
        rows = pl.ds(pl.multiple_of(y * CELLS, CELLS), CELLS)
        conv_out[rows, :] = total
        send_out[rows, :] = total.astype(BF16)
        return carry

    lax.fori_loop(0, TS, row, 0)

    def keep(y, carry):
        rows = pl.ds(pl.multiple_of(y * 112, 112), 112)
        ext_out[rows, :] = ext_ref[y].reshape(112, LANES).astype(BF16)
        return carry

    lax.fori_loop(0, 14, keep, 0)


CHUNK = 128


def pointwise_kernel(
    own_ref, other_ref, own_gain_ref, other_gain_ref, cotangent_ref, expand_ref, reduce_ref,
    normed_out, active_out, hidden_out, grad_out, message_out, standard_out, inverse_out, wide_ref,
):
    own_at = pl.multiple_of(lax.axis_index("chan") * LANES, LANES)
    other_at = pl.multiple_of(LANES - own_at, LANES)
    own_gain, other_gain = own_gain_ref[...], other_gain_ref[...]
    ones = jnp.ones((8, LANES), BF16)

    def step(i, carry):
        rows = pl.ds(pl.multiple_of(i * CHUNK, CHUNK), CHUNK)
        own, other = own_ref[rows, :], other_ref[rows, :].astype(F32)
        mean = jnp.sum(own + other, axis=-1, keepdims=True) * (1.0 / WIDTH)
        own, other = own - mean, other - mean
        variance = jnp.sum(own * own + other * other, axis=-1, keepdims=True) * (1.0 / WIDTH)
        inverse = lax.rsqrt(variance + norm_eps)
        own, other = own * inverse, other * inverse
        standard_out[rows, :] = own
        inverse_out[rows, :] = jnp.broadcast_to(inverse, (CHUNK, LANES))
        normed_out[rows, pl.ds(own_at, LANES)] = (own * own_gain).astype(BF16)
        normed_out[rows, pl.ds(other_at, LANES)] = (other * other_gain).astype(BF16)
        hidden = dot(normed_out[rows, :], expand_ref[...])
        half = 0.5 * (1.0 + lax.erf(hidden * root_half))
        active_out[rows, :] = (hidden * half).astype(BF16)
        slope = half + hidden * jnp.exp(-0.5 * hidden * hidden) * inv_root_tau
        grad_hidden = (dot(cotangent_ref[rows, :], reduce_ref[...], NT) * slope).astype(BF16)
        hidden_out[rows, :] = grad_hidden
        wide_ref[...] = dot(grad_hidden, expand_ref[...], NT)
        own_grad = wide_ref[:, pl.ds(own_at, LANES)]
        other_grad = wide_ref[:, pl.ds(other_at, LANES)]
        grad_out[rows, :] = own_grad
        message_out[rows, :] = other_grad.astype(BF16)
        own_grad, other_grad = own_grad * own_gain, other_grad * other_gain
        first = (own_grad + other_grad).astype(BF16)
        second = (own_grad * own + other_grad * other).astype(BF16)
        moments = jnp.concatenate([dot(ones, first, NT), dot(ones, second, NT)], axis=0)
        message_out[pl.ds(pl.multiple_of(ROWS + i * 16, 16), 16), :] = moments.astype(BF16)
        return carry

    lax.fori_loop(0, ROWS // CHUNK, step, 0)


def weights_kernel(
    normed_ref, active_ref, hidden_ref, cotangent_ref, reduce_ref,
    mixed_out, mixed_send, keep_out, send_out, wide_ref,
):
    own_at = pl.multiple_of(lax.axis_index("chan") * LANES, LANES)
    other_at = pl.multiple_of(LANES - own_at, LANES)
    first_core = (lax.axis_index("tiles") & 1) == 0
    wide_ref[...] = dot(active_ref[...], reduce_ref[...])
    mixed_out[...] = wide_ref[:, pl.ds(own_at, LANES)]
    mixed_send[...] = wide_ref[:, pl.ds(other_at, LANES)].astype(BF16)

    def write(out_ref, expand_kind):
        if expand_kind:
            for k in range(4):
                block = dot(normed_ref[...], hidden_ref[:, k * LANES : (k + 1) * LANES], TN)
                out_ref[k * WIDTH : (k + 1) * WIDTH, :] = block.astype(out_ref.dtype)
        else:
            for k in range(2):
                block = dot(active_ref[...], cotangent_ref[:, k * LANES : (k + 1) * LANES], TN)
                out_ref[k * HALF_HID : (k + 1) * HALF_HID, :] = block.astype(out_ref.dtype)

    @pl.when(first_core)
    def _():
        write(send_out, False)
        write(keep_out, True)

    @pl.when(jnp.logical_not(first_core))
    def _():
        write(send_out, True)
        write(keep_out, False)


def norm_back_kernel(
    grad_ref, own_message_ref, message_ref, standard_ref, inverse_ref, gain_ref, extended_ref,
    grad_conv_out, east_out, west_out, fold_out, sums_out, conv_ref,
):
    gain = gain_ref[...]
    kind = (iota((32, LANES), 0) & 8) == 0
    first_pick = jnp.where(kind, 1.0 / (8 * WIDTH), 0.0).astype(BF16)
    second_pick = jnp.where(kind, 0.0, 1.0 / (8 * WIDTH)).astype(BF16)

    def step(i, gain_total):
        rows = pl.ds(pl.multiple_of(i * CHUNK, CHUNK), CHUNK)
        tail = pl.ds(pl.multiple_of(ROWS + i * 16, 16), 16)
        moments = jnp.concatenate([own_message_ref[tail, :], message_ref[tail, :]], axis=0)
        first, second = dot(moments, first_pick, TN), dot(moments, second_pick, TN)
        grad = grad_ref[rows, :] + message_ref[rows, :].astype(F32)
        standard = standard_ref[rows, :]
        back = inverse_ref[rows, :] * (grad * gain - first - standard * second)
        back = back.astype(BF16)
        grad_conv_out[rows, :] = back
        conv_ref[rows, :] = back.astype(F32)
        return gain_total + jnp.sum((grad * standard).reshape(CHUNK // 8, 8, LANES), axis=0)

    gain_total = lax.fori_loop(0, ROWS // CHUNK, step, jnp.zeros((8, LANES), F32))
    write_edges(conv_ref[...].reshape(TS, TS, SLOTS, LANES), east_out, west_out, fold_out)
    sums_out[pl.ds(50, 14)] = jnp.zeros((14, 8, LANES), F32)
    sums_out[49] = gain_total

    def tap_row(a, carry):
        totals = [jnp.zeros((SLOTS, LANES), F32) for _ in range(7)]
        for y in range(TS):
            rows = pl.ds(pl.multiple_of((y + a) * 112, 112), 112)
            line = extended_ref[rows, :].astype(F32).reshape(14, SLOTS, LANES)
            grads = conv_ref[y * CELLS : (y + 1) * CELLS, :].reshape(TS, SLOTS, LANES)
            for b in range(7):
                totals[b] = totals[b] + jnp.sum(grads * line[b : b + TS], axis=0)
        for b in range(7):
            sums_out[a * 7 + b] = totals[b]
        return carry

    lax.fori_loop(0, 7, tap_row, 0)


def pack_kernel(keep_ref, arrived_ref, sums_ref, pieces_out):
    def step(i, carry):
        for k in range(8):
            at = i * 8 + k
            rows = pl.ds(pl.multiple_of(at * 16, 16), 16)
            big = keep_ref[rows, :] + arrived_ref[rows, :].astype(F32)
            pieces_out[pl.ds(at * PIECE, 8)] = big.astype(BF16).reshape(8, 2, LANES)
            small = sums_ref[at]
            small = small + pltpu.roll(small, 4, 0)
            small = small + pltpu.roll(small, 2, 0)
            pieces_out[at * PIECE + 8] = small[0:2].astype(BF16)
        return carry

    lax.fori_loop(0, 8, step, 0)


def total_kernel(scale, pieces_ref, pieces_out):
    total = jnp.zeros((PIECE, 2, LANES), F32)
    for at in range(64):
        total = total + pieces_ref[at * PIECE : (at + 1) * PIECE].astype(F32)
    total = total * scale
    small = jnp.sum(total[8], axis=0, keepdims=True)
    high = small.astype(BF16).astype(F32)
    small = jnp.where(iota((2, LANES), 0) == 0, high, small - high)
    big = total[0:8].astype(BF16)
    small = small.astype(BF16)
    for at in range(64):
        pieces_out[at * PIECE : at * PIECE + 8] = big
        pieces_out[at * PIECE + 8] = small


def unpack_kernel(own_ref, other_ref, expand_out, reduce_out, gain_out, kernel_out):
    first_core = (lax.axis_index("tiles") & 1) == 0

    def write(expand_from, reduce_from):
        for at in range(64):
            rows = slice(at * PIECE, at * PIECE + 8)
            piece = expand_from[rows].reshape(16, LANES).astype(F32)
            k, r = at // 16, at % 16
            expand_out[r * 16 : (r + 1) * 16, k * LANES : (k + 1) * LANES] = piece
            piece = reduce_from[rows].reshape(16, LANES).astype(F32)
            k, r = at // 32, at % 32
            reduce_out[r * 16 : (r + 1) * 16, k * LANES : (k + 1) * LANES] = piece

    @pl.when(first_core)
    def _():
        write(own_ref, other_ref)

    @pl.when(jnp.logical_not(first_core))
    def _():
        write(other_ref, own_ref)

    for at in range(50):
        total = own_ref[at * PIECE + 8].astype(F32) + other_ref[at * PIECE + 8].astype(F32)
        line = jnp.sum(total, axis=0, keepdims=True)
        if at < 49:
            kernel_out[at // 7, at % 7 : at % 7 + 1, :] = line
        else:
            gain_out[...] = line


def finish_kernel(
    ids_ref, mask_ref, ocean_ref, grad_ref, kernel_ref, mixed_ref, mixed_in_ref,
    grad_conv_ref, west_ref, east_ref, fold_ref,
    state_out, input_out, ext_ref, taps_ref, live_ref, back_ref, mixed_all,
):
    live_ref[...] = live_rows(mask_ref)
    mixed_all[...] = mixed_ref[...] + mixed_in_ref[...].astype(F32)
    build_extended(ext_ref, grad_conv_ref, west_ref, east_ref, None)
    spread_taps(kernel_ref, taps_ref, True)

    def row(y, carry):
        total = correlate_row(ext_ref, taps_ref, y).reshape(CELLS, LANES)
        back_ref[pl.ds(pl.multiple_of(y * CELLS, CELLS), CELLS), :] = total
        return carry

    lax.fori_loop(0, TS, row, 0)
    odd = (iota((1, SLOTS, LANES), 1) & 1) == 1
    top = iota((1, SLOTS, LANES), 1) >= 6
    mirrored = fold_ref[...].astype(F32).reshape(3, TS, SLOTS, LANES)
    swapped = jnp.where(
        odd[None],
        pltpu.roll(mirrored.reshape(24, SLOTS, LANES), 1, 1).reshape(3, TS, SLOTS, LANES),
        pltpu.roll(mirrored.reshape(24, SLOTS, LANES), 7, 1).reshape(3, TS, SLOTS, LANES),
    )
    swapped = jnp.where(top[None], swapped, 0.0)
    blank = jnp.zeros((3, SLOTS, LANES), F32)
    for r in range(3):
        band = jnp.zeros((TS, SLOTS, LANES), F32)
        for y in range(5 + r, 8):
            padded = jnp.concatenate([blank, swapped[y - 5], blank], axis=0)
            a = 11 + r - y
            for b in range(7):
                tap = taps_ref[(6 - a) * 7 + 6 - b]
                band = band + padded[6 - b : 14 - b] * tap[None]
        at = (7 - r) * CELLS
        turned = jnp.stack([band[7 - x] for x in range(TS)]).reshape(CELLS, LANES)
        back_ref[at : at + CELLS, :] = back_ref[at : at + CELLS, :] + turned
    for slot in range(SLOTS):
        rows = pl.ds(position(ids_ref[slot]), CELLS, stride=SLOTS)
        wet = jnp.where(ids_ref[slot] >= 0, 1.0, 0.0)
        live = live_ref[pl.ds(slot * CELLS, CELLS), :] * wet
        state = ocean_ref[slot].astype(F32).reshape(CELLS, LANES) * live
        state = (state + mixed_all[rows, :]) * live
        state_out[slot] = state.astype(BF16).reshape(TS, TS, LANES)
        cotangent = grad_ref[slot].astype(F32).reshape(CELLS, LANES) * live
        cotangent = (cotangent + back_ref[rows, :]) * live
        input_out[slot] = cotangent.astype(BF16).reshape(TS, TS, LANES)


def call(body, inputs, outputs, scratch=(), scalars=0, work=1.0):
    specs = [pl.BlockSpec(memory_space=pltpu.SMEM)] * scalars
    specs += [pl.BlockSpec(memory_space=pltpu.VMEM)] * (len(inputs) - scalars)
    return pl.pallas_call(
        body,
        out_shape=[jax.ShapeDtypeStruct(shape, kind) for shape, kind in outputs],
        in_specs=specs,
        out_specs=[pl.BlockSpec(memory_space=pltpu.VMEM)] * len(outputs),
        scratch_shapes=[pltpu.VMEM(shape, kind) for shape, kind in scratch],
        compiler_params=pltpu.CompilerParams(vmem_limit_bytes=40 * 1024 * 1024),
        cost_estimate=pl.CostEstimate(flops=int(work * WORK), bytes_accessed=0, transcendentals=0),
    )(*inputs)


def per_device(
    ocean_state, grad_state, sea_mask, tile_ids, neighbours, fold_partner,
    kernel, norm_gain, expand_weight, reduce_weight,
):
    devices = lax.axis_size("tiles")
    swap_chan = [(0, 1), (1, 0)]
    swap_core = [(i, i ^ 1) for i in range(devices)]
    ring = list(range(0, devices, 2)) + list(range(devices - 1, 0, -2))
    eastward = [(ring[i], ring[(i + 1) % devices]) for i in range(devices)]
    westward = [(there, here) for here, there in eastward]
    same_core = [list(range(core, devices, 2)) for core in range(2)]
    block = (ROWS, LANES)
    edge, top = (96, LANES), (192, LANES)
    ext_scratch = ((14, 14, SLOTS, LANES), F32)
    taps_scratch = ((49, SLOTS, LANES), F32)

    gain = norm_gain.reshape(1, LANES)
    grad_other = lax.ppermute(grad_state, "chan", swap_chan)
    gain_other = lax.ppermute(gain, "chan", swap_chan)

    dense, east, west, fold = call(
        prepare_kernel, [tile_ids, sea_mask, ocean_state],
        [(block, BF16), (edge, BF16), (edge, BF16), (top, BF16)],
        [(block, F32), (block, F32)], scalars=1, work=2,
    )
    from_west = lax.ppermute(east, "tiles", eastward)
    from_east = lax.ppermute(west, "tiles", westward)
    from_partner = lax.ppermute(fold, "tiles", swap_core)
    (cotangent,) = call(
        cotangent_kernel, [tile_ids, sea_mask, grad_state, grad_other],
        [((ROWS, WIDTH), BF16)], [(block, F32), (block, F32)], scalars=1, work=2,
    )
    conv, conv_send, extended = call(
        convolve_kernel, [dense, from_west, from_east, from_partner, kernel],
        [(block, F32), (block, BF16), ((14 * 14 * SLOTS, LANES), BF16)],
        [ext_scratch, taps_scratch], work=3,
    )
    conv_other = lax.ppermute(conv_send, "chan", swap_chan)
    normed, active, grad_hidden, grad_own, message, standard, inverse = call(
        pointwise_kernel,
        [conv, conv_other, gain, gain_other, cotangent, expand_weight, reduce_weight],
        [
            ((ROWS, WIDTH), BF16), ((ROWS, HALF_HID), BF16), ((ROWS, HALF_HID), BF16), (block, F32),
            ((ROWS + 64, LANES), BF16), (block, F32), (block, F32),
        ],
        [((CHUNK, WIDTH), F32)], work=6,
    )
    message_in = lax.ppermute(message, "chan", swap_chan)
    mixed, mixed_send, keep, send = call(
        weights_kernel, [normed, active, grad_hidden, cotangent, reduce_weight],
        [(block, F32), (block, BF16), ((1024, LANES), F32), ((1024, LANES), BF16)],
        [((ROWS, WIDTH), F32)], work=6,
    )
    arrived = lax.ppermute(send, "tiles", swap_core)
    mixed_in = lax.ppermute(mixed_send, "chan", swap_chan)
    grad_conv, east, west, fold, sums = call(
        norm_back_kernel, [grad_own, message, message_in, standard, inverse, gain, extended],
        [(block, BF16), (edge, BF16), (edge, BF16), (top, BF16), ((64, 8, LANES), F32)],
        [(block, F32)], work=6,
    )
    grad_west = lax.ppermute(east, "tiles", eastward)
    grad_east = lax.ppermute(west, "tiles", westward)
    grad_partner = lax.ppermute(fold, "tiles", swap_core)
    pieces_shape = ((64 * PIECE, 2, LANES), BF16)
    (pieces,) = call(pack_kernel, [keep, arrived, sums], [pieces_shape])
    pieces = lax.all_to_all(pieces, "tiles", 0, 0, tiled=True, axis_index_groups=same_core)
    pieces, grad_west, grad_east, grad_partner, mixed_in = lax.optimization_barrier(
        (pieces, grad_west, grad_east, grad_partner, mixed_in)
    )
    scale = 1.0 / math.sqrt(SLOTS * devices * CELLS)
    (pieces,) = call(functools.partial(total_kernel, scale), [pieces], [pieces_shape])
    pieces = lax.all_to_all(pieces, "tiles", 0, 0, tiled=True, axis_index_groups=same_core)
    new_state, grad_input = call(
        finish_kernel,
        [
            tile_ids, sea_mask, ocean_state, grad_state, kernel, mixed, mixed_in,
            grad_conv, grad_west, grad_east, grad_partner,
        ],
        [((SLOTS, TS, TS, LANES), BF16), ((SLOTS, TS, TS, LANES), BF16)],
        [ext_scratch, taps_scratch, (block, F32), (block, F32), (block, F32)],
        scalars=1, work=10,
    )
    pieces, new_state, grad_input = lax.optimization_barrier((pieces, new_state, grad_input))
    pieces_other = lax.ppermute(pieces, "tiles", swap_core)
    expand_out, reduce_out, gain_out, kernel_out = call(
        unpack_kernel, [pieces, pieces_other],
        [((WIDTH, HALF_HID), F32), ((HALF_HID, WIDTH), F32), ((1, LANES), F32), ((7, 7, LANES), F32)],
    )
    return (new_state, grad_input, expand_out, reduce_out, gain_out.reshape(LANES), kernel_out)


def solution(mesh):
    return jax.shard_map(
        per_device,
        mesh=mesh,
        in_specs=(
            P("tiles", None, None, "chan"),
            P("tiles", None, None, "chan"),
            P("tiles", None, None),
            P("tiles"),
            P("tiles", None),
            P("tiles"),
            P(None, None, "chan"),
            P("chan"),
            P(None, "chan"),
            P("chan", None),
        ),
        out_specs=(
            P("tiles", None, None, "chan"),
            P("tiles", None, None, "chan"),
            P(None, "chan"),
            P("chan", None),
            P("chan"),
            P(None, None, "chan"),
        ),
        check_vma=False,
    )
```

```python
import functools
import math

import jax
import jax.numpy as jnp
from jax import lax
from jax.experimental import pallas as pl
from jax.experimental.pallas import tpu as pltpu
from jax.sharding import PartitionSpec as P

F32, BF16 = jnp.float32, jnp.bfloat16
TS = 8
CELLS = TS * TS
SLOTS = 8
ROWS = CELLS * SLOTS
LANES = 128
WIDTH = 256
HALF_HID = 512
GRID_COLUMNS = 256
PIECE = 9
WORK = 1_000_000_000
norm_eps = 1e-06
root_half = 0.7071067811865476
inv_root_tau = 0.3989422804014327

NN = (((1,), (0,)), ((), ()))
NT = (((1,), (1,)), ((), ()))
TN = (((0,), (0,)), ((), ()))


def dot(left, right, dims=NN):
    return lax.dot_general(left, right, dims, preferred_element_type=F32)


def iota(shape, axis):
    return lax.broadcasted_iota(jnp.int32, shape, axis)


def position(tile_id):
    safe = jnp.maximum(tile_id, 0)
    return lax.shift_right_logical(safe, 8) * 2 + (safe & 1)


def live_rows(mask_ref):
    marks = mask_ref[...].reshape(SLOTS * TS, TS).astype(F32).astype(BF16)
    wide = (ROWS, SLOTS * TS)
    owner = jnp.where(lax.shift_right_logical(iota(wide, 0), 3) == iota(wide, 1), 1.0, 0.0)
    spread = dot(owner.astype(BF16), marks)
    slim = (ROWS, TS)
    picked = jnp.where((iota(slim, 0) & 7) == iota(slim, 1), spread, 0.0)
    return dot(picked.astype(BF16), jnp.ones((TS, LANES), BF16))


def to_dense(ids_ref, field_ref, live_ref, dense_ref):
    dense_ref[...] = jnp.zeros((ROWS, LANES), F32)
    for slot in range(SLOTS):

        @pl.when(ids_ref[slot] >= 0)
        def _():
            values = field_ref[slot].astype(F32).reshape(CELLS, LANES)
            values = values * live_ref[pl.ds(slot * CELLS, CELLS), :]
            dense_ref[pl.ds(position(ids_ref[slot]), CELLS, stride=SLOTS), :] = values


def write_edges(cells, east_ref, west_ref, fold_ref):
    odd = (iota((1, SLOTS, LANES), 1) & 1) == 1
    for y in range(4):
        rows = slice(y * 24, (y + 1) * 24)
        packed = jnp.where(odd, cells[y, 5:8], pltpu.roll(cells[y + 4, 5:8], 7, 1))
        east_ref[rows, :] = packed.reshape(24, LANES).astype(BF16)
        packed = jnp.where(odd, pltpu.roll(cells[y + 4, 0:3], 1, 1), cells[y, 0:3])
        west_ref[rows, :] = packed.reshape(24, LANES).astype(BF16)
    fold_ref[...] = cells[5:8].reshape(192, LANES).astype(BF16)


def prepare_kernel(ids_ref, mask_ref, ocean_ref, dense_out, east_out, west_out, fold_out, live_ref, dense_ref):
    live_ref[...] = live_rows(mask_ref)
    to_dense(ids_ref, ocean_ref, live_ref, dense_ref)
    values = dense_ref[...]
    dense_out[...] = values.astype(BF16)
    write_edges(values.reshape(TS, TS, SLOTS, LANES), east_out, west_out, fold_out)


def cotangent_kernel(ids_ref, mask_ref, own_ref, other_ref, full_out, live_ref, dense_ref):
    own_at = pl.multiple_of(lax.axis_index("chan") * LANES, LANES)
    other_at = pl.multiple_of(LANES - own_at, LANES)
    live_ref[...] = live_rows(mask_ref)
    to_dense(ids_ref, own_ref, live_ref, dense_ref)
    full_out[:, pl.ds(own_at, LANES)] = dense_ref[...].astype(BF16)
    to_dense(ids_ref, other_ref, live_ref, dense_ref)
    full_out[:, pl.ds(other_at, LANES)] = dense_ref[...].astype(BF16)


def build_extended(ext_ref, dense_ref, west_ref, east_ref, fold_ref):
    odd = (iota((1, SLOTS, LANES), 1) & 1) == 1
    place = iota((1, SLOTS, LANES), 1)
    from_west = west_ref[...].astype(F32).reshape(4, 3, SLOTS, LANES)
    from_east = east_ref[...].astype(F32).reshape(4, 3, SLOTS, LANES)
    for y in range(TS):
        line = dense_ref[pl.ds(y * CELLS, CELLS), :].astype(F32).reshape(TS, SLOTS, LANES)
        ext_ref[3 + y, 3:11] = line
        west = pltpu.roll(from_west[y], 7, 1) if y < 4 else from_west[y - 4]
        east = pltpu.roll(from_east[y], 1, 1) if y < 4 else from_east[y - 4]
        ext_ref[3 + y, 0:3] = jnp.where(odd, pltpu.roll(line[5:8], 1, 1), west)
        ext_ref[3 + y, 11:14] = jnp.where(odd, east, pltpu.roll(line[0:3], 7, 1))
    for r in range(3):
        ext_ref[r] = jnp.where(place >= 2, pltpu.roll(ext_ref[8 + r], 2, 1), 0.0)
        ext_ref[11 + r] = jnp.where(place < 6, pltpu.roll(ext_ref[3 + r], 6, 1), 0.0)
    if fold_ref is not None:
        mirrored = fold_ref[...].astype(F32).reshape(3, TS, SLOTS, LANES)
        for r in range(3):
            cells = jnp.stack([mirrored[2 - r, 7 - j] for j in range(TS)])
            swapped = jnp.where(odd, pltpu.roll(cells, 1, 1), pltpu.roll(cells, 7, 1))
            ext_ref[11 + r, 3:11] = jnp.where(place >= 6, swapped, ext_ref[11 + r, 3:11])


def spread_taps(kernel_ref, taps_ref, flipped):
    for a in range(7):
        for b in range(7):
            at = (6 - a) * 7 + 6 - b if flipped else a * 7 + b
            taps_ref[at] = jnp.broadcast_to(kernel_ref[a, b : b + 1, :], (SLOTS, LANES))


def correlate_row(ext_ref, taps_ref, y):
    total = None
    for a in range(7):
        line = ext_ref[y + a]
        for b in range(7):
            term = line[b : b + TS] * taps_ref[7 * a + b][None]
            total = term if total is None else total + term
    return total


def convolve_kernel(dense_ref, west_ref, east_ref, fold_ref, kernel_ref, conv_out, send_out, ext_out, ext_ref, taps_ref):
    build_extended(ext_ref, dense_ref, west_ref, east_ref, fold_ref)
    spread_taps(kernel_ref, taps_ref, False)

    def row(y, carry):
        total = correlate_row(ext_ref, taps_ref, y).reshape(CELLS, LANES)
        rows = pl.ds(pl.multiple_of(y * CELLS, CELLS), CELLS)
        conv_out[rows, :] = total
        send_out[rows, :] = total.astype(BF16)
        return carry

    lax.fori_loop(0, TS, row, 0)

    def keep(y, carry):
        rows = pl.ds(pl.multiple_of(y * 112, 112), 112)
        ext_out[rows, :] = ext_ref[y].reshape(112, LANES).astype(BF16)
        return carry

    lax.fori_loop(0, 14, keep, 0)


CHUNK = 128


def pointwise_kernel(
    own_ref, other_ref, own_gain_ref, other_gain_ref, cotangent_ref, expand_ref, reduce_ref,
    normed_out, active_out, hidden_out, grad_out, message_out, standard_out, inverse_out, wide_ref,
):
    own_at = pl.multiple_of(lax.axis_index("chan") * LANES, LANES)
    other_at = pl.multiple_of(LANES - own_at, LANES)
    own_gain, other_gain = own_gain_ref[...], other_gain_ref[...]
    ones = jnp.ones((8, LANES), BF16)

    def step(i, carry):
        rows = pl.ds(pl.multiple_of(i * CHUNK, CHUNK), CHUNK)
        own, other = own_ref[rows, :], other_ref[rows, :].astype(F32)
        mean = jnp.sum(own + other, axis=-1, keepdims=True) * (1.0 / WIDTH)
        own, other = own - mean, other - mean
        variance = jnp.sum(own * own + other * other, axis=-1, keepdims=True) * (1.0 / WIDTH)
        inverse = lax.rsqrt(variance + norm_eps)
        own, other = own * inverse, other * inverse
        standard_out[rows, :] = own
        inverse_out[rows, :] = jnp.broadcast_to(inverse, (CHUNK, LANES))
        normed_out[rows, pl.ds(own_at, LANES)] = (own * own_gain).astype(BF16)
        normed_out[rows, pl.ds(other_at, LANES)] = (other * other_gain).astype(BF16)
        hidden = dot(normed_out[rows, :], expand_ref[...])
        half = 0.5 * (1.0 + lax.erf(hidden * root_half))
        active_out[rows, :] = (hidden * half).astype(BF16)
        slope = half + hidden * jnp.exp(-0.5 * hidden * hidden) * inv_root_tau
        grad_hidden = (dot(cotangent_ref[rows, :], reduce_ref[...], NT) * slope).astype(BF16)
        hidden_out[rows, :] = grad_hidden
        wide_ref[...] = dot(grad_hidden, expand_ref[...], NT)
        own_grad = wide_ref[:, pl.ds(own_at, LANES)]
        other_grad = wide_ref[:, pl.ds(other_at, LANES)]
        grad_out[rows, :] = own_grad
        message_out[rows, :] = other_grad.astype(BF16)
        own_grad, other_grad = own_grad * own_gain, other_grad * other_gain
        first = (own_grad + other_grad).astype(BF16)
        second = (own_grad * own + other_grad * other).astype(BF16)
        moments = jnp.concatenate([dot(ones, first, NT), dot(ones, second, NT)], axis=0)
        message_out[pl.ds(pl.multiple_of(ROWS + i * 16, 16), 16), :] = moments.astype(BF16)
        return carry

    lax.fori_loop(0, ROWS // CHUNK, step, 0)


def weights_kernel(
    normed_ref, active_ref, hidden_ref, cotangent_ref, reduce_ref,
    mixed_out, mixed_send, keep_out, send_out, wide_ref,
):
    own_at = pl.multiple_of(lax.axis_index("chan") * LANES, LANES)
    other_at = pl.multiple_of(LANES - own_at, LANES)
    first_core = (lax.axis_index("tiles") & 1) == 0
    wide_ref[...] = dot(active_ref[...], reduce_ref[...])
    mixed_out[...] = wide_ref[:, pl.ds(own_at, LANES)]
    mixed_send[...] = wide_ref[:, pl.ds(other_at, LANES)].astype(BF16)

    def write(out_ref, expand_kind):
        if expand_kind:
            for k in range(4):
                block = dot(normed_ref[...], hidden_ref[:, k * LANES : (k + 1) * LANES], TN)
                out_ref[k * WIDTH : (k + 1) * WIDTH, :] = block.astype(out_ref.dtype)
        else:
            for k in range(2):
                block = dot(active_ref[...], cotangent_ref[:, k * LANES : (k + 1) * LANES], TN)
                out_ref[k * HALF_HID : (k + 1) * HALF_HID, :] = block.astype(out_ref.dtype)

    @pl.when(first_core)
    def _():
        write(send_out, False)
        write(keep_out, True)

    @pl.when(jnp.logical_not(first_core))
    def _():
        write(send_out, True)
        write(keep_out, False)


def norm_back_kernel(
    grad_ref, own_message_ref, message_ref, standard_ref, inverse_ref, gain_ref, extended_ref,
    grad_conv_out, east_out, west_out, fold_out, sums_out, conv_ref,
):
    gain = gain_ref[...]
    kind = (iota((32, LANES), 0) & 8) == 0
    first_pick = jnp.where(kind, 1.0 / (8 * WIDTH), 0.0).astype(BF16)
    second_pick = jnp.where(kind, 0.0, 1.0 / (8 * WIDTH)).astype(BF16)

    def step(i, gain_total):
        rows = pl.ds(pl.multiple_of(i * CHUNK, CHUNK), CHUNK)
        tail = pl.ds(pl.multiple_of(ROWS + i * 16, 16), 16)
        moments = jnp.concatenate([own_message_ref[tail, :], message_ref[tail, :]], axis=0)
        first, second = dot(moments, first_pick, TN), dot(moments, second_pick, TN)
        grad = grad_ref[rows, :] + message_ref[rows, :].astype(F32)
        standard = standard_ref[rows, :]
        back = inverse_ref[rows, :] * (grad * gain - first - standard * second)
        back = back.astype(BF16)
        grad_conv_out[rows, :] = back
        conv_ref[rows, :] = back.astype(F32)
        return gain_total + jnp.sum((grad * standard).reshape(CHUNK // 8, 8, LANES), axis=0)

    gain_total = lax.fori_loop(0, ROWS // CHUNK, step, jnp.zeros((8, LANES), F32))
    write_edges(conv_ref[...].reshape(TS, TS, SLOTS, LANES), east_out, west_out, fold_out)
    sums_out[pl.ds(50, 14)] = jnp.zeros((14, 8, LANES), F32)
    sums_out[49] = gain_total

    def tap_row(a, carry):
        totals = [jnp.zeros((SLOTS, LANES), F32) for _ in range(7)]
        for y in range(TS):
            rows = pl.ds(pl.multiple_of((y + a) * 112, 112), 112)
            line = extended_ref[rows, :].astype(F32).reshape(14, SLOTS, LANES)
            grads = conv_ref[y * CELLS : (y + 1) * CELLS, :].reshape(TS, SLOTS, LANES)
            for b in range(7):
                totals[b] = totals[b] + jnp.sum(grads * line[b : b + TS], axis=0)
        for b in range(7):
            sums_out[a * 7 + b] = totals[b]
        return carry

    lax.fori_loop(0, 7, tap_row, 0)


def pack_kernel(keep_ref, arrived_ref, sums_ref, pieces_out):
    def step(i, carry):
        for k in range(8):
            at = i * 8 + k
            rows = pl.ds(pl.multiple_of(at * 16, 16), 16)
            big = keep_ref[rows, :] + arrived_ref[rows, :].astype(F32)
            pieces_out[pl.ds(at * PIECE, 8)] = big.astype(BF16).reshape(8, 2, LANES)
            small = sums_ref[at]
            small = small + pltpu.roll(small, 4, 0)
            small = small + pltpu.roll(small, 2, 0)
            pieces_out[at * PIECE + 8] = small[0:2].astype(BF16)
        return carry

    lax.fori_loop(0, 8, step, 0)


def total_kernel(scale, pieces_ref, pieces_out):
    total = jnp.zeros((PIECE, 2, LANES), F32)
    for at in range(64):
        total = total + pieces_ref[at * PIECE : (at + 1) * PIECE].astype(F32)
    total = total * scale
    small = jnp.sum(total[8], axis=0, keepdims=True)
    high = small.astype(BF16).astype(F32)
    small = jnp.where(iota((2, LANES), 0) == 0, high, small - high)
    big = total[0:8].astype(BF16)
    small = small.astype(BF16)
    for at in range(64):
        pieces_out[at * PIECE : at * PIECE + 8] = big
        pieces_out[at * PIECE + 8] = small


def unpack_kernel(own_ref, other_ref, expand_out, reduce_out, gain_out, kernel_out):
    first_core = (lax.axis_index("tiles") & 1) == 0

    def write(expand_from, reduce_from):
        for at in range(64):
            rows = slice(at * PIECE, at * PIECE + 8)
            piece = expand_from[rows].reshape(16, LANES).astype(F32)
            k, r = at // 16, at % 16
            expand_out[r * 16 : (r + 1) * 16, k * LANES : (k + 1) * LANES] = piece
            piece = reduce_from[rows].reshape(16, LANES).astype(F32)
            k, r = at // 32, at % 32
            reduce_out[r * 16 : (r + 1) * 16, k * LANES : (k + 1) * LANES] = piece

    @pl.when(first_core)
    def _():
        write(own_ref, other_ref)

    @pl.when(jnp.logical_not(first_core))
    def _():
        write(other_ref, own_ref)

    for at in range(50):
        total = own_ref[at * PIECE + 8].astype(F32) + other_ref[at * PIECE + 8].astype(F32)
        line = jnp.sum(total, axis=0, keepdims=True)
        if at < 49:
            kernel_out[at // 7, at % 7 : at % 7 + 1, :] = line
        else:
            gain_out[...] = line


def finish_kernel(
    ids_ref, mask_ref, ocean_ref, grad_ref, kernel_ref, mixed_ref, mixed_in_ref,
    grad_conv_ref, west_ref, east_ref, fold_ref,
    state_out, input_out, ext_ref, taps_ref, live_ref, back_ref, mixed_all,
):
    live_ref[...] = live_rows(mask_ref)
    mixed_all[...] = mixed_ref[...] + mixed_in_ref[...].astype(F32)
    build_extended(ext_ref, grad_conv_ref, west_ref, east_ref, None)
    spread_taps(kernel_ref, taps_ref, True)

    def row(y, carry):
        total = correlate_row(ext_ref, taps_ref, y).reshape(CELLS, LANES)
        back_ref[pl.ds(pl.multiple_of(y * CELLS, CELLS), CELLS), :] = total
        return carry

    lax.fori_loop(0, TS, row, 0)
    odd = (iota((1, SLOTS, LANES), 1) & 1) == 1
    top = iota((1, SLOTS, LANES), 1) >= 6
    mirrored = fold_ref[...].astype(F32).reshape(3, TS, SLOTS, LANES)
    swapped = jnp.where(
        odd[None],
        pltpu.roll(mirrored.reshape(24, SLOTS, LANES), 1, 1).reshape(3, TS, SLOTS, LANES),
        pltpu.roll(mirrored.reshape(24, SLOTS, LANES), 7, 1).reshape(3, TS, SLOTS, LANES),
    )
    swapped = jnp.where(top[None], swapped, 0.0)
    blank = jnp.zeros((3, SLOTS, LANES), F32)
    for r in range(3):
        band = jnp.zeros((TS, SLOTS, LANES), F32)
        for y in range(5 + r, 8):
            padded = jnp.concatenate([blank, swapped[y - 5], blank], axis=0)
            a = 11 + r - y
            for b in range(7):
                tap = taps_ref[(6 - a) * 7 + 6 - b]
                band = band + padded[6 - b : 14 - b] * tap[None]
        at = (7 - r) * CELLS
        turned = jnp.stack([band[7 - x] for x in range(TS)]).reshape(CELLS, LANES)
        back_ref[at : at + CELLS, :] = back_ref[at : at + CELLS, :] + turned
    for slot in range(SLOTS):
        rows = pl.ds(position(ids_ref[slot]), CELLS, stride=SLOTS)
        wet = jnp.where(ids_ref[slot] >= 0, 1.0, 0.0)
        live = live_ref[pl.ds(slot * CELLS, CELLS), :] * wet
        state = ocean_ref[slot].astype(F32).reshape(CELLS, LANES) * live
        state = (state + mixed_all[rows, :]) * live
        state_out[slot] = state.astype(BF16).reshape(TS, TS, LANES)
        cotangent = grad_ref[slot].astype(F32).reshape(CELLS, LANES) * live
        cotangent = (cotangent + back_ref[rows, :]) * live
        input_out[slot] = cotangent.astype(BF16).reshape(TS, TS, LANES)


def call(body, inputs, outputs, scratch=(), scalars=0, work=1.0):
    specs = [pl.BlockSpec(memory_space=pltpu.SMEM)] * scalars
    specs += [pl.BlockSpec(memory_space=pltpu.VMEM)] * (len(inputs) - scalars)
    return pl.pallas_call(
        body,
        out_shape=[jax.ShapeDtypeStruct(shape, kind) for shape, kind in outputs],
        in_specs=specs,
        out_specs=[pl.BlockSpec(memory_space=pltpu.VMEM)] * len(outputs),
        scratch_shapes=[pltpu.VMEM(shape, kind) for shape, kind in scratch],
        compiler_params=pltpu.CompilerParams(vmem_limit_bytes=40 * 1024 * 1024),
        cost_estimate=pl.CostEstimate(flops=int(work * WORK), bytes_accessed=0, transcendentals=0),
    )(*inputs)


def per_device(
    ocean_state, grad_state, sea_mask, tile_ids, neighbours, fold_partner,
    kernel, norm_gain, expand_weight, reduce_weight,
):
    devices = lax.axis_size("tiles")
    swap_chan = [(0, 1), (1, 0)]
    swap_core = [(i, i ^ 1) for i in range(devices)]
    ring = list(range(0, devices, 2)) + list(range(devices - 1, 0, -2))
    eastward = [(ring[i], ring[(i + 1) % devices]) for i in range(devices)]
    westward = [(there, here) for here, there in eastward]
    same_core = [list(range(core, devices, 2)) for core in range(2)]
    block = (ROWS, LANES)
    edge, top = (96, LANES), (192, LANES)
    ext_scratch = ((14, 14, SLOTS, LANES), F32)
    taps_scratch = ((49, SLOTS, LANES), F32)

    gain = norm_gain.reshape(1, LANES)
    grad_other = lax.ppermute(grad_state, "chan", swap_chan)
    gain_other = lax.ppermute(gain, "chan", swap_chan)

    dense, east, west, fold = call(
        prepare_kernel, [tile_ids, sea_mask, ocean_state],
        [(block, BF16), (edge, BF16), (edge, BF16), (top, BF16)],
        [(block, F32), (block, F32)], scalars=1, work=2,
    )
    from_west = lax.ppermute(east, "tiles", eastward)
    from_east = lax.ppermute(west, "tiles", westward)
    from_partner = lax.ppermute(fold, "tiles", swap_core)
    (cotangent,) = call(
        cotangent_kernel, [tile_ids, sea_mask, grad_state, grad_other],
        [((ROWS, WIDTH), BF16)], [(block, F32), (block, F32)], scalars=1, work=2,
    )
    conv, conv_send, extended = call(
        convolve_kernel, [dense, from_west, from_east, from_partner, kernel],
        [(block, F32), (block, BF16), ((14 * 14 * SLOTS, LANES), BF16)],
        [ext_scratch, taps_scratch], work=3,
    )
    conv_other = lax.ppermute(conv_send, "chan", swap_chan)
    normed, active, grad_hidden, grad_own, message, standard, inverse = call(
        pointwise_kernel,
        [conv, conv_other, gain, gain_other, cotangent, expand_weight, reduce_weight],
        [
            ((ROWS, WIDTH), BF16), ((ROWS, HALF_HID), BF16), ((ROWS, HALF_HID), BF16), (block, F32),
            ((ROWS + 64, LANES), BF16), (block, F32), (block, F32),
        ],
        [((CHUNK, WIDTH), F32)], work=6,
    )
    message_in = lax.ppermute(message, "chan", swap_chan)
    mixed, mixed_send, keep, send = call(
        weights_kernel, [normed, active, grad_hidden, cotangent, reduce_weight],
        [(block, F32), (block, BF16), ((1024, LANES), F32), ((1024, LANES), BF16)],
        [((ROWS, WIDTH), F32)], work=6,
    )
    arrived = lax.ppermute(send, "tiles", swap_core)
    mixed_in = lax.ppermute(mixed_send, "chan", swap_chan)
    grad_conv, east, west, fold, sums = call(
        norm_back_kernel, [grad_own, message, message_in, standard, inverse, gain, extended],
        [(block, BF16), (edge, BF16), (edge, BF16), (top, BF16), ((64, 8, LANES), F32)],
        [(block, F32)], work=6,
    )
    grad_west = lax.ppermute(east, "tiles", eastward)
    grad_east = lax.ppermute(west, "tiles", westward)
    grad_partner = lax.ppermute(fold, "tiles", swap_core)
    pieces_shape = ((64 * PIECE, 2, LANES), BF16)
    arrived, mixed_in = lax.optimization_barrier((arrived, mixed_in))
    (pieces,) = call(pack_kernel, [keep, arrived, sums], [pieces_shape])
    pieces = lax.all_to_all(pieces, "tiles", 0, 0, tiled=True, axis_index_groups=same_core)
    scale = 1.0 / math.sqrt(SLOTS * devices * CELLS)
    (pieces,) = call(functools.partial(total_kernel, scale), [pieces], [pieces_shape])
    pieces = lax.all_to_all(pieces, "tiles", 0, 0, tiled=True, axis_index_groups=same_core)
    new_state, grad_input = call(
        finish_kernel,
        [
            tile_ids, sea_mask, ocean_state, grad_state, kernel, mixed, mixed_in,
            grad_conv, grad_west, grad_east, grad_partner,
        ],
        [((SLOTS, TS, TS, LANES), BF16), ((SLOTS, TS, TS, LANES), BF16)],
        [ext_scratch, taps_scratch, (block, F32), (block, F32), (block, F32)],
        scalars=1, work=10,
    )
    pieces_other = lax.ppermute(pieces, "tiles", swap_core)
    expand_out, reduce_out, gain_out, kernel_out = call(
        unpack_kernel, [pieces, pieces_other],
        [((WIDTH, HALF_HID), F32), ((HALF_HID, WIDTH), F32), ((1, LANES), F32), ((7, 7, LANES), F32)],
    )
    return (new_state, grad_input, expand_out, reduce_out, gain_out.reshape(LANES), kernel_out)


def solution(mesh):
    return jax.shard_map(
        per_device,
        mesh=mesh,
        in_specs=(
            P("tiles", None, None, "chan"),
            P("tiles", None, None, "chan"),
            P("tiles", None, None),
            P("tiles"),
            P("tiles", None),
            P("tiles"),
            P(None, None, "chan"),
            P("chan"),
            P(None, "chan"),
            P("chan", None),
        ),
        out_specs=(
            P("tiles", None, None, "chan"),
            P("tiles", None, None, "chan"),
            P(None, "chan"),
            P("chan", None),
            P("chan"),
            P(None, None, "chan"),
        ),
        check_vma=False,
    )
```

```python
import functools
import math

import jax
import jax.numpy as jnp
from jax import lax
from jax.experimental import pallas as pl
from jax.experimental.pallas import tpu as pltpu
from jax.sharding import PartitionSpec as P

F32, BF16 = jnp.float32, jnp.bfloat16
TS = 8
CELLS = TS * TS
SLOTS = 8
ROWS = CELLS * SLOTS
LANES = 128
WIDTH = 256
HALF_HID = 512
GRID_COLUMNS = 256
PIECE = 9
MIB = 1024 * 1024
LARGE = 56 * MIB
WORK = 1_000_000_000
norm_eps = 1e-06
root_half = 0.7071067811865476
inv_root_tau = 0.3989422804014327

NN = (((1,), (0,)), ((), ()))
NT = (((1,), (1,)), ((), ()))
TN = (((0,), (0,)), ((), ()))


def dot(left, right, dims=NN):
    return lax.dot_general(left, right, dims, preferred_element_type=F32)


def iota(shape, axis):
    return lax.broadcasted_iota(jnp.int32, shape, axis)


def position(tile_id):
    safe = jnp.maximum(tile_id, 0)
    return lax.shift_right_logical(safe, 8) * 2 + (safe & 1)


def live_rows(mask_ref):
    marks = mask_ref[...].reshape(SLOTS * TS, TS).astype(F32).astype(BF16)
    wide = (ROWS, SLOTS * TS)
    owner = jnp.where(lax.shift_right_logical(iota(wide, 0), 3) == iota(wide, 1), 1.0, 0.0)
    spread = dot(owner.astype(BF16), marks)
    slim = (ROWS, TS)
    picked = jnp.where((iota(slim, 0) & 7) == iota(slim, 1), spread, 0.0)
    return dot(picked.astype(BF16), jnp.ones((TS, LANES), BF16))


def to_dense(ids_ref, field_ref, live_ref, dense_ref):
    dense_ref[...] = jnp.zeros((ROWS, LANES), F32)
    for slot in range(SLOTS):

        @pl.when(ids_ref[slot] >= 0)
        def _():
            values = field_ref[slot].astype(F32).reshape(CELLS, LANES)
            values = values * live_ref[pl.ds(slot * CELLS, CELLS), :]
            dense_ref[pl.ds(position(ids_ref[slot]), CELLS, stride=SLOTS), :] = values


def write_edges(cells, east_ref, west_ref, fold_ref):
    odd = (iota((1, SLOTS, LANES), 1) & 1) == 1
    for y in range(4):
        rows = slice(y * 24, (y + 1) * 24)
        packed = jnp.where(odd, cells[y, 5:8], pltpu.roll(cells[y + 4, 5:8], 7, 1))
        east_ref[rows, :] = packed.reshape(24, LANES).astype(BF16)
        packed = jnp.where(odd, pltpu.roll(cells[y + 4, 0:3], 1, 1), cells[y, 0:3])
        west_ref[rows, :] = packed.reshape(24, LANES).astype(BF16)
    fold_ref[...] = cells[5:8].reshape(192, LANES).astype(BF16)


def prepare_kernel(
    ids_hbm, mask_hbm, ocean_hbm, dense_out, east_out, west_out, fold_out,
    live_ref, dense_ref, ids_ref, mask_ref, ocean_ref, arrived,
):
    copies = [
        pltpu.make_async_copy(ids_hbm, ids_ref, arrived.at[0]),
        pltpu.make_async_copy(mask_hbm, mask_ref, arrived.at[1]),
        pltpu.make_async_copy(ocean_hbm, ocean_ref, arrived.at[2]),
    ]
    for copy in copies:
        copy.start()
    for copy in copies:
        copy.wait()
    live_ref[...] = live_rows(mask_ref)
    to_dense(ids_ref, ocean_ref, live_ref, dense_ref)
    values = dense_ref[...]
    dense_out[...] = values.astype(BF16)
    write_edges(values.reshape(TS, TS, SLOTS, LANES), east_out, west_out, fold_out)


def cotangent_kernel(ids_ref, mask_ref, own_ref, other_ref, full_out, live_ref, dense_ref):
    own_at = pl.multiple_of(lax.axis_index("chan") * LANES, LANES)
    other_at = pl.multiple_of(LANES - own_at, LANES)
    live_ref[...] = live_rows(mask_ref)
    to_dense(ids_ref, own_ref, live_ref, dense_ref)
    full_out[:, pl.ds(own_at, LANES)] = dense_ref[...].astype(BF16)
    to_dense(ids_ref, other_ref, live_ref, dense_ref)
    full_out[:, pl.ds(other_at, LANES)] = dense_ref[...].astype(BF16)


def build_extended(ext_ref, dense_ref, west_ref, east_ref, fold_ref):
    odd = (iota((1, SLOTS, LANES), 1) & 1) == 1
    place = iota((1, SLOTS, LANES), 1)
    from_west = west_ref[...].astype(F32).reshape(4, 3, SLOTS, LANES)
    from_east = east_ref[...].astype(F32).reshape(4, 3, SLOTS, LANES)
    for y in range(TS):
        line = dense_ref[pl.ds(y * CELLS, CELLS), :].astype(F32).reshape(TS, SLOTS, LANES)
        ext_ref[3 + y, 3:11] = line
        west = pltpu.roll(from_west[y], 7, 1) if y < 4 else from_west[y - 4]
        east = pltpu.roll(from_east[y], 1, 1) if y < 4 else from_east[y - 4]
        ext_ref[3 + y, 0:3] = jnp.where(odd, pltpu.roll(line[5:8], 1, 1), west)
        ext_ref[3 + y, 11:14] = jnp.where(odd, east, pltpu.roll(line[0:3], 7, 1))
    for r in range(3):
        ext_ref[r] = jnp.where(place >= 2, pltpu.roll(ext_ref[8 + r], 2, 1), 0.0)
        ext_ref[11 + r] = jnp.where(place < 6, pltpu.roll(ext_ref[3 + r], 6, 1), 0.0)
    if fold_ref is not None:
        mirrored = fold_ref[...].astype(F32).reshape(3, TS, SLOTS, LANES)
        for r in range(3):
            cells = jnp.stack([mirrored[2 - r, 7 - j] for j in range(TS)])
            swapped = jnp.where(odd, pltpu.roll(cells, 1, 1), pltpu.roll(cells, 7, 1))
            ext_ref[11 + r, 3:11] = jnp.where(place >= 6, swapped, ext_ref[11 + r, 3:11])


def spread_taps(kernel_ref, taps_ref, flipped):
    for a in range(7):
        for b in range(7):
            at = (6 - a) * 7 + 6 - b if flipped else a * 7 + b
            taps_ref[at] = jnp.broadcast_to(kernel_ref[a, b : b + 1, :], (SLOTS, LANES))


def correlate_row(ext_ref, taps_ref, y):
    total = None
    for a in range(7):
        line = ext_ref[y + a]
        for b in range(7):
            term = line[b : b + TS] * taps_ref[7 * a + b][None]
            total = term if total is None else total + term
    return total


def convolve_kernel(
    dense_ref, west_ref, east_ref, fold_ref, kernel_ref,
    lower_out, upper_out, lower_send, upper_send, ext_out, ext_ref, taps_ref,
):
    build_extended(ext_ref, dense_ref, west_ref, east_ref, fold_ref)
    spread_taps(kernel_ref, taps_ref, False)
    for first, conv_out, send_out in ((0, lower_out, lower_send), (TS // 2, upper_out, upper_send)):

        def row(y, carry):
            total = correlate_row(ext_ref, taps_ref, first + y).reshape(CELLS, LANES)
            rows = pl.ds(pl.multiple_of(y * CELLS, CELLS), CELLS)
            conv_out[rows, :] = total
            send_out[rows, :] = total.astype(BF16)
            return carry

        lax.fori_loop(0, TS // 2, row, 0)

    def keep(y, carry):
        rows = pl.ds(pl.multiple_of(y * 112, 112), 112)
        ext_out[rows, :] = ext_ref[y].reshape(112, LANES).astype(BF16)
        return carry

    lax.fori_loop(0, 14, keep, 0)


CHUNK = 128
HALF = ROWS // 2


def pointwise_kernel(
    first_row, own_ref, other_ref, own_gain_ref, other_gain_ref, cotangent_ref, expand_ref, reduce_ref,
    normed_out, active_out, hidden_out, grad_out, message_out, standard_out, inverse_out, wide_ref,
):
    own_at = pl.multiple_of(lax.axis_index("chan") * LANES, LANES)
    other_at = pl.multiple_of(LANES - own_at, LANES)
    own_gain, other_gain = own_gain_ref[...], other_gain_ref[...]
    ones = jnp.ones((8, LANES), BF16)

    def step(i, carry):
        rows = pl.ds(pl.multiple_of(i * CHUNK, CHUNK), CHUNK)
        own, other = own_ref[rows, :], other_ref[rows, :].astype(F32)
        mean = jnp.sum(own + other, axis=-1, keepdims=True) * (1.0 / WIDTH)
        own, other = own - mean, other - mean
        variance = jnp.sum(own * own + other * other, axis=-1, keepdims=True) * (1.0 / WIDTH)
        inverse = lax.rsqrt(variance + norm_eps)
        own, other = own * inverse, other * inverse
        standard_out[rows, :] = own
        inverse_out[rows, :] = jnp.broadcast_to(inverse, (CHUNK, LANES))
        normed_out[rows, pl.ds(own_at, LANES)] = (own * own_gain).astype(BF16)
        normed_out[rows, pl.ds(other_at, LANES)] = (other * other_gain).astype(BF16)
        hidden = dot(normed_out[rows, :], expand_ref[...])
        half = 0.5 * (1.0 + lax.erf(hidden * root_half))
        active_out[rows, :] = (hidden * half).astype(BF16)
        slope = half + hidden * jnp.exp(-0.5 * hidden * hidden) * inv_root_tau
        cotangent = cotangent_ref[pl.ds(pl.multiple_of(first_row + i * CHUNK, CHUNK), CHUNK), :]
        grad_hidden = (dot(cotangent, reduce_ref[...], NT) * slope).astype(BF16)
        hidden_out[rows, :] = grad_hidden
        wide_ref[...] = dot(grad_hidden, expand_ref[...], NT)
        own_grad = wide_ref[:, pl.ds(own_at, LANES)]
        other_grad = wide_ref[:, pl.ds(other_at, LANES)]
        grad_out[rows, :] = own_grad
        message_out[rows, :] = other_grad.astype(BF16)
        own_grad, other_grad = own_grad * own_gain, other_grad * other_gain
        first = (own_grad + other_grad).astype(BF16)
        second = (own_grad * own + other_grad * other).astype(BF16)
        moments = jnp.concatenate([dot(ones, first, NT), dot(ones, second, NT)], axis=0)
        message_out[pl.ds(pl.multiple_of(HALF + i * 16, 16), 16), :] = moments.astype(BF16)
        return carry

    lax.fori_loop(0, HALF // CHUNK, step, 0)


def weights_kernel(
    normed_lower, normed_upper, active_lower, active_upper, hidden_lower, hidden_upper, cotangent_ref, reduce_ref,
    mixed_out, mixed_send, keep_out, send_out, wide_ref,
):
    own_at = pl.multiple_of(lax.axis_index("chan") * LANES, LANES)
    other_at = pl.multiple_of(LANES - own_at, LANES)
    first_core = (lax.axis_index("tiles") & 1) == 0

    def write(out_ref, expand_kind):
        if expand_kind:
            for k in range(4):
                lanes = slice(k * LANES, (k + 1) * LANES)
                block = dot(normed_lower[...], hidden_lower[:, lanes], TN)
                block = block + dot(normed_upper[...], hidden_upper[:, lanes], TN)
                out_ref[k * WIDTH : (k + 1) * WIDTH, :] = block.astype(out_ref.dtype)
        else:
            for k in range(2):
                lanes = slice(k * LANES, (k + 1) * LANES)
                block = dot(active_lower[...], cotangent_ref[0:HALF, lanes], TN)
                block = block + dot(active_upper[...], cotangent_ref[HALF:ROWS, lanes], TN)
                out_ref[k * HALF_HID : (k + 1) * HALF_HID, :] = block.astype(out_ref.dtype)

    @pl.when(first_core)
    def _():
        write(send_out, False)
        write(keep_out, True)

    @pl.when(jnp.logical_not(first_core))
    def _():
        write(send_out, True)
        write(keep_out, False)

    wide_ref[0:HALF, :] = dot(active_lower[...], reduce_ref[...])
    wide_ref[HALF:ROWS, :] = dot(active_upper[...], reduce_ref[...])
    mixed_out[...] = wide_ref[:, pl.ds(own_at, LANES)]
    mixed_send[...] = wide_ref[:, pl.ds(other_at, LANES)].astype(BF16)


def norm_back_kernel(
    grad_lower, grad_upper, own_message_lower, own_message_upper, message_lower, message_upper,
    standard_lower, standard_upper, inverse_lower, inverse_upper, gain_ref, extended_ref,
    grad_conv_out, east_out, west_out, fold_out, sums_out, conv_ref,
):
    gain = gain_ref[...]
    kind = (iota((32, LANES), 0) & 8) == 0
    first_pick = jnp.where(kind, 1.0 / (8 * WIDTH), 0.0).astype(BF16)
    second_pick = jnp.where(kind, 0.0, 1.0 / (8 * WIDTH)).astype(BF16)
    gain_total = jnp.zeros((8, LANES), F32)
    halves = (
        (grad_lower, own_message_lower, message_lower, standard_lower, inverse_lower),
        (grad_upper, own_message_upper, message_upper, standard_upper, inverse_upper),
    )
    for first_row, (grad_ref, own_message_ref, message_ref, standard_ref, inverse_ref) in zip((0, HALF), halves):
        for i in range(HALF // CHUNK):
            rows = slice(i * CHUNK, (i + 1) * CHUNK)
            tail = slice(HALF + i * 16, HALF + (i + 1) * 16)
            moments = jnp.concatenate([own_message_ref[tail, :], message_ref[tail, :]], axis=0)
            first, second = dot(moments, first_pick, TN), dot(moments, second_pick, TN)
            grad = grad_ref[rows, :] + message_ref[rows, :].astype(F32)
            standard = standard_ref[rows, :]
            back = inverse_ref[rows, :] * (grad * gain - first - standard * second)
            back = back.astype(BF16)
            at = slice(first_row + i * CHUNK, first_row + (i + 1) * CHUNK)
            grad_conv_out[at, :] = back
            conv_ref[at, :] = back.astype(F32)
            gain_total = gain_total + jnp.sum((grad * standard).reshape(CHUNK // 8, 8, LANES), axis=0)

    write_edges(conv_ref[...].reshape(TS, TS, SLOTS, LANES), east_out, west_out, fold_out)
    sums_out[pl.ds(50, 14)] = jnp.zeros((14, 8, LANES), F32)
    sums_out[49] = gain_total

    def tap_row(a, carry):
        totals = [jnp.zeros((SLOTS, LANES), F32) for _ in range(7)]
        for y in range(TS):
            rows = pl.ds(pl.multiple_of((y + a) * 112, 112), 112)
            line = extended_ref[rows, :].astype(F32).reshape(14, SLOTS, LANES)
            grads = conv_ref[y * CELLS : (y + 1) * CELLS, :].reshape(TS, SLOTS, LANES)
            for b in range(7):
                totals[b] = totals[b] + jnp.sum(grads * line[b : b + TS], axis=0)
        for b in range(7):
            sums_out[a * 7 + b] = totals[b]
        return carry

    lax.fori_loop(0, 7, tap_row, 0)


def pack_kernel(keep_ref, arrived_ref, sums_ref, pieces_out):
    def step(i, carry):
        for k in range(8):
            at = i * 8 + k
            rows = pl.ds(pl.multiple_of(at * 16, 16), 16)
            big = keep_ref[rows, :] + arrived_ref[rows, :].astype(F32)
            pieces_out[pl.ds(at * PIECE, 8)] = big.astype(BF16).reshape(8, 2, LANES)
            small = sums_ref[at]
            small = small + pltpu.roll(small, 4, 0)
            small = small + pltpu.roll(small, 2, 0)
            pieces_out[at * PIECE + 8] = small[0:2].astype(BF16)
        return carry

    lax.fori_loop(0, 8, step, 0)


def total_kernel(scale, pieces_ref, pieces_out):
    total = jnp.zeros((PIECE, 2, LANES), F32)
    for at in range(64):
        total = total + pieces_ref[at * PIECE : (at + 1) * PIECE].astype(F32)
    total = total * scale
    small = jnp.sum(total[8], axis=0, keepdims=True)
    high = small.astype(BF16).astype(F32)
    small = jnp.where(iota((2, LANES), 0) == 0, high, small - high)
    big = total[0:8].astype(BF16)
    small = small.astype(BF16)
    for at in range(64):
        pieces_out[at * PIECE : at * PIECE + 8] = big
        pieces_out[at * PIECE + 8] = small


def unpack_kernel(own_ref, other_ref, expand_out, reduce_out, gain_out, kernel_out):
    first_core = (lax.axis_index("tiles") & 1) == 0

    def write(expand_from, reduce_from):
        for at in range(64):
            rows = slice(at * PIECE, at * PIECE + 8)
            piece = expand_from[rows].reshape(16, LANES).astype(F32)
            k, r = at // 16, at % 16
            expand_out[r * 16 : (r + 1) * 16, k * LANES : (k + 1) * LANES] = piece
            piece = reduce_from[rows].reshape(16, LANES).astype(F32)
            k, r = at // 32, at % 32
            reduce_out[r * 16 : (r + 1) * 16, k * LANES : (k + 1) * LANES] = piece

    @pl.when(first_core)
    def _():
        write(own_ref, other_ref)

    @pl.when(jnp.logical_not(first_core))
    def _():
        write(other_ref, own_ref)

    for at in range(50):
        total = own_ref[at * PIECE + 8].astype(F32) + other_ref[at * PIECE + 8].astype(F32)
        line = jnp.sum(total, axis=0, keepdims=True)
        if at < 49:
            kernel_out[at // 7, at % 7 : at % 7 + 1, :] = line
        else:
            gain_out[...] = line


def state_kernel(ids_ref, mask_ref, ocean_ref, mixed_ref, mixed_in_ref, state_out, live_out, mixed_all):
    live_out[...] = live_rows(mask_ref)
    mixed_all[...] = mixed_ref[...] + mixed_in_ref[...].astype(F32)
    for slot in range(SLOTS):
        rows = pl.ds(position(ids_ref[slot]), CELLS, stride=SLOTS)
        wet = jnp.where(ids_ref[slot] >= 0, 1.0, 0.0)
        own = pl.ds(slot * CELLS, CELLS)
        live = live_out[own, :] * wet
        live_out[own, :] = live
        state = ocean_ref[slot].astype(F32).reshape(CELLS, LANES) * live
        state = (state + mixed_all[rows, :]) * live
        state_out[slot] = state.astype(BF16).reshape(TS, TS, LANES)


def finish_kernel(
    ids_ref, live_ref, grad_ref, kernel_ref, grad_conv_ref, west_ref, east_ref, fold_ref,
    input_out, ext_ref, taps_ref, back_ref,
):
    build_extended(ext_ref, grad_conv_ref, west_ref, east_ref, None)
    spread_taps(kernel_ref, taps_ref, True)

    def row(y, carry):
        total = correlate_row(ext_ref, taps_ref, y).reshape(CELLS, LANES)
        back_ref[pl.ds(pl.multiple_of(y * CELLS, CELLS), CELLS), :] = total
        return carry

    lax.fori_loop(0, TS, row, 0)
    odd = (iota((1, SLOTS, LANES), 1) & 1) == 1
    top = iota((1, SLOTS, LANES), 1) >= 6
    mirrored = fold_ref[...].astype(F32).reshape(3, TS, SLOTS, LANES)
    swapped = jnp.where(
        odd[None],
        pltpu.roll(mirrored.reshape(24, SLOTS, LANES), 1, 1).reshape(3, TS, SLOTS, LANES),
        pltpu.roll(mirrored.reshape(24, SLOTS, LANES), 7, 1).reshape(3, TS, SLOTS, LANES),
    )
    swapped = jnp.where(top[None], swapped, 0.0)
    blank = jnp.zeros((3, SLOTS, LANES), F32)
    for r in range(3):
        band = jnp.zeros((TS, SLOTS, LANES), F32)
        for y in range(5 + r, 8):
            padded = jnp.concatenate([blank, swapped[y - 5], blank], axis=0)
            a = 11 + r - y
            for b in range(7):
                tap = taps_ref[(6 - a) * 7 + 6 - b]
                band = band + padded[6 - b : 14 - b] * tap[None]
        at = (7 - r) * CELLS
        turned = jnp.stack([band[7 - x] for x in range(TS)]).reshape(CELLS, LANES)
        back_ref[at : at + CELLS, :] = back_ref[at : at + CELLS, :] + turned
    for slot in range(SLOTS):
        rows = pl.ds(position(ids_ref[slot]), CELLS, stride=SLOTS)
        live = live_ref[pl.ds(slot * CELLS, CELLS), :]
        cotangent = grad_ref[slot].astype(F32).reshape(CELLS, LANES) * live
        cotangent = (cotangent + back_ref[rows, :]) * live
        input_out[slot] = cotangent.astype(BF16).reshape(TS, TS, LANES)


def call(body, inputs, outputs, scratch=(), scalars=0, work=1.0, own_copies=()):
    specs = [pl.BlockSpec(memory_space=pltpu.SMEM)] * scalars
    specs += [pl.BlockSpec(memory_space=pltpu.VMEM)] * (len(inputs) - scalars)
    if own_copies:
        specs = [pl.BlockSpec(memory_space=pltpu.HBM)] * len(inputs)
    return pl.pallas_call(
        body,
        out_shape=[jax.ShapeDtypeStruct(shape, kind) for shape, kind in outputs],
        in_specs=specs,
        out_specs=[pl.BlockSpec(memory_space=pltpu.VMEM)] * len(outputs),
        scratch_shapes=[pltpu.VMEM(shape, kind) for shape, kind in scratch] + list(own_copies),
        compiler_params=pltpu.CompilerParams(vmem_limit_bytes=(LARGE if own_copies else 40 * MIB)),
        cost_estimate=pl.CostEstimate(flops=int(work * WORK), bytes_accessed=0, transcendentals=0),
    )(*inputs)


def per_device(
    ocean_state, grad_state, sea_mask, tile_ids, neighbours, fold_partner,
    kernel, norm_gain, expand_weight, reduce_weight,
):
    devices = lax.axis_size("tiles")
    swap_chan = [(0, 1), (1, 0)]
    swap_core = [(i, i ^ 1) for i in range(devices)]
    ring = list(range(0, devices, 2)) + list(range(devices - 1, 0, -2))
    eastward = [(ring[i], ring[(i + 1) % devices]) for i in range(devices)]
    westward = [(there, here) for here, there in eastward]
    same_core = [list(range(core, devices, 2)) for core in range(2)]
    block = (ROWS, LANES)
    edge, top = (96, LANES), (192, LANES)
    ext_scratch = ((14, 14, SLOTS, LANES), F32)
    taps_scratch = ((49, SLOTS, LANES), F32)

    gain = norm_gain.reshape(1, LANES)
    grad_other = lax.ppermute(grad_state, "chan", swap_chan)
    gain_other = lax.ppermute(gain, "chan", swap_chan)

    dense, east, west, fold = call(
        prepare_kernel, [tile_ids, sea_mask, ocean_state],
        [(block, BF16), (edge, BF16), (edge, BF16), (top, BF16)],
        [(block, F32), (block, F32)], work=2,
        own_copies=[
            pltpu.SMEM((SLOTS,), jnp.int32), pltpu.VMEM((SLOTS, TS, TS), jnp.int32),
            pltpu.VMEM((SLOTS, TS, TS, LANES), BF16), pltpu.SemaphoreType.DMA((3,)),
        ],
    )
    from_west = lax.ppermute(east, "tiles", eastward)
    from_east = lax.ppermute(west, "tiles", westward)
    from_partner = lax.ppermute(fold, "tiles", swap_core)
    (cotangent,) = call(
        cotangent_kernel, [tile_ids, sea_mask, grad_state, grad_other],
        [((ROWS, WIDTH), BF16)], [(block, F32), (block, F32)], scalars=1, work=2,
    )
    part = (HALF, LANES)
    conv_lower, conv_upper, send_lower, send_upper, extended = call(
        convolve_kernel, [dense, from_west, from_east, from_partner, kernel],
        [(part, F32), (part, F32), (part, BF16), (part, BF16), ((14 * 14 * SLOTS, LANES), BF16)],
        [ext_scratch, taps_scratch], work=3,
    )
    other_lower = lax.ppermute(send_lower, "chan", swap_chan)
    other_upper = lax.ppermute(send_upper, "chan", swap_chan)
    stages = []
    for first_row, conv, conv_other in ((0, conv_lower, other_lower), (HALF, conv_upper, other_upper)):
        stages.append(call(
            functools.partial(pointwise_kernel, first_row),
            [conv, conv_other, gain, gain_other, cotangent, expand_weight, reduce_weight],
            [
                ((HALF, WIDTH), BF16), ((HALF, HALF_HID), BF16), ((HALF, HALF_HID), BF16), (part, F32),
                ((HALF + 32, LANES), BF16), (part, F32), (part, F32),
            ],
            [((CHUNK, WIDTH), F32)], work=3,
        ))
    normed, active, grad_hidden, grad_own, message, standard, inverse = (list(pair) for pair in zip(*stages))
    message_in = [lax.ppermute(half, "chan", swap_chan) for half in message]
    mixed, mixed_send, keep, send = call(
        weights_kernel, [*normed, *active, *grad_hidden, cotangent, reduce_weight],
        [(block, F32), (block, BF16), ((1024, LANES), F32), ((1024, LANES), BF16)],
        [((ROWS, WIDTH), F32)], work=6,
    )
    arrived = lax.ppermute(send, "tiles", swap_core)
    mixed_in = lax.ppermute(mixed_send, "chan", swap_chan)
    grad_conv, east, west, fold, sums = call(
        norm_back_kernel,
        [*grad_own, *message, *message_in, *standard, *inverse, gain, extended],
        [(block, BF16), (edge, BF16), (edge, BF16), (top, BF16), ((64, 8, LANES), F32)],
        [(block, F32)], work=6,
    )
    grad_west = lax.ppermute(east, "tiles", eastward)
    grad_east = lax.ppermute(west, "tiles", westward)
    grad_partner = lax.ppermute(fold, "tiles", swap_core)
    pieces_shape = ((64 * PIECE, 2, LANES), BF16)
    (pieces,) = call(pack_kernel, [keep, arrived, sums], [pieces_shape])
    pieces = lax.all_to_all(pieces, "tiles", 0, 0, tiled=True, axis_index_groups=same_core)
    scale = 1.0 / math.sqrt(SLOTS * devices * CELLS)
    (pieces,) = call(functools.partial(total_kernel, scale), [pieces], [pieces_shape])
    pieces = lax.all_to_all(pieces, "tiles", 0, 0, tiled=True, axis_index_groups=same_core)
    new_state, live = call(
        state_kernel, [tile_ids, sea_mask, ocean_state, mixed, mixed_in],
        [((SLOTS, TS, TS, LANES), BF16), (block, F32)], [(block, F32)], scalars=1, work=2,
    )
    pieces, new_state = lax.optimization_barrier((pieces, new_state))
    pieces_other = lax.ppermute(pieces, "tiles", swap_core)
    (grad_input,) = call(
        finish_kernel,
        [tile_ids, live, grad_state, kernel, grad_conv, grad_west, grad_east, grad_partner],
        [((SLOTS, TS, TS, LANES), BF16)],
        [ext_scratch, taps_scratch, (block, F32)], scalars=1, work=10,
    )
    expand_out, reduce_out, gain_out, kernel_out = call(
        unpack_kernel, [pieces, pieces_other],
        [((WIDTH, HALF_HID), F32), ((HALF_HID, WIDTH), F32), ((1, LANES), F32), ((7, 7, LANES), F32)],
    )
    return (new_state, grad_input, expand_out, reduce_out, gain_out.reshape(LANES), kernel_out)


def solution(mesh):
    return jax.shard_map(
        per_device,
        mesh=mesh,
        in_specs=(
            P("tiles", None, None, "chan"),
            P("tiles", None, None, "chan"),
            P("tiles", None, None),
            P("tiles"),
            P("tiles", None),
            P("tiles"),
            P(None, None, "chan"),
            P("chan"),
            P(None, "chan"),
            P("chan", None),
        ),
        out_specs=(
            P("tiles", None, None, "chan"),
            P("tiles", None, None, "chan"),
            P(None, "chan"),
            P("chan", None),
            P("chan"),
            P(None, None, "chan"),
        ),
        check_vma=False,
    )
```

```python
import functools
import math

import jax
import jax.numpy as jnp
from jax import lax
from jax.experimental import pallas as pl
from jax.experimental.pallas import tpu as pltpu
from jax.sharding import PartitionSpec as P

F32, BF16 = jnp.float32, jnp.bfloat16
TS = 8
CELLS = TS * TS
SLOTS = 8
ROWS = CELLS * SLOTS
LANES = 128
WIDTH = 256
HALF_HID = 512
GRID_COLUMNS = 256
PIECE = 9
MIB = 1024 * 1024
LARGE = 56 * MIB
WORK = 1_000_000_000
norm_eps = 1e-06
root_half = 0.7071067811865476
inv_root_tau = 0.3989422804014327

NN = (((1,), (0,)), ((), ()))
NT = (((1,), (1,)), ((), ()))
TN = (((0,), (0,)), ((), ()))


def dot(left, right, dims=NN):
    return lax.dot_general(left, right, dims, preferred_element_type=F32)


def iota(shape, axis):
    return lax.broadcasted_iota(jnp.int32, shape, axis)


def position(tile_id):
    safe = jnp.maximum(tile_id, 0)
    return lax.shift_right_logical(safe, 8) * 2 + (safe & 1)


def live_rows(mask_ref):
    marks = mask_ref[...].reshape(SLOTS * TS, TS).astype(F32).astype(BF16)
    wide = (ROWS, SLOTS * TS)
    owner = jnp.where(lax.shift_right_logical(iota(wide, 0), 3) == iota(wide, 1), 1.0, 0.0)
    spread = dot(owner.astype(BF16), marks)
    slim = (ROWS, TS)
    picked = jnp.where((iota(slim, 0) & 7) == iota(slim, 1), spread, 0.0)
    return dot(picked.astype(BF16), jnp.ones((TS, LANES), BF16))


def to_dense(ids_ref, field_ref, live_ref, dense_ref):
    dense_ref[...] = jnp.zeros((ROWS, LANES), F32)
    for slot in range(SLOTS):

        @pl.when(ids_ref[slot] >= 0)
        def _():
            values = field_ref[slot].astype(F32).reshape(CELLS, LANES)
            values = values * live_ref[pl.ds(slot * CELLS, CELLS), :]
            dense_ref[pl.ds(position(ids_ref[slot]), CELLS, stride=SLOTS), :] = values


def write_edges(cells, east_ref, west_ref, fold_ref):
    odd = (iota((1, SLOTS, LANES), 1) & 1) == 1
    for y in range(4):
        rows = slice(y * 24, (y + 1) * 24)
        packed = jnp.where(odd, cells[y, 5:8], pltpu.roll(cells[y + 4, 5:8], 7, 1))
        east_ref[rows, :] = packed.reshape(24, LANES).astype(BF16)
        packed = jnp.where(odd, pltpu.roll(cells[y + 4, 0:3], 1, 1), cells[y, 0:3])
        west_ref[rows, :] = packed.reshape(24, LANES).astype(BF16)
    fold_ref[...] = cells[5:8].reshape(192, LANES).astype(BF16)


def prepare_kernel(
    ids_hbm, mask_hbm, ocean_hbm, dense_out, east_out, west_out, fold_out,
    live_ref, dense_ref, ids_ref, mask_ref, ocean_ref, arrived,
):
    copies = [
        pltpu.make_async_copy(ids_hbm, ids_ref, arrived.at[0]),
        pltpu.make_async_copy(mask_hbm, mask_ref, arrived.at[1]),
        pltpu.make_async_copy(ocean_hbm, ocean_ref, arrived.at[2]),
    ]
    for copy in copies:
        copy.start()
    for copy in copies:
        copy.wait()
    live_ref[...] = live_rows(mask_ref)
    to_dense(ids_ref, ocean_ref, live_ref, dense_ref)
    values = dense_ref[...]
    dense_out[...] = values.astype(BF16)
    write_edges(values.reshape(TS, TS, SLOTS, LANES), east_out, west_out, fold_out)


def cotangent_kernel(ids_ref, mask_ref, own_ref, other_ref, full_out, live_ref, dense_ref):
    own_at = pl.multiple_of(lax.axis_index("chan") * LANES, LANES)
    other_at = pl.multiple_of(LANES - own_at, LANES)
    live_ref[...] = live_rows(mask_ref)
    to_dense(ids_ref, own_ref, live_ref, dense_ref)
    full_out[:, pl.ds(own_at, LANES)] = dense_ref[...].astype(BF16)
    to_dense(ids_ref, other_ref, live_ref, dense_ref)
    full_out[:, pl.ds(other_at, LANES)] = dense_ref[...].astype(BF16)


def extend_locally(ext_ref, dense_ref):
    place = iota((1, SLOTS, LANES), 1)
    odd = (place & 1) == 1
    for y in range(TS):
        line = dense_ref[pl.ds(y * CELLS, CELLS), :].astype(F32).reshape(TS, SLOTS, LANES)
        ext_ref[3 + y, 3:11] = line
        ext_ref[3 + y, 0:3] = jnp.where(odd, pltpu.roll(line[5:8], 1, 1), 0.0)
        ext_ref[3 + y, 11:14] = jnp.where(odd, 0.0, pltpu.roll(line[0:3], 7, 1))
    for r in range(3):
        ext_ref[r] = jnp.where(place >= 2, pltpu.roll(ext_ref[8 + r], 2, 1), 0.0)
        ext_ref[11 + r] = jnp.where(place < 6, pltpu.roll(ext_ref[3 + r], 6, 1), 0.0)


def add_columns(ext_ref, west_ref, east_ref):
    place = iota((1, SLOTS, LANES), 1)
    odd = (place & 1) == 1
    from_west = west_ref[...].astype(F32).reshape(4, 3, SLOTS, LANES)
    from_east = east_ref[...].astype(F32).reshape(4, 3, SLOTS, LANES)
    for y in range(TS):
        west = pltpu.roll(from_west[y], 7, 1) if y < 4 else from_west[y - 4]
        east = pltpu.roll(from_east[y], 1, 1) if y < 4 else from_east[y - 4]
        ext_ref[3 + y, 0:3] = jnp.where(odd, ext_ref[3 + y, 0:3], west)
        ext_ref[3 + y, 11:14] = jnp.where(odd, east, ext_ref[3 + y, 11:14])
    for r in range(3):
        for side in (slice(0, 3), slice(11, 14)):
            ext_ref[r, side] = jnp.where(place >= 2, pltpu.roll(ext_ref[8 + r, side], 2, 1), 0.0)
            ext_ref[11 + r, side] = jnp.where(place < 6, pltpu.roll(ext_ref[3 + r, side], 6, 1), 0.0)


def add_fold(ext_ref, fold_ref):
    place = iota((1, SLOTS, LANES), 1)
    odd = (place & 1) == 1
    mirrored = fold_ref[...].astype(F32).reshape(3, TS, SLOTS, LANES)
    for r in range(3):
        cells = jnp.stack([mirrored[2 - r, 7 - j] for j in range(TS)])
        swapped = jnp.where(odd, pltpu.roll(cells, 1, 1), pltpu.roll(cells, 7, 1))
        ext_ref[11 + r, 3:11] = jnp.where(place >= 6, swapped, ext_ref[11 + r, 3:11])


def spread_taps(kernel_ref, taps_ref, flipped):
    for a in range(7):
        for b in range(7):
            at = (6 - a) * 7 + 6 - b if flipped else a * 7 + b
            taps_ref[at] = jnp.broadcast_to(kernel_ref[a, b : b + 1, :], (SLOTS, LANES))


def correlate_row(ext_ref, taps_ref, y):
    total = None
    for a in range(7):
        line = ext_ref[y + a]
        for b in range(7):
            term = line[b : b + TS] * taps_ref[7 * a + b][None]
            total = term if total is None else total + term
    return total


def extend_kernel(dense_ref, kernel_ref, ext_out, taps_out):
    extend_locally(ext_out, dense_ref)
    spread_taps(kernel_ref, taps_out, False)


def convolve_kernel(
    local_ref, taps_ref, west_ref, east_ref, fold_ref,
    lower_out, upper_out, lower_send, upper_send, ext_out, ext_ref,
):
    ext_ref[...] = local_ref[...]
    add_columns(ext_ref, west_ref, east_ref)
    add_fold(ext_ref, fold_ref)
    for first, conv_out, send_out in ((0, lower_out, lower_send), (TS // 2, upper_out, upper_send)):

        def row(y, carry):
            total = correlate_row(ext_ref, taps_ref, first + y).reshape(CELLS, LANES)
            rows = pl.ds(pl.multiple_of(y * CELLS, CELLS), CELLS)
            conv_out[rows, :] = total
            send_out[rows, :] = total.astype(BF16)
            return carry

        lax.fori_loop(0, TS // 2, row, 0)

    def keep(y, carry):
        rows = pl.ds(pl.multiple_of(y * 112, 112), 112)
        ext_out[rows, :] = ext_ref[y].reshape(112, LANES).astype(BF16)
        return carry

    lax.fori_loop(0, 14, keep, 0)


CHUNK = 128
HALF = ROWS // 2


def pointwise_kernel(
    first_row, own_ref, other_ref, own_gain_ref, other_gain_ref, cotangent_ref, expand_ref, reduce_ref,
    normed_out, active_out, hidden_out, grad_out, message_out, standard_out, inverse_out, wide_ref,
):
    own_at = pl.multiple_of(lax.axis_index("chan") * LANES, LANES)
    other_at = pl.multiple_of(LANES - own_at, LANES)
    own_gain, other_gain = own_gain_ref[...], other_gain_ref[...]
    ones = jnp.ones((8, LANES), BF16)

    def step(i, carry):
        rows = pl.ds(pl.multiple_of(i * CHUNK, CHUNK), CHUNK)
        own, other = own_ref[rows, :], other_ref[rows, :].astype(F32)
        mean = jnp.sum(own + other, axis=-1, keepdims=True) * (1.0 / WIDTH)
        own, other = own - mean, other - mean
        variance = jnp.sum(own * own + other * other, axis=-1, keepdims=True) * (1.0 / WIDTH)
        inverse = lax.rsqrt(variance + norm_eps)
        own, other = own * inverse, other * inverse
        standard_out[rows, :] = own
        inverse_out[rows, :] = jnp.broadcast_to(inverse, (CHUNK, LANES))
        normed_out[rows, pl.ds(own_at, LANES)] = (own * own_gain).astype(BF16)
        normed_out[rows, pl.ds(other_at, LANES)] = (other * other_gain).astype(BF16)
        hidden = dot(normed_out[rows, :], expand_ref[...])
        half = 0.5 * (1.0 + lax.erf(hidden * root_half))
        active_out[rows, :] = (hidden * half).astype(BF16)
        slope = half + hidden * jnp.exp(-0.5 * hidden * hidden) * inv_root_tau
        cotangent = cotangent_ref[pl.ds(pl.multiple_of(first_row + i * CHUNK, CHUNK), CHUNK), :]
        grad_hidden = (dot(cotangent, reduce_ref[...], NT) * slope).astype(BF16)
        hidden_out[rows, :] = grad_hidden
        wide_ref[...] = dot(grad_hidden, expand_ref[...], NT)
        own_grad = wide_ref[:, pl.ds(own_at, LANES)]
        other_grad = wide_ref[:, pl.ds(other_at, LANES)]
        grad_out[rows, :] = own_grad
        message_out[rows, :] = other_grad.astype(BF16)
        own_grad, other_grad = own_grad * own_gain, other_grad * other_gain
        first = (own_grad + other_grad).astype(BF16)
        second = (own_grad * own + other_grad * other).astype(BF16)
        moments = jnp.concatenate([dot(ones, first, NT), dot(ones, second, NT)], axis=0)
        message_out[pl.ds(pl.multiple_of(HALF + i * 16, 16), 16), :] = moments.astype(BF16)
        return carry

    lax.fori_loop(0, HALF // CHUNK, step, 0)


def weights_kernel(
    normed_lower, normed_upper, active_lower, active_upper, hidden_lower, hidden_upper, cotangent_ref, reduce_ref,
    mixed_out, mixed_send, keep_out, send_out, wide_ref,
):
    own_at = pl.multiple_of(lax.axis_index("chan") * LANES, LANES)
    other_at = pl.multiple_of(LANES - own_at, LANES)
    first_core = (lax.axis_index("tiles") & 1) == 0

    def write(out_ref, expand_kind):
        if expand_kind:
            for k in range(4):
                lanes = slice(k * LANES, (k + 1) * LANES)
                block = dot(normed_lower[...], hidden_lower[:, lanes], TN)
                block = block + dot(normed_upper[...], hidden_upper[:, lanes], TN)
                out_ref[k * WIDTH : (k + 1) * WIDTH, :] = block.astype(out_ref.dtype)
        else:
            for k in range(2):
                lanes = slice(k * LANES, (k + 1) * LANES)
                block = dot(active_lower[...], cotangent_ref[0:HALF, lanes], TN)
                block = block + dot(active_upper[...], cotangent_ref[HALF:ROWS, lanes], TN)
                out_ref[k * HALF_HID : (k + 1) * HALF_HID, :] = block.astype(out_ref.dtype)

    @pl.when(first_core)
    def _():
        write(send_out, False)
        write(keep_out, True)

    @pl.when(jnp.logical_not(first_core))
    def _():
        write(send_out, True)
        write(keep_out, False)

    wide_ref[0:HALF, :] = dot(active_lower[...], reduce_ref[...])
    wide_ref[HALF:ROWS, :] = dot(active_upper[...], reduce_ref[...])
    mixed_out[...] = wide_ref[:, pl.ds(own_at, LANES)]
    mixed_send[...] = wide_ref[:, pl.ds(other_at, LANES)].astype(BF16)


def norm_back_kernel(
    grad_lower, grad_upper, own_message_lower, own_message_upper, message_lower, message_upper,
    standard_lower, standard_upper, inverse_lower, inverse_upper, gain_ref, extended_ref,
    grad_conv_out, east_out, west_out, fold_out, sums_out, conv_ref,
):
    gain = gain_ref[...]
    kind = (iota((32, LANES), 0) & 8) == 0
    first_pick = jnp.where(kind, 1.0 / (8 * WIDTH), 0.0).astype(BF16)
    second_pick = jnp.where(kind, 0.0, 1.0 / (8 * WIDTH)).astype(BF16)
    gain_total = jnp.zeros((8, LANES), F32)
    halves = (
        (grad_lower, own_message_lower, message_lower, standard_lower, inverse_lower),
        (grad_upper, own_message_upper, message_upper, standard_upper, inverse_upper),
    )
    for first_row, (grad_ref, own_message_ref, message_ref, standard_ref, inverse_ref) in zip((0, HALF), halves):
        for i in range(HALF // CHUNK):
            rows = slice(i * CHUNK, (i + 1) * CHUNK)
            tail = slice(HALF + i * 16, HALF + (i + 1) * 16)
            moments = jnp.concatenate([own_message_ref[tail, :], message_ref[tail, :]], axis=0)
            first, second = dot(moments, first_pick, TN), dot(moments, second_pick, TN)
            grad = grad_ref[rows, :] + message_ref[rows, :].astype(F32)
            standard = standard_ref[rows, :]
            back = inverse_ref[rows, :] * (grad * gain - first - standard * second)
            back = back.astype(BF16)
            at = slice(first_row + i * CHUNK, first_row + (i + 1) * CHUNK)
            grad_conv_out[at, :] = back
            conv_ref[at, :] = back.astype(F32)
            gain_total = gain_total + jnp.sum((grad * standard).reshape(CHUNK // 8, 8, LANES), axis=0)

    write_edges(conv_ref[...].reshape(TS, TS, SLOTS, LANES), east_out, west_out, fold_out)
    sums_out[pl.ds(50, 14)] = jnp.zeros((14, 8, LANES), F32)
    sums_out[49] = gain_total

    def tap_row(a, carry):
        totals = [jnp.zeros((SLOTS, LANES), F32) for _ in range(7)]
        for y in range(TS):
            rows = pl.ds(pl.multiple_of((y + a) * 112, 112), 112)
            line = extended_ref[rows, :].astype(F32).reshape(14, SLOTS, LANES)
            grads = conv_ref[y * CELLS : (y + 1) * CELLS, :].reshape(TS, SLOTS, LANES)
            for b in range(7):
                totals[b] = totals[b] + jnp.sum(grads * line[b : b + TS], axis=0)
        for b in range(7):
            sums_out[a * 7 + b] = totals[b]
        return carry

    lax.fori_loop(0, 7, tap_row, 0)


def pack_kernel(keep_ref, arrived_ref, sums_ref, pieces_out):
    def step(i, carry):
        for k in range(8):
            at = i * 8 + k
            rows = pl.ds(pl.multiple_of(at * 16, 16), 16)
            big = keep_ref[rows, :] + arrived_ref[rows, :].astype(F32)
            pieces_out[pl.ds(at * PIECE, 8)] = big.astype(BF16).reshape(8, 2, LANES)
            small = sums_ref[at]
            small = small + pltpu.roll(small, 4, 0)
            small = small + pltpu.roll(small, 2, 0)
            pieces_out[at * PIECE + 8] = small[0:2].astype(BF16)
        return carry

    lax.fori_loop(0, 8, step, 0)


def total_kernel(scale, pieces_ref, pieces_out):
    total = jnp.zeros((PIECE, 2, LANES), F32)
    for at in range(64):
        total = total + pieces_ref[at * PIECE : (at + 1) * PIECE].astype(F32)
    total = total * scale
    small = jnp.sum(total[8], axis=0, keepdims=True)
    high = small.astype(BF16).astype(F32)
    small = jnp.where(iota((2, LANES), 0) == 0, high, small - high)
    big = total[0:8].astype(BF16)
    small = small.astype(BF16)
    for at in range(64):
        pieces_out[at * PIECE : at * PIECE + 8] = big
        pieces_out[at * PIECE + 8] = small


def unpack_kernel(own_ref, other_ref, expand_out, reduce_out, gain_out, kernel_out):
    first_core = (lax.axis_index("tiles") & 1) == 0

    def write(expand_from, reduce_from):
        for at in range(64):
            rows = slice(at * PIECE, at * PIECE + 8)
            piece = expand_from[rows].reshape(16, LANES).astype(F32)
            k, r = at // 16, at % 16
            expand_out[r * 16 : (r + 1) * 16, k * LANES : (k + 1) * LANES] = piece
            piece = reduce_from[rows].reshape(16, LANES).astype(F32)
            k, r = at // 32, at % 32
            reduce_out[r * 16 : (r + 1) * 16, k * LANES : (k + 1) * LANES] = piece

    @pl.when(first_core)
    def _():
        write(own_ref, other_ref)

    @pl.when(jnp.logical_not(first_core))
    def _():
        write(other_ref, own_ref)

    for at in range(50):
        total = own_ref[at * PIECE + 8].astype(F32) + other_ref[at * PIECE + 8].astype(F32)
        line = jnp.sum(total, axis=0, keepdims=True)
        if at < 49:
            kernel_out[at // 7, at % 7 : at % 7 + 1, :] = line
        else:
            gain_out[...] = line


def state_kernel(ids_ref, mask_ref, ocean_ref, mixed_ref, mixed_in_ref, state_out, live_out, mixed_all):
    live_out[...] = live_rows(mask_ref)
    mixed_all[...] = mixed_ref[...] + mixed_in_ref[...].astype(F32)
    for slot in range(SLOTS):
        rows = pl.ds(position(ids_ref[slot]), CELLS, stride=SLOTS)
        wet = jnp.where(ids_ref[slot] >= 0, 1.0, 0.0)
        own = pl.ds(slot * CELLS, CELLS)
        live = live_out[own, :] * wet
        live_out[own, :] = live
        state = ocean_ref[slot].astype(F32).reshape(CELLS, LANES) * live
        state = (state + mixed_all[rows, :]) * live
        state_out[slot] = state.astype(BF16).reshape(TS, TS, LANES)


def finish_kernel(
    ids_ref, live_ref, grad_ref, kernel_ref, grad_conv_ref, west_ref, east_ref, fold_ref,
    input_out, ext_ref, taps_ref, back_ref,
):
    extend_locally(ext_ref, grad_conv_ref)
    add_columns(ext_ref, west_ref, east_ref)
    spread_taps(kernel_ref, taps_ref, True)

    def row(y, carry):
        total = correlate_row(ext_ref, taps_ref, y).reshape(CELLS, LANES)
        back_ref[pl.ds(pl.multiple_of(y * CELLS, CELLS), CELLS), :] = total
        return carry

    lax.fori_loop(0, TS, row, 0)
    odd = (iota((1, SLOTS, LANES), 1) & 1) == 1
    top = iota((1, SLOTS, LANES), 1) >= 6
    mirrored = fold_ref[...].astype(F32).reshape(3, TS, SLOTS, LANES)
    swapped = jnp.where(
        odd[None],
        pltpu.roll(mirrored.reshape(24, SLOTS, LANES), 1, 1).reshape(3, TS, SLOTS, LANES),
        pltpu.roll(mirrored.reshape(24, SLOTS, LANES), 7, 1).reshape(3, TS, SLOTS, LANES),
    )
    swapped = jnp.where(top[None], swapped, 0.0)
    blank = jnp.zeros((3, SLOTS, LANES), F32)
    for r in range(3):
        band = jnp.zeros((TS, SLOTS, LANES), F32)
        for y in range(5 + r, 8):
            padded = jnp.concatenate([blank, swapped[y - 5], blank], axis=0)
            a = 11 + r - y
            for b in range(7):
                tap = taps_ref[(6 - a) * 7 + 6 - b]
                band = band + padded[6 - b : 14 - b] * tap[None]
        at = (7 - r) * CELLS
        turned = jnp.stack([band[7 - x] for x in range(TS)]).reshape(CELLS, LANES)
        back_ref[at : at + CELLS, :] = back_ref[at : at + CELLS, :] + turned
    for slot in range(SLOTS):
        rows = pl.ds(position(ids_ref[slot]), CELLS, stride=SLOTS)
        live = live_ref[pl.ds(slot * CELLS, CELLS), :]
        cotangent = grad_ref[slot].astype(F32).reshape(CELLS, LANES) * live
        cotangent = (cotangent + back_ref[rows, :]) * live
        input_out[slot] = cotangent.astype(BF16).reshape(TS, TS, LANES)


def call(body, inputs, outputs, scratch=(), scalars=0, work=1.0, own_copies=()):
    specs = [pl.BlockSpec(memory_space=pltpu.SMEM)] * scalars
    specs += [pl.BlockSpec(memory_space=pltpu.VMEM)] * (len(inputs) - scalars)
    if own_copies:
        specs = [pl.BlockSpec(memory_space=pltpu.HBM)] * len(inputs)
    return pl.pallas_call(
        body,
        out_shape=[jax.ShapeDtypeStruct(shape, kind) for shape, kind in outputs],
        in_specs=specs,
        out_specs=[pl.BlockSpec(memory_space=pltpu.VMEM)] * len(outputs),
        scratch_shapes=[pltpu.VMEM(shape, kind) for shape, kind in scratch] + list(own_copies),
        compiler_params=pltpu.CompilerParams(vmem_limit_bytes=(LARGE if own_copies else 40 * MIB)),
        cost_estimate=pl.CostEstimate(flops=int(work * WORK), bytes_accessed=0, transcendentals=0),
    )(*inputs)


def per_device(
    ocean_state, grad_state, sea_mask, tile_ids, neighbours, fold_partner,
    kernel, norm_gain, expand_weight, reduce_weight,
):
    devices = lax.axis_size("tiles")
    swap_chan = [(0, 1), (1, 0)]
    swap_core = [(i, i ^ 1) for i in range(devices)]
    ring = list(range(0, devices, 2)) + list(range(devices - 1, 0, -2))
    eastward = [(ring[i], ring[(i + 1) % devices]) for i in range(devices)]
    westward = [(there, here) for here, there in eastward]
    same_core = [list(range(core, devices, 2)) for core in range(2)]
    block = (ROWS, LANES)
    edge, top = (96, LANES), (192, LANES)
    ext_scratch = ((14, 14, SLOTS, LANES), F32)
    taps_scratch = ((49, SLOTS, LANES), F32)

    gain = norm_gain.reshape(1, LANES)
    grad_other = lax.ppermute(grad_state, "chan", swap_chan)
    gain_other = lax.ppermute(gain, "chan", swap_chan)

    dense, east, west, fold = call(
        prepare_kernel, [tile_ids, sea_mask, ocean_state],
        [(block, BF16), (edge, BF16), (edge, BF16), (top, BF16)],
        [(block, F32), (block, F32)], work=2,
        own_copies=[
            pltpu.SMEM((SLOTS,), jnp.int32), pltpu.VMEM((SLOTS, TS, TS), jnp.int32),
            pltpu.VMEM((SLOTS, TS, TS, LANES), BF16), pltpu.SemaphoreType.DMA((3,)),
        ],
    )
    from_west = lax.ppermute(east, "tiles", eastward)
    from_east = lax.ppermute(west, "tiles", westward)
    from_partner = lax.ppermute(fold, "tiles", swap_core)
    (cotangent,) = call(
        cotangent_kernel, [tile_ids, sea_mask, grad_state, grad_other],
        [((ROWS, WIDTH), BF16)], [(block, F32), (block, F32)], scalars=1, work=2,
    )
    part = (HALF, LANES)
    local, taps = call(extend_kernel, [dense, kernel], [ext_scratch, taps_scratch], work=2)
    conv_lower, conv_upper, send_lower, send_upper, extended = call(
        convolve_kernel, [local, taps, from_west, from_east, from_partner],
        [(part, F32), (part, F32), (part, BF16), (part, BF16), ((14 * 14 * SLOTS, LANES), BF16)],
        [ext_scratch], work=3,
    )
    other_lower = lax.ppermute(send_lower, "chan", swap_chan)
    other_upper = lax.ppermute(send_upper, "chan", swap_chan)
    stages = []
    for first_row, conv, conv_other in ((0, conv_lower, other_lower), (HALF, conv_upper, other_upper)):
        stages.append(call(
            functools.partial(pointwise_kernel, first_row),
            [conv, conv_other, gain, gain_other, cotangent, expand_weight, reduce_weight],
            [
                ((HALF, WIDTH), BF16), ((HALF, HALF_HID), BF16), ((HALF, HALF_HID), BF16), (part, F32),
                ((HALF + 32, LANES), BF16), (part, F32), (part, F32),
            ],
            [((CHUNK, WIDTH), F32)], work=3,
        ))
    normed, active, grad_hidden, grad_own, message, standard, inverse = (list(pair) for pair in zip(*stages))
    message_in = [lax.ppermute(half, "chan", swap_chan) for half in message]
    mixed, mixed_send, keep, send = call(
        weights_kernel, [*normed, *active, *grad_hidden, cotangent, reduce_weight],
        [(block, F32), (block, BF16), ((1024, LANES), F32), ((1024, LANES), BF16)],
        [((ROWS, WIDTH), F32)], work=6,
    )
    arrived = lax.ppermute(send, "tiles", swap_core)
    mixed_in = lax.ppermute(mixed_send, "chan", swap_chan)
    grad_conv, east, west, fold, sums = call(
        norm_back_kernel,
        [*grad_own, *message, *message_in, *standard, *inverse, gain, extended],
        [(block, BF16), (edge, BF16), (edge, BF16), (top, BF16), ((64, 8, LANES), F32)],
        [(block, F32)], work=6,
    )
    grad_west = lax.ppermute(east, "tiles", eastward)
    grad_east = lax.ppermute(west, "tiles", westward)
    grad_partner = lax.ppermute(fold, "tiles", swap_core)
    pieces_shape = ((64 * PIECE, 2, LANES), BF16)
    (pieces,) = call(pack_kernel, [keep, arrived, sums], [pieces_shape])
    pieces = lax.all_to_all(pieces, "tiles", 0, 0, tiled=True, axis_index_groups=same_core)
    scale = 1.0 / math.sqrt(SLOTS * devices * CELLS)
    (pieces,) = call(functools.partial(total_kernel, scale), [pieces], [pieces_shape])
    pieces = lax.all_to_all(pieces, "tiles", 0, 0, tiled=True, axis_index_groups=same_core)
    new_state, live = call(
        state_kernel, [tile_ids, sea_mask, ocean_state, mixed, mixed_in],
        [((SLOTS, TS, TS, LANES), BF16), (block, F32)], [(block, F32)], scalars=1, work=2,
    )
    pieces, new_state = lax.optimization_barrier((pieces, new_state))
    pieces_other = lax.ppermute(pieces, "tiles", swap_core)
    (grad_input,) = call(
        finish_kernel,
        [tile_ids, live, grad_state, kernel, grad_conv, grad_west, grad_east, grad_partner],
        [((SLOTS, TS, TS, LANES), BF16)],
        [ext_scratch, taps_scratch, (block, F32)], scalars=1, work=10,
    )
    expand_out, reduce_out, gain_out, kernel_out = call(
        unpack_kernel, [pieces, pieces_other],
        [((WIDTH, HALF_HID), F32), ((HALF_HID, WIDTH), F32), ((1, LANES), F32), ((7, 7, LANES), F32)],
    )
    return (new_state, grad_input, expand_out, reduce_out, gain_out.reshape(LANES), kernel_out)


def solution(mesh):
    return jax.shard_map(
        per_device,
        mesh=mesh,
        in_specs=(
            P("tiles", None, None, "chan"),
            P("tiles", None, None, "chan"),
            P("tiles", None, None),
            P("tiles"),
            P("tiles", None),
            P("tiles"),
            P(None, None, "chan"),
            P("chan"),
            P(None, "chan"),
            P("chan", None),
        ),
        out_specs=(
            P("tiles", None, None, "chan"),
            P("tiles", None, None, "chan"),
            P(None, "chan"),
            P("chan", None),
            P("chan"),
            P(None, None, "chan"),
        ),
        check_vma=False,
    )
```
